32 devices in a mesh: doc: 8 (over z, y), tensor: 4 (over x, core).
Axes of the slice: x: 2, y: 2, z: 4, core: 2. Of those that a mesh axis runs over, the one named last changes fastest.
Arguments:
- tokens: bfloat16 [64, 288, 768], P('doc', None, 'tensor'), may hold values from -6 to 6
- query_states: bfloat16 [8, 768], P(None, 'doc'), may hold values from -6 to 6
- w_qkv: bfloat16 [3, 768, 768], P(None, None, 'tensor'), may hold values from -0.21875 to 0.21875
- b_qv: float32 [2, 768], P(None, 'tensor'), may hold values from -3 to 3
- w_out: bfloat16 [768, 768], P('tensor'), may hold values from -0.625 to 0.625
- b_out: float32 [768], replicated, may hold values from -2 to 2
- ln1_gain: float32 [768], replicated, may hold values from 0.5 to 1.5
- ln1_bias: float32 [768], replicated, may hold values from -2 to 2
- w_up: bfloat16 [768, 3072], P(None, 'tensor'), may hold values from -0.21875 to 0.21875
- b_up: float32 [3072], P('tensor'), may hold values from -3 to 3
- w_down: bfloat16 [3072, 768], P('tensor'), may hold values from -0.15625 to 0.15625
- b_down: float32 [768], replicated, may hold values from -2 to 2
- ln2_gain: float32 [768], replicated, may hold values from 0.5 to 1.5
- ln2_bias: float32 [768], replicated, may hold values from -2 to 2
- w_query: bfloat16 [768, 128], replicated, may hold values from -0.21875 to 0.21875
- doc_table: float32 [32, 128], replicated, may hold values from -1.2 to 1.2
- vocab_table: bfloat16 [15360, 768], P('tensor'), may hold values from -0.5 to 0.5
- doc_ids: int32 [8, 8], replicated, may hold values from 0 to 31, all different within a row
- lengths: int32 [8, 8], replicated, may hold values from 36 to 288, as said below
- positions: int32 [8, 8], replicated, may hold values from 0 to 31
- targets: int32 [8, 8], replicated, may hold values from 0 to 15359
- out_grad: bfloat16 [64, 288, 768], P('doc'), may hold values from -6 to 6
- query_weight: float32 [8], replicated, may hold values from 2 to 8
Outputs:
- output: bfloat16 [64, 288, 768], P('doc')
- query_nll: float32 [8], replicated
- grad_tokens: float32 [64, 288, 768], P('doc', None, 'tensor')
- grad_states: float32 [8, 768], P(None, 'doc')
- grad_w_qkv: float32 [3, 768, 768], P(None, 'doc', 'tensor')
- grad_b_qv: float32 [2, 768], P(None, 'tensor')
- grad_w_out: float32 [768, 768], P('tensor', 'doc')
- grad_b_out: float32 [768], P('doc')
- grad_ln1_gain: float32 [768], P('doc')
- grad_ln1_bias: float32 [768], P('doc')
- grad_w_up: float32 [768, 3072], P('doc', 'tensor')
- grad_b_up: float32 [3072], P('tensor')
- grad_w_down: float32 [3072, 768], P('tensor', 'doc')
- grad_b_down: float32 [768], P('doc')
- grad_ln2_gain: float32 [768], P('doc')
- grad_ln2_bias: float32 [768], P('doc')
- grad_w_query: float32 [768, 128], P('doc')
The draws below stay inside these ranges and needn't reach their ends.
Inputs may be any that keep to these rules, and one draw needn't show every extreme that they name: `lengths`: slot 0 (null) holds 36 to 64 tokens, the others 288 // 2 to 288; query 0's slot 1 holds 288. `doc_ids`: each query's 8 document ids are different. positions lie inside every slot of the query.
All inputs are finite; a program needn't handle non-finite values.
Results may differ from the reference program's by a relative error of at most 0.023.
The reference program's roundings to bfloat16 on the way count: a program that leaves them out, or rounds other values in their place, can miss the bound.
Values may be sent and summed in bfloat16 or wider, within the bound.
A program may use at most 192 MiB of HBM per device.

```python
import math
import jax
import jax.numpy as jnp
import numpy as np
from jax import lax

D = 768
FF = 3072
QDIM = 128
VOCAB = 15360
SEQ = 288
SLOTS = 8
TARGETS = 8
SEQ_DEV = 8
ROWS = 64
QUERIES = 8
TABLE = 32


def draw_lengths(key, part):
    first_key, second_key = jax.random.split(jax.random.fold_in(key, 17))
    null_slot = jax.random.randint(first_key, (QUERIES, 1), SEQ // 8, SEQ * 2 // 9 + 1)
    pair_slots = jax.random.randint(second_key, (QUERIES, SLOTS - 1), SEQ // 2, SEQ + 1)
    pair_slots = pair_slots.at[0, 0].set(SEQ)
    return jnp.concatenate([null_slot, pair_slots], 1).astype(jnp.int32)


def set_ends(entries, stream_key, low, high):
    longest = entries.shape.index(max(entries.shape))
    spots = []
    for shift in (0, 1):
        where = [jax.random.randint(jax.random.fold_in(stream_key, axis), (), 0, length) for axis, length in enumerate(entries.shape)]
        where[longest] = (where[longest] + shift) % entries.shape[longest]
        spots.append(tuple(where))
    return entries.at[spots[0]].set(low).at[spots[1]].set(high)


def level_of(own_key, dims, cuts, least, largest):
    def one(position, parts):
        heights = jax.random.uniform(jax.random.fold_in(jax.random.fold_in(own_key, 6), position), (parts,), jnp.float32, least / len(cuts), largest / len(cuts))
        return jnp.repeat(jnp.exp(heights), dims[position] // parts).reshape((-1,) + (1,) * (len(dims) - position - 1))

    gain = one(*cuts[0])
    for cut in cuts[1:]:
        gain = gain * one(*cut)
    return gain


def rank_table(number_of, lean):
    portions = [(1 << 20) // math.isqrt(rank ** lean) + 1 for rank in range(1, number_of + 1)]
    scale = 1 + sum(portions) // (1 << 30)
    return np.cumsum(np.array([max(1, weight // scale) for weight in portions]))


def ranked(key, shape, amount, lean):
    listing = rank_table(amount, lean)
    ticket = jax.random.randint(jax.random.fold_in(key, 1), shape, 0, int(listing[amount - 1]))
    rank = jnp.searchsorted(jnp.asarray(listing, jnp.int32), ticket, side="right")
    return jax.random.permutation(jax.random.fold_in(key, 2), amount)[rank].astype(jnp.int32)


def different_ones(rng, rows, number_of, top, lift):
    sequence = jax.random.permutation(jax.random.fold_in(rng, 1), number_of)
    favour = sequence
    for power in range(3):
        favour = favour * favour // number_of
    favour = favour * lift // number_of
    tickets = jax.random.randint(jax.random.fold_in(rng, 2), (rows, number_of), 0, 4096) + favour
    holders = jax.random.permutation(jax.random.fold_in(rng, 3), rows)[jnp.arange(number_of) % rows]
    tickets = jnp.where(jnp.arange(rows)[:, None] == holders[None, :], 1 << 14, tickets)
    priority = tickets * number_of + jnp.arange(number_of)
    return lax.top_k(priority.astype(jnp.int32), top)[1].astype(jnp.int32)


def noise(stream_key, dims, scale, bound, cuts=(), kind=jnp.bfloat16):
    array = jax.random.normal(stream_key, dims, jnp.float32) * scale
    if len(cuts) > 0:
        array = level_of(stream_key, dims, cuts, -0.22, 0.18) * array
    return jnp.clip(array, min=-bound, max=bound).astype(kind)


def setup_inputs(seed: int = 0) -> dict:
    key_list = jax.random.split(jax.random.key(seed), 24)
    tokens = noise(key_list[0], (ROWS, SEQ, D), 1.0, 6.0, ((0, 8), (2, 4)))
    query_states = noise(key_list[1], (QUERIES, D), 1.0, 6.0, ((1, 8),))
    w_qkv = noise(key_list[2], (3, D, D), D ** -0.5, 0.21875, ((2, 4),))
    b_qv = noise(key_list[3], (2, D), 0.5, 3.0, ((1, 4),), jnp.float32)
    w_out = noise(key_list[4], (D, D), (D // 8) ** -0.5, 0.625, ((0, 4),))
    b_out = noise(key_list[5], (D,), 0.3, 2.0, (), jnp.float32)
    ln1_gain = jnp.clip(1.0 + 0.1 * jax.random.normal(key_list[6], (D,), jnp.float32), 0.5, 1.5)
    ln1_bias = noise(key_list[7], (D,), 0.3, 2.0, (), jnp.float32)
    w_up = noise(key_list[8], (D, FF), D ** -0.5, 0.21875, ((1, 4),))
    b_up = noise(key_list[9], (FF,), 0.5, 3.0, ((0, 4),), jnp.float32)
    w_down = noise(key_list[10], (FF, D), (FF // 2) ** -0.5, 0.15625, ((0, 4),))
    b_down = noise(key_list[11], (D,), 0.3, 2.0, (), jnp.float32)
    ln2_gain = jnp.clip(1.0 + 0.1 * jax.random.normal(key_list[12], (D,), jnp.float32), 0.5, 1.5)
    ln2_bias = noise(key_list[13], (D,), 0.3, 2.0, (), jnp.float32)
    w_query = noise(key_list[14], (D, QDIM), D ** -0.5, 0.21875)
    doc_table = noise(key_list[15], (TABLE, QDIM), 0.2, 1.2, (), jnp.float32)
    vocab_table = noise(key_list[16], (VOCAB, D), 0.08, 0.5, ((0, 4),))
    doc_ids = different_ones(key_list[17], QUERIES, TABLE, SLOTS, 0)
    lengths = draw_lengths(jax.random.fold_in(key_list[23], 71), 0)
    positions = set_ends(jax.random.randint(key_list[19], (QUERIES, TARGETS), 0, SEQ // 9), jax.random.fold_in(key_list[19], 1), 0, (SEQ // 9) - 1).astype(jnp.int32)
    targets = set_ends(ranked(key_list[20], (QUERIES, TARGETS), VOCAB, 2), jax.random.fold_in(key_list[20], 3), 0, VOCAB - 1).astype(jnp.int32)
    out_grad = noise(key_list[21], (ROWS, SEQ, D), 1.0, 6.0, ((0, 8),))
    query_weight = jnp.clip(jnp.exp(jax.random.uniform(key_list[22], (QUERIES,), jnp.float32, math.log(2.0), math.log(8.0))), 2.0, 8.0)
    return {"tokens": tokens, "query_states": query_states, "w_qkv": w_qkv, "b_qv": b_qv, "w_out": w_out, "b_out": b_out, "ln1_gain": ln1_gain, "ln1_bias": ln1_bias, "w_up": w_up, "b_up": b_up, "w_down": w_down, "b_down": b_down, "ln2_gain": ln2_gain, "ln2_bias": ln2_bias, "w_query": w_query, "doc_table": doc_table, "vocab_table": vocab_table, "doc_ids": doc_ids, "lengths": lengths, "positions": positions, "targets": targets, "out_grad": out_grad, "query_weight": query_weight}


@jax.custom_vjp
def low(v):
    return lax.optimization_barrier(v.astype(jnp.bfloat16)).astype(jnp.float32)

@jax.custom_vjp
def low_back(v):
    return v

def low_keep(v):
    return (low(v), None)

def low_pass(kept, grad):
    return (grad,)

def back_keep(v):
    return (v, None)

def back_low(kept, grad):
    return (low(grad),)
low.defvjp(low_keep, low_pass)
low_back.defvjp(back_keep, back_low)
precise = lax.Precision.HIGHEST

def layer_norm(values, gain_vec, shift_vec):
    centred = values - lax.optimization_barrier(jnp.mean(values, -1, keepdims=True))
    normed = centred * lax.rsqrt(lax.optimization_barrier(jnp.mean(centred * centred, -1, keepdims=True)) + 1e-12)
    return normed * gain_vec + shift_vec

def layer_block(params, vocab_rows, pieces):
    tokens, row_length, row_position, row_target = pieces
    w_qkv, b_qv, w_out, b_out, gain_one, shift_one, w_up, b_up, w_down, b_down, gain_two, shift_two = params
    sequences, seq_length, model_width = tokens.shape
    head_count = model_width // 64

    def project(which):
        return jnp.einsum('bsd,de->bse', tokens, w_qkv[which], precision=precise)
    head_shape = (sequences, seq_length, head_count, 64)
    query_heads = low(low_back(project(0) + b_qv[0])).reshape(head_shape)
    key_heads = low(low_back(project(1))).reshape(head_shape)
    value_heads = low(low_back(project(2) + b_qv[1])).reshape(head_shape)
    scores = jnp.einsum('bqhe,bkhe->bhqk', query_heads, key_heads, precision=precise) * 0.125
    key_mask = (jnp.arange(seq_length, dtype=jnp.int32)[None, :] < row_length[:, None])[:, None, None, :]
    scores = low_back(jnp.where(key_mask, scores, -1000000000.0))
    weights_att = low(jax.nn.softmax(scores, -1))
    context = jnp.einsum('bhqk,bkhe->bqhe', weights_att, value_heads, precision=precise)
    context = low(low_back(context.reshape(sequences, seq_length, model_width)))
    attended = low_back(jnp.einsum('bsi,id->bsd', context, w_out, precision=precise))
    hidden_one = layer_norm(tokens + attended + b_out, gain_one, shift_one)
    up_proj = low_back(jnp.einsum('bsd,df->bsf', low(hidden_one), w_up, precision=precise) + b_up)
    active = low(jax.nn.gelu(up_proj, approximate=False))
    lowered = low_back(jnp.einsum('bsf,fd->bsd', active, w_down, precision=precise))
    result = layer_norm(hidden_one + lowered + b_down, gain_two, shift_two)
    picked = low(result[jnp.arange(sequences)[:, None], row_position])
    vocab_logits = low_back(jnp.einsum('btd,vd->btv', picked, vocab_rows, precision=precise))
    chosen = jnp.take_along_axis(vocab_logits, row_target[:, :, None], 2)[:, :, 0]
    loglik = lax.optimization_barrier(jnp.sum(chosen - jax.nn.logsumexp(vocab_logits, -1), -1))
    return (result, loglik)

def reference(tokens, query_states, w_qkv, b_qv, w_out, b_out, ln1_gain, ln1_bias, w_up, b_up, w_down, b_down, ln2_gain, ln2_bias, w_query, doc_table, vocab_table, doc_ids, lengths, positions, targets, out_grad, query_weight):
    row_index = jnp.arange(ROWS, dtype=jnp.int32)
    slot_index = row_index // QUERIES
    query_index = row_index % QUERIES
    row_length = lengths[query_index, slot_index]
    row_position = positions[query_index]
    row_target = targets[query_index]
    embeds = doc_table[doc_ids[query_index, slot_index]].astype(jnp.float32)
    vocab_rows = vocab_table.astype(jnp.float32)
    block_count = ROWS // SEQ_DEV
    block_step = jax.checkpoint(layer_block)

    def forward(inputs, states, params):

        def scan_step(carried, pieces):
            return (carried, block_step(params[:12], vocab_rows, pieces))
        pieces = (inputs.reshape(block_count, SEQ_DEV, SEQ, D), row_length.reshape(block_count, SEQ_DEV), row_position.reshape(block_count, SEQ_DEV, TARGETS), row_target.reshape(block_count, SEQ_DEV, TARGETS))
        unused, outcome = lax.scan(scan_step, jnp.float32(0.0), pieces)
        result, loglik = outcome
        query_emb = low_back(jnp.dot(states, params[12], precision=precise))
        retrieval = lax.optimization_barrier(jnp.sum(query_emb[query_index] * embeds, -1))
        joint_score = retrieval + loglik.reshape(ROWS)
        prior_lse = jax.nn.logsumexp(retrieval.reshape(SLOTS, QUERIES), 0)
        joint_lse = jax.nn.logsumexp(joint_score.reshape(SLOTS, QUERIES), 0)
        return (result.reshape(ROWS, SEQ, D), prior_lse - joint_lse)
    params = tuple((item.astype(jnp.float32) for item in (w_qkv, b_qv, w_out, b_out, ln1_gain, ln1_bias, w_up, b_up, w_down, b_down, ln2_gain, ln2_bias, w_query)))
    primal, pullback = jax.vjp(forward, tokens.astype(jnp.float32), query_states.astype(jnp.float32), params)
    result, query_nll = primal
    grad_tokens, grad_states, grads = pullback((out_grad.astype(jnp.float32), query_weight.astype(jnp.float32)))
    return (result.astype(jnp.bfloat16), query_nll, grad_tokens, grad_states, grads[0], grads[1], grads[2], grads[3], grads[4], grads[5], grads[6], grads[7], grads[8], grads[9], grads[10], grads[11], grads[12])
```

```python
import functools

import jax
import jax.numpy as jnp
from jax import lax
from jax.experimental import pallas as pl
from jax.experimental.pallas import tpu as pltpu
from jax.sharding import PartitionSpec as P

MESH = pl.DeviceIdType.MESH
f32 = jnp.float32
bf16 = jnp.bfloat16
MIB = 1024 * 1024


def flip(index, bit):
    return index + bit * (1 - 2 * lax.rem(lax.div(index, bit), 2))


def dot(a, b):
    return lax.dot_general(a, b, (((1,), (0,)), ((), ())), preferred_element_type=f32)


def dot_nt(a, b):
    return lax.dot_general(a, b, (((1,), (1,)), ((), ())), preferred_element_type=f32)


def dot_tn(a, b):
    return lax.dot_general(a, b, (((0,), (0,)), ((), ())), preferred_element_type=f32)


def rows_of(block):
    return block.reshape(block.shape[0] * block.shape[1], block.shape[2])


def norm_forward(y):
    centred = y - jnp.mean(y, -1, keepdims=True)
    factor = lax.rsqrt(jnp.mean(centred * centred, -1, keepdims=True) + 1e-12)
    return centred * factor, factor


def forward_kernel(
    cfg,
    lengths,
    tokens,
    w_qkv,
    w_out,
    w_up,
    w_down,
    vectors,
    b_out,
    gain_one,
    bias_one,
    b_down,
    gain_two,
    bias_two,
    x_out,
    qkv_out,
    lse_out,
    ctx_out,
    n1_out,
    f1_out,
    hl_out,
    act_out,
    gp_out,
    n2_out,
    f2_out,
    res_out,
    wq_all,
    wo_all,
    wu_all,
    wd_all,
    tok,
    x_s,
    qkv_s,
    lse_s,
    ctx_s,
    att_s,
    n1_s,
    f1_s,
    hl_s,
    act_s,
    gp_s,
    n2_s,
    f2_s,
    res_s,
    wq,
    wo,
    wu,
    wd,
    vec,
    send_sem,
    recv_sem,
    local_sem,
    out_sem,
):
    n_seq, seq, model, queries = cfg
    d = lax.axis_index("doc")
    t = lax.axis_index("tensor")
    t1, t2 = flip(t, 1), flip(t, 2)
    t3 = flip(t1, 2)
    d1, d2 = flip(d, 1), flip(d, 2)
    q = lax.rem(d, 4)
    q1, q2 = flip(q, 1), flip(q, 2)
    q3 = flip(q1, 2)

    barrier = pltpu.get_barrier_semaphore()
    peers = ({"tensor": t1}, {"tensor": t2}, {"tensor": t3}, {"doc": d1}, {"doc": d2})
    for peer in peers:
        pl.semaphore_signal(barrier, inc=1, device_id=peer, device_id_type=MESH)
    pl.semaphore_wait(barrier, len(peers))

    def remote(number, src, dst, peer):
        return pltpu.make_async_remote_copy(
            src_ref=src,
            dst_ref=dst,
            send_sem=send_sem.at[number],
            recv_sem=recv_sem.at[number],
            device_id=peer,
            device_id_type=MESH,
        )

    gathered = (wq, wo, wu, wd)
    inputs = (w_qkv, w_out, w_up, w_down)
    outputs = (wq_all, wo_all, wu_all, wd_all)
    started = []

    def send(number, src, dst, peer):
        copy = remote(number, src, dst, peer)
        copy.start()
        started.append(copy)

    def send_x(a):
        send(9 * a, inputs[a].at[q], gathered[a].at[t, q], {"tensor": t2})

    def send_core(a):
        send(9 * a + 4, inputs[a], gathered[a].at[t], {"tensor": t1})

    def arrived(number, ref):
        remote(number, ref, ref, {"tensor": t1}).wait_recv()

    def piece(a, part):
        return gathered[a].at[t2, part]

    def after_x(a):
        arrived(9 * a, piece(a, q))
        send(9 * a + 1, piece(a, q), piece(a, q), {"doc": d1})
        send(9 * a + 2, piece(a, q), piece(a, q), {"doc": d2})
        send(9 * a + 5, piece(a, q), piece(a, q), {"tensor": t1})

    def after_y(a):
        arrived(9 * a + 1, piece(a, q1))
        send(9 * a + 3, piece(a, q1), piece(a, q1), {"doc": d2})
        send(9 * a + 6, piece(a, q1), piece(a, q1), {"tensor": t1})

    def after_z(a):
        arrived(9 * a + 2, piece(a, q2))
        send(9 * a + 7, piece(a, q2), piece(a, q2), {"tensor": t1})
        arrived(9 * a + 3, piece(a, q3))
        send(9 * a + 8, piece(a, q3), piece(a, q3), {"tensor": t1})

    def after_core(a):
        for k, part in enumerate((q, q1, q2, q3)):
            arrived(9 * a + 5 + k, gathered[a].at[t3, part])

    tok_base, vec_base = 36, 39
    own = pl.multiple_of(t * n_seq, n_seq)

    def local(number, src, dst):
        copy = pltpu.make_async_copy(src, dst, local_sem.at[number])
        copy.start()
        return copy

    send_x(0)
    own_q = local(0, w_qkv, wq.at[t])
    own_tok = local(1, tokens.at[pl.ds(own, n_seq)], tok.at[t])
    for k, peer in enumerate((t1, t2, t3)):
        theirs = pl.multiple_of(peer * n_seq, n_seq)
        send(tok_base + k, tokens.at[pl.ds(theirs, n_seq)], tok.at[t], {"tensor": peer})
        send(vec_base + k, vectors, vec.at[t], {"tensor": peer})
    send_core(0)
    own_vec = local(2, vectors, vec.at[t])
    own_o = local(3, w_out, wo.at[t])
    own_u = local(4, w_up, wu.at[t])
    own_d = local(5, w_down, wd.at[t])
    after_x(0)
    after_y(0)
    own_tok.wait()
    own_vec.wait()
    for k, peer in enumerate((t1, t2, t3)):
        arrived(tok_base + k, tok.at[peer])
        arrived(vec_base + k, vec.at[peer])
    for a in (1, 2):
        send_x(a)
        send_core(a)

    stores = []

    def store(src, dst):
        copy = pltpu.make_async_copy(src, dst, out_sem.at[len(stores)])
        copy.start()
        stores.append(copy)

    @pl.loop(0, n_seq)
    def _(s):
        x_s[s] = jnp.concatenate([tok[j, s] for j in range(4)], axis=1)

    store(x_s, x_out)

    key_index = lax.broadcasted_iota(jnp.int32, (seq, seq), 0)

    def attention(part, first):
        @pl.loop(0, n_seq)
        def _(s):
            row = d * (4 * n_seq) + t * n_seq + s
            length = lengths[lax.rem(row, queries), lax.div(row, queries)]
            bias = vec[part, 1:2, :576]
            z = (dot(x_s[s], rows_of(wq[part])) + bias).astype(bf16)
            qkv_s[part, s] = z
            pieces = []
            for h in range(3):
                qh = z[:, h * 64 : h * 64 + 64] * 0.125
                kh = z[:, 192 + h * 64 : 256 + h * 64]
                vh = z[:, 384 + h * 64 : 448 + h * 64]
                st = jnp.where(key_index < length, dot_nt(kh, qh), -1000000000.0)
                high = jnp.max(st, 0, keepdims=True)
                e = jnp.exp(st - high)
                total = jnp.sum(e, 0, keepdims=True)
                prob = (e * (1.0 / total)).astype(bf16)
                lse_s[part, s, h] = high + jnp.log(total)
                pieces.append(dot_tn(vh, prob))
            ctx_s[part, s] = jnp.concatenate(pieces, axis=0).T.astype(bf16)

    def project(part, first):
        @pl.loop(0, n_seq)
        def _(s):
            for n in range(model // 256):
                cols = slice(n * 256, n * 256 + 256)
                term = dot(ctx_s[part, s], rows_of(wo[part, :, :, cols]))
                if first:
                    att_s[s, :, cols] = term
                else:
                    att_s[s, :, cols] += term

    own_q.wait()
    attention(t, True)
    after_x(1)
    after_y(1)
    after_z(0)
    own_o.wait()
    project(t, True)
    arrived(4, wq.at[t1])
    attention(t1, False)
    arrived(9 + 4, wo.at[t1])
    project(t1, False)
    send_x(3)
    send_core(3)
    after_z(1)
    after_x(2)
    after_y(2)
    attention(t2, False)
    project(t2, False)
    after_core(0)
    after_z(2)
    attention(t3, False)
    after_core(1)
    project(t3, False)
    store(qkv_s, qkv_out)
    store(lse_s, lse_out)
    store(ctx_s, ctx_out)
    store(wq, wq_all)
    store(wo, wo_all)

    chunk = 96
    chunks = seq // chunk

    @pl.loop(0, n_seq * chunks)
    def _(i):
        s, r = lax.div(i, chunks), pl.multiple_of(lax.rem(i, chunks) * chunk, chunk)
        rows = pl.ds(r, chunk)
        y = x_s[s, rows].astype(f32) + att_s[s, rows] + b_out[...]
        n1, f1 = norm_forward(y)
        n1_s[s, rows] = n1
        f1_s[s, rows] = f1
        hl_s[s, rows] = (n1 * gain_one[...] + bias_one[...]).astype(bf16)

    store(n1_s, n1_out)
    store(f1_s, f1_out)
    store(hl_s, hl_out)
    after_x(3)
    after_y(3)
    own_u.wait()
    own_d.wait()

    def ffn_up(part):
        @pl.loop(0, n_seq * (model // 256))
        def _(i):
            s, n = lax.div(i, model // 256), lax.rem(i, model // 256)
            cols = pl.ds(pl.multiple_of(n * 256, 256), 256)
            u = dot(hl_s[s], rows_of(wu[part, :, :, cols])) + vec[part, 0:1, cols]
            cdf = 0.5 * (1.0 + lax.erf(u * 0.7071067811865476))
            pdf = jnp.exp(u * u * -0.5) * 0.3989422804014327
            act_s[part, s, :, cols] = (u * cdf).astype(bf16)
            gp_s[part, s, :, cols] = (cdf + u * pdf).astype(bf16)

    def ffn_down(part, first):
        @pl.loop(0, n_seq * (model // 256))
        def _(i):
            s, n = lax.div(i, model // 256), lax.rem(i, model // 256)
            cols = pl.ds(pl.multiple_of(n * 256, 256), 256)
            term = dot(act_s[part, s], rows_of(wd[part, :, :, cols]))
            if first:
                att_s[s, :, cols] = term
            else:
                att_s[s, :, cols] += term

    ffn_up(t)
    ffn_down(t, True)
    after_z(3)
    arrived(2 * 9 + 4, wu.at[t1])
    ffn_up(t1)
    arrived(3 * 9 + 4, wd.at[t1])
    ffn_down(t1, False)
    ffn_up(t2)
    ffn_down(t2, False)
    after_core(2)
    ffn_up(t3)
    after_core(3)
    store(act_s, act_out)
    store(gp_s, gp_out)
    store(wu, wu_all)
    store(wd, wd_all)
    ffn_down(t3, False)

    @pl.loop(0, n_seq * chunks)
    def _(i):
        s, r = lax.div(i, chunks), pl.multiple_of(lax.rem(i, chunks) * chunk, chunk)
        rows = pl.ds(r, chunk)
        y = n1_s[s, rows] * gain_one[...] + bias_one[...] + att_s[s, rows] + b_down[...]
        n2, f2 = norm_forward(y)
        n2_s[s, rows] = n2
        f2_s[s, rows] = f2
        res_s[s, rows] = (n2 * gain_two[...] + bias_two[...]).astype(bf16)

    store(n2_s, n2_out)
    store(f2_s, f2_out)
    store(res_s, res_out)
    for copy in stores:
        copy.wait()
    for copy in started:
        copy.wait_send()


def forward(n_seq, seq, model, queries, lengths, tokens, w_qkv, w_out, w_up, w_down, vectors, rows):
    def sds(shape, dtype):
        return jax.ShapeDtypeStruct(shape, dtype)

    acts = [
        ((n_seq, seq, model), bf16),
        ((4, n_seq, seq, 576), bf16),
        ((4, n_seq, 3, 1, seq), f32),
        ((4, n_seq, seq, 192), bf16),
        ((n_seq, seq, model), f32),
        ((n_seq, seq, 1), f32),
        ((n_seq, seq, model), bf16),
        ((4, n_seq, seq, model), bf16),
        ((4, n_seq, seq, model), bf16),
        ((n_seq, seq, model), f32),
        ((n_seq, seq, 1), f32),
        ((n_seq, seq, model), bf16),
    ]
    weights = [(4,) + w.shape for w in (w_qkv, w_out, w_up, w_down)]
    any_spec = pl.BlockSpec(memory_space=pl.ANY)
    vmem_spec = pl.BlockSpec(memory_space=pltpu.VMEM)
    scratch = [pltpu.VMEM((4, n_seq, seq, model // 4), bf16)]
    scratch += [pltpu.VMEM(*a) for a in acts[:4]]
    scratch += [pltpu.VMEM((n_seq, seq, model), f32)]
    scratch += [pltpu.VMEM(*a) for a in acts[4:]]
    scratch += [pltpu.VMEM(w, bf16) for w in weights]
    scratch += [pltpu.VMEM((4,) + vectors.shape, f32)]
    scratch += [
        pltpu.SemaphoreType.DMA((42,)),
        pltpu.SemaphoreType.DMA((42,)),
        pltpu.SemaphoreType.DMA((6,)),
        pltpu.SemaphoreType.DMA((16,)),
    ]
    return pl.pallas_call(
        functools.partial(forward_kernel, (n_seq, seq, model, queries)),
        out_shape=[sds(*a) for a in acts] + [sds(w, bf16) for w in weights],
        in_specs=[pl.BlockSpec(memory_space=pltpu.SMEM)] + [any_spec] * 6 + [vmem_spec] * 6,
        out_specs=[any_spec] * 16,
        scratch_shapes=scratch,
        compiler_params=pltpu.CompilerParams(
            collective_id=0, has_side_effects=True, vmem_limit_bytes=60 * MIB
        ),
        name="layer_forward",
    )(lengths, tokens, w_qkv, w_out, w_up, w_down, vectors, *rows)


precise = lax.Precision.HIGHEST


def joined(array, axis, combine):
    everything = jax.tree.map(lambda part: lax.all_gather(part, axis), array)
    initial = jax.tree.map(lambda part: part[0], everything)

    def step(k, so_far):
        return combine(so_far, jax.tree.map(lambda part: part[k], everything))

    return lax.fori_loop(1, lax.axis_size(axis), step, initial)


def norm_back(upstream, normed, factor, gain_vec):
    scaled = upstream * gain_vec
    inner = (
        scaled
        - jnp.mean(scaled, -1, keepdims=True)
        - normed * jnp.mean(scaled * normed, -1, keepdims=True)
    )
    return (inner * factor, jnp.sum(upstream * normed, 0), jnp.sum(upstream, 0))


def merge_pair(high_first, mass_first, high_second, mass_second):
    highest = jnp.maximum(high_first, high_second)
    return (
        highest,
        mass_first * jnp.exp(high_first - highest) + mass_second * jnp.exp(high_second - highest),
    )


def vocab_combine(first, second):
    highest, summed = merge_pair(first[0], first[1], second[0], second[1])
    return (highest, summed, first[2] + second[2])


def query_combine(first, second):
    prior_high, prior_mass = merge_pair(first[0], first[1], second[0], second[1])
    joint_high, joint_mass = merge_pair(first[2], first[3], second[2], second[3])
    return (prior_high, prior_mass, joint_high, joint_mass)


def partial_lse(members, values):
    highest = jnp.max(jnp.where(members, values[:, None], -1e30), 0)
    summed = jnp.sum(jnp.where(members, jnp.exp(values[:, None] - highest[None, :]), 0.0), 0)
    return (highest, summed)


def shards(
    tokens,
    query_states,
    w_qkv,
    b_qv,
    w_out,
    b_out,
    ln1_gain,
    ln1_bias,
    w_up,
    b_up,
    w_down,
    b_down,
    ln2_gain,
    ln2_bias,
    w_query,
    doc_table,
    vocab_table,
    doc_ids,
    lengths,
    positions,
    targets,
    out_grad,
    query_weight,
):
    sequences, seq_length, part_width = tokens.shape
    model_width = w_qkv.shape[1]
    n_seq = sequences // 4
    row_count = n_seq * seq_length
    queries = lengths.shape[0]
    t = lax.axis_index("tensor")
    packed_qkv = jnp.concatenate([w_qkv[0], w_qkv[1], w_qkv[2]], 1).reshape(4, 192, 576)
    hidden = w_up.shape[1]
    vectors = jnp.zeros((8, hidden), f32)
    vectors = vectors.at[0].set(b_up).at[1, :192].set(b_qv[0]).at[1, 384:576].set(b_qv[1])
    rows = [v[None, :] for v in (b_out, ln1_gain, ln1_bias, b_down, ln2_gain, ln2_bias)]
    (x, qkv, lse, ctx, n1, f1, hl, act, gp, n2, f2, res, wq, wo, wu, wd) = forward(
        n_seq,
        seq_length,
        model_width,
        queries,
        lengths,
        tokens,
        packed_qkv,
        w_out.reshape(4, 48, model_width),
        w_up.reshape(4, 192, hidden),
        w_down.reshape(4, 192, model_width),
        vectors,
        rows,
    )
    output = lax.all_gather(res, "tensor", axis=0, tiled=True)
    row_index = lax.axis_index("doc") * sequences + jnp.arange(sequences, dtype=jnp.int32)
    slot_index = row_index // queries
    query_index = row_index % queries
    row_position = positions[query_index]
    row_target = targets[query_index]
    own = lambda a: lax.dynamic_slice_in_dim(a, t * n_seq, n_seq, 0)
    own_position = own(row_position)
    seq_base = jnp.arange(n_seq, dtype=jnp.int32)[:, None]
    picked = lax.all_gather(res[seq_base, own_position], "tensor", axis=0, tiled=True)
    vocab_logits = jnp.einsum("btd,vd->btv", picked, vocab_table, preferred_element_type=f32)
    vocab_local = vocab_table.shape[0]
    vocab_ids = t * vocab_local + jnp.arange(vocab_local, dtype=jnp.int32)
    target_hits = vocab_ids[None, None, :] == row_target[:, :, None]
    local_high = jnp.max(vocab_logits, -1)
    local_mass = jnp.sum(jnp.exp(vocab_logits - local_high[:, :, None]), -1)
    local_chosen = jnp.sum(jnp.where(target_hits, vocab_logits, 0.0), -1)
    vocab_high, vocab_mass, chosen = joined(
        (local_high, local_mass, local_chosen), "tensor", vocab_combine
    )
    vocab_lse = vocab_high + jnp.log(vocab_mass)
    loglik = jnp.sum(chosen - vocab_lse, -1)
    states = lax.all_gather(query_states, "doc", axis=1, tiled=True)
    query_emb = jnp.dot(states, w_query, preferred_element_type=f32)
    members = query_index[:, None] == jnp.arange(queries, dtype=jnp.int32)[None, :]
    member_weights = members.astype(f32)
    own_emb = jnp.dot(member_weights, query_emb, precision=precise)
    embeds = doc_table[doc_ids[query_index, slot_index]]
    retrieval = jnp.sum(own_emb * embeds, -1)
    joint_score = retrieval + loglik
    prior_high, prior_mass = partial_lse(members, retrieval)
    joint_high, joint_mass = partial_lse(members, joint_score)
    prior_high, prior_mass, joint_high, joint_mass = joined(
        (prior_high, prior_mass, joint_high, joint_mass), "doc", query_combine
    )
    prior_lse = prior_high + jnp.log(prior_mass)
    joint_lse = joint_high + jnp.log(joint_mass)
    query_nll = prior_lse - joint_lse
    row_weight = query_weight[query_index]
    posterior = jnp.exp(joint_score - jnp.dot(member_weights, joint_lse, precision=precise))
    prior_prob = jnp.exp(retrieval - jnp.dot(member_weights, prior_lse, precision=precise))
    grad_loglik = -row_weight * posterior
    grad_retrieval = row_weight * (prior_prob - posterior)
    vocab_probs = jnp.exp(vocab_logits - vocab_lse[:, :, None])
    grad_logits = (grad_loglik[:, None, None] * (target_hits.astype(f32) - vocab_probs)).astype(
        bf16
    )
    grad_picked = lax.psum_scatter(
        jnp.einsum("btv,vd->btd", grad_logits, vocab_table, preferred_element_type=f32),
        "tensor",
        scatter_dimension=0,
        tiled=True,
    )
    grad_emb = jnp.dot(
        member_weights.T, grad_retrieval[:, None] * embeds, precision=precise
    ).astype(bf16)
    grad_w_query = jnp.dot(states.T, grad_emb, preferred_element_type=f32)
    grad_states = jnp.dot(grad_emb, w_query.T, preferred_element_type=f32)
    flat = lambda a: a.reshape(row_count, a.shape[-1])
    grad_result = flat(own(out_grad).astype(f32).at[seq_base, own_position].add(grad_picked))
    n1, f1, n2, f2, hl, x = flat(n1), flat(f1), flat(n2), flat(f2), flat(hl), flat(x)
    dy2, dg2, db2 = norm_back(grad_result, n2, f2, ln2_gain)
    d_low = dy2.astype(bf16)
    act, gp = act.reshape(4, row_count, hidden), gp.reshape(4, row_count, hidden)
    wu, wd = wu.reshape(4, model_width, hidden), wd.reshape(4, hidden, model_width)
    wq, wo = wq.reshape(4, model_width, 576), wo.reshape(4, 192, model_width)
    qkv, ctx = qkv.reshape(4, n_seq, seq_length, 576), ctx.reshape(4, row_count, 192)
    g_down = jnp.einsum("tmf,md->tfd", act, d_low, preferred_element_type=f32)
    d_act = jnp.einsum("md,tfd->tmf", d_low, wd, preferred_element_type=f32)
    d_up = (d_act * gp.astype(f32)).astype(bf16)
    g_up = jnp.einsum("md,tmf->tdf", hl, d_up, preferred_element_type=f32)
    g_b_up = jnp.sum(d_up.astype(f32), 1)
    d_hidden = dy2 + jnp.einsum("tmf,tdf->md", d_up, wu, preferred_element_type=f32)
    dy1, dg1, db1 = norm_back(d_hidden, n1, f1, ln1_gain)
    d_att = dy1.astype(bf16)
    g_out = jnp.einsum("tme,md->ted", ctx, d_att, preferred_element_type=f32)
    d_ctx = jnp.einsum("md,ted->tme", d_att, wo, preferred_element_type=f32).astype(bf16)
    d_ctx = d_ctx.reshape(4, n_seq, seq_length, 3, 64)
    heads = qkv.reshape(4, n_seq, seq_length, 3, 3, 64)
    hq, hk, hv = heads[:, :, :, 0], heads[:, :, :, 1], heads[:, :, :, 2]
    row_length = own(lengths[query_index, slot_index])
    key_mask = (jnp.arange(seq_length, dtype=jnp.int32)[None, :] < row_length[:, None])[
        None, :, None, None, :
    ]
    scores = jnp.einsum("tbqhe,tbkhe->tbhqk", hq, hk, preferred_element_type=f32) * 0.125
    scores = jnp.where(key_mask, scores, -1000000000.0)
    prob = jnp.exp(scores - lse.reshape(4, n_seq, 3, seq_length, 1))
    d_v = jnp.einsum("tbhqk,tbqhe->tbkhe", prob.astype(bf16), d_ctx, preferred_element_type=f32)
    d_prob = jnp.einsum("tbqhe,tbkhe->tbhqk", d_ctx, hv, preferred_element_type=f32)
    d_s = (prob * (d_prob - jnp.sum(d_prob * prob, -1, keepdims=True))).astype(bf16)
    d_q = jnp.einsum("tbhqk,tbkhe->tbqhe", d_s, hk, preferred_element_type=f32) * 0.125
    d_k = jnp.einsum("tbhqk,tbqhe->tbkhe", d_s, hq, preferred_element_type=f32) * 0.125
    d_qkv = jnp.stack([d_q, d_k, d_v], 3).reshape(4, row_count, 576).astype(bf16)
    g_b = jnp.sum(d_qkv.astype(f32), 1)
    g_qkv = jnp.einsum("md,tme->tde", x, d_qkv, preferred_element_type=f32)
    d_x = dy1 + jnp.einsum("tme,tde->md", d_qkv, wq, preferred_element_type=f32)
    d_x = d_x.reshape(n_seq, seq_length, 4, part_width).astype(bf16)
    grad_tokens = lax.all_to_all(d_x, "tensor", split_axis=2, concat_axis=0, tiled=True)
    grad_tokens = grad_tokens.reshape(sequences, seq_length, part_width).astype(f32)
    over_t = lambda a: lax.psum_scatter(a, "tensor", scatter_dimension=0, tiled=True)[0]
    docs = lambda a, k: lax.psum_scatter(a, "doc", scatter_dimension=k, tiled=True)
    g_qkv = docs(over_t(g_qkv), 0)
    g_qkv = jnp.stack([g_qkv[:, :192], g_qkv[:, 192:384], g_qkv[:, 384:]])
    g_b = lax.psum(over_t(g_b), "doc")
    small = lambda v: docs(lax.psum(v, "tensor"), 0)
    return (
        output,
        query_nll,
        grad_tokens,
        docs(grad_states, 1),
        g_qkv,
        jnp.stack([g_b[:192], g_b[384:]]),
        docs(over_t(g_out), 1),
        small(jnp.sum(dy1, 0)),
        small(dg1),
        small(db1),
        docs(over_t(g_up), 0),
        lax.psum(over_t(g_b_up), "doc"),
        docs(over_t(g_down), 1),
        small(jnp.sum(dy2, 0)),
        small(dg2),
        small(db2),
        docs(grad_w_query, 0),
    )


def solution(mesh):
    in_specs = (
        P("doc", None, "tensor"),
        P(None, "doc"),
        P(None, None, "tensor"),
        P(None, "tensor"),
        P("tensor", None),
        P(),
        P(),
        P(),
        P(None, "tensor"),
        P("tensor"),
        P("tensor", None),
        P(),
        P(),
        P(),
        P(),
        P(),
        P("tensor", None),
        P(),
        P(),
        P(),
        P(),
        P("doc", None, None),
        P(),
    )
    out_specs = (
        P("doc", None, None),
        P(),
        P("doc", None, "tensor"),
        P(None, "doc"),
        P(None, "doc", "tensor"),
        P(None, "tensor"),
        P("tensor", "doc"),
        P("doc"),
        P("doc"),
        P("doc"),
        P("doc", "tensor"),
        P("tensor"),
        P("tensor", "doc"),
        P("doc"),
        P("doc"),
        P("doc"),
        P("doc", None),
    )
    return jax.shard_map(shards, mesh=mesh, in_specs=in_specs, out_specs=out_specs, check_vma=False)
```

```python
import functools

import jax
import jax.numpy as jnp
from jax import lax
from jax.experimental import pallas as pl
from jax.experimental.pallas import tpu as pltpu
from jax.sharding import PartitionSpec as P

MESH = pl.DeviceIdType.MESH
f32 = jnp.float32
bf16 = jnp.bfloat16
MIB = 1024 * 1024


def flip(index, bit):
    return index + bit * (1 - 2 * lax.rem(lax.div(index, bit), 2))


def dot(a, b):
    return lax.dot_general(a, b, (((1,), (0,)), ((), ())), preferred_element_type=f32)


def dot_nt(a, b):
    return lax.dot_general(a, b, (((1,), (1,)), ((), ())), preferred_element_type=f32)


def dot_tn(a, b):
    return lax.dot_general(a, b, (((0,), (0,)), ((), ())), preferred_element_type=f32)


def rows_of(block):
    return block.reshape(block.shape[0] * block.shape[1], block.shape[2])


def norm_forward(y):
    centred = y - jnp.mean(y, -1, keepdims=True)
    factor = lax.rsqrt(jnp.mean(centred * centred, -1, keepdims=True) + 1e-12)
    return centred * factor, factor


def forward_kernel(
    cfg,
    lengths,
    tokens,
    w_qkv,
    w_out,
    w_up,
    w_down,
    vectors,
    b_out,
    gain_one,
    bias_one,
    b_down,
    gain_two,
    bias_two,
    x_out,
    qkv_out,
    lse_out,
    ctx_out,
    n1_out,
    f1_out,
    hl_out,
    act_out,
    gp_out,
    n2_out,
    f2_out,
    res_out,
    wq_all,
    wo_all,
    wu_all,
    wd_all,
    tok,
    x_s,
    qkv_s,
    lse_s,
    ctx_s,
    att_s,
    n1_s,
    f1_s,
    hl_s,
    act_s,
    gp_s,
    n2_s,
    f2_s,
    res_s,
    wq,
    wo,
    wu,
    wd,
    vec,
    send_sem,
    recv_sem,
    local_sem,
    out_sem,
):
    n_seq, seq, model, queries = cfg
    d = lax.axis_index("doc")
    t = lax.axis_index("tensor")
    t1, t2 = flip(t, 1), flip(t, 2)
    t3 = flip(t1, 2)
    d1, d2 = flip(d, 1), flip(d, 2)
    q = lax.rem(d, 4)
    q1, q2 = flip(q, 1), flip(q, 2)
    q3 = flip(q1, 2)

    barrier = pltpu.get_barrier_semaphore()
    peers = ({"tensor": t1}, {"tensor": t2}, {"tensor": t3}, {"doc": d1}, {"doc": d2})
    for peer in peers:
        pl.semaphore_signal(barrier, inc=1, device_id=peer, device_id_type=MESH)
    pl.semaphore_wait(barrier, len(peers))

    def remote(number, src, dst, peer):
        return pltpu.make_async_remote_copy(
            src_ref=src,
            dst_ref=dst,
            send_sem=send_sem.at[number],
            recv_sem=recv_sem.at[number],
            device_id=peer,
            device_id_type=MESH,
        )

    gathered = (wq, wo, wu, wd)
    inputs = (w_qkv, w_out, w_up, w_down)
    outputs = (wq_all, wo_all, wu_all, wd_all)
    started = []

    def send(number, src, dst, peer):
        copy = remote(number, src, dst, peer)
        copy.start()
        started.append(copy)

    def send_x(a):
        send(9 * a, inputs[a].at[q], gathered[a].at[t, q], {"tensor": t2})

    def send_core(a):
        send(9 * a + 4, inputs[a], gathered[a].at[t], {"tensor": t1})

    def arrived(number, ref):
        remote(number, ref, ref, {"tensor": t1}).wait_recv()

    def piece(a, part):
        return gathered[a].at[t2, part]

    def after_x(a):
        arrived(9 * a, piece(a, q))
        send(9 * a + 1, piece(a, q), piece(a, q), {"doc": d1})
        send(9 * a + 2, piece(a, q), piece(a, q), {"doc": d2})
        send(9 * a + 5, piece(a, q), piece(a, q), {"tensor": t1})

    def after_y(a):
        arrived(9 * a + 1, piece(a, q1))
        send(9 * a + 3, piece(a, q1), piece(a, q1), {"doc": d2})
        send(9 * a + 6, piece(a, q1), piece(a, q1), {"tensor": t1})

    def after_z(a):
        arrived(9 * a + 2, piece(a, q2))
        send(9 * a + 7, piece(a, q2), piece(a, q2), {"tensor": t1})
        arrived(9 * a + 3, piece(a, q3))
        send(9 * a + 8, piece(a, q3), piece(a, q3), {"tensor": t1})

    def after_core(a):
        for k, part in enumerate((q, q1, q2, q3)):
            arrived(9 * a + 5 + k, gathered[a].at[t3, part])

    tok_base, vec_base = 36, 39
    own = pl.multiple_of(t * n_seq, n_seq)

    def local(number, src, dst):
        copy = pltpu.make_async_copy(src, dst, local_sem.at[number])
        copy.start()
        return copy

    send_x(0)
    own_q = local(0, w_qkv, wq.at[t])
    own_tok = local(1, tokens.at[pl.ds(own, n_seq)], tok.at[t])
    for k, peer in enumerate((t1, t2, t3)):
        theirs = pl.multiple_of(peer * n_seq, n_seq)
        send(tok_base + k, tokens.at[pl.ds(theirs, n_seq)], tok.at[t], {"tensor": peer})
        send(vec_base + k, vectors, vec.at[t], {"tensor": peer})
    send_core(0)
    own_vec = local(2, vectors, vec.at[t])
    own_o = local(3, w_out, wo.at[t])
    own_u = local(4, w_up, wu.at[t])
    own_d = local(5, w_down, wd.at[t])
    after_x(0)
    after_y(0)
    own_tok.wait()
    own_vec.wait()
    for k, peer in enumerate((t1, t2, t3)):
        arrived(tok_base + k, tok.at[peer])
        arrived(vec_base + k, vec.at[peer])
    for a in (1, 2):
        send_x(a)
        send_core(a)

    stores = []

    def store(src, dst):
        copy = pltpu.make_async_copy(src, dst, out_sem.at[len(stores)])
        copy.start()
        stores.append(copy)

    @pl.loop(0, n_seq)
    def _(s):
        x_s[s] = jnp.concatenate([tok[j, s] for j in range(4)], axis=1)

    store(x_s, x_out)

    key_index = lax.broadcasted_iota(jnp.int32, (seq, seq), 0)

    def attention(part, first):
        @pl.loop(0, n_seq)
        def _(s):
            row = d * (4 * n_seq) + t * n_seq + s
            length = lengths[lax.rem(row, queries), lax.div(row, queries)]
            bias = vec[part, 1:2, :576]
            z = (dot(x_s[s], rows_of(wq[part])) + bias).astype(bf16)
            qkv_s[part, s] = z
            pieces = []
            for h in range(3):
                qh = z[:, h * 64 : h * 64 + 64] * 0.125
                kh = z[:, 192 + h * 64 : 256 + h * 64]
                vh = z[:, 384 + h * 64 : 448 + h * 64]
                st = jnp.where(key_index < length, dot_nt(kh, qh), -1000000000.0)
                high = jnp.max(st, 0, keepdims=True)
                e = jnp.exp(st - high)
                total = jnp.sum(e, 0, keepdims=True)
                prob = (e * (1.0 / total)).astype(bf16)
                lse_s[part, s, h] = high + jnp.log(total)
                pieces.append(dot_tn(vh, prob))
            ctx_s[part, s] = jnp.concatenate(pieces, axis=0).T.astype(bf16)

    def project(part, first):
        @pl.loop(0, n_seq)
        def _(s):
            for n in range(model // 256):
                cols = slice(n * 256, n * 256 + 256)
                term = dot(ctx_s[part, s], rows_of(wo[part, :, :, cols]))
                if first:
                    att_s[s, :, cols] = term
                else:
                    att_s[s, :, cols] += term

    own_q.wait()
    attention(t, True)
    after_x(1)
    after_y(1)
    after_z(0)
    own_o.wait()
    project(t, True)
    arrived(4, wq.at[t1])
    attention(t1, False)
    arrived(9 + 4, wo.at[t1])
    project(t1, False)
    send_x(3)
    send_core(3)
    after_z(1)
    after_x(2)
    after_y(2)
    attention(t2, False)
    project(t2, False)
    after_core(0)
    after_z(2)
    attention(t3, False)
    after_core(1)
    project(t3, False)
    store(qkv_s, qkv_out)
    store(lse_s, lse_out)
    store(ctx_s, ctx_out)
    store(wq, wq_all)
    store(wo, wo_all)

    chunk = 96
    chunks = seq // chunk

    @pl.loop(0, n_seq * chunks)
    def _(i):
        s, r = lax.div(i, chunks), pl.multiple_of(lax.rem(i, chunks) * chunk, chunk)
        rows = pl.ds(r, chunk)
        y = x_s[s, rows].astype(f32) + att_s[s, rows] + b_out[...]
        n1, f1 = norm_forward(y)
        n1_s[s, rows] = n1
        f1_s[s, rows] = f1
        hl_s[s, rows] = (n1 * gain_one[...] + bias_one[...]).astype(bf16)

    store(n1_s, n1_out)
    store(f1_s, f1_out)
    store(hl_s, hl_out)
    after_x(3)
    after_y(3)
    own_u.wait()
    own_d.wait()

    def ffn_up(part):
        @pl.loop(0, n_seq * (model // 256))
        def _(i):
            s, n = lax.div(i, model // 256), lax.rem(i, model // 256)
            cols = pl.ds(pl.multiple_of(n * 256, 256), 256)
            u = dot(hl_s[s], rows_of(wu[part, :, :, cols])) + vec[part, 0:1, cols]
            cdf = 0.5 * (1.0 + lax.erf(u * 0.7071067811865476))
            pdf = jnp.exp(u * u * -0.5) * 0.3989422804014327
            act_s[part, s, :, cols] = (u * cdf).astype(bf16)
            gp_s[part, s, :, cols] = (cdf + u * pdf).astype(bf16)

    def ffn_down(part, first):
        @pl.loop(0, n_seq * (model // 256))
        def _(i):
            s, n = lax.div(i, model // 256), lax.rem(i, model // 256)
            cols = pl.ds(pl.multiple_of(n * 256, 256), 256)
            term = dot(act_s[part, s], rows_of(wd[part, :, :, cols]))
            if first:
                att_s[s, :, cols] = term
            else:
                att_s[s, :, cols] += term

    ffn_up(t)
    ffn_down(t, True)
    after_z(3)
    arrived(2 * 9 + 4, wu.at[t1])
    ffn_up(t1)
    arrived(3 * 9 + 4, wd.at[t1])
    ffn_down(t1, False)
    ffn_up(t2)
    ffn_down(t2, False)
    after_core(2)
    ffn_up(t3)
    after_core(3)
    store(act_s, act_out)
    store(gp_s, gp_out)
    store(wu, wu_all)
    store(wd, wd_all)
    ffn_down(t3, False)

    @pl.loop(0, n_seq * chunks)
    def _(i):
        s, r = lax.div(i, chunks), pl.multiple_of(lax.rem(i, chunks) * chunk, chunk)
        rows = pl.ds(r, chunk)
        y = n1_s[s, rows] * gain_one[...] + bias_one[...] + att_s[s, rows] + b_down[...]
        n2, f2 = norm_forward(y)
        n2_s[s, rows] = n2
        f2_s[s, rows] = f2
        res_s[s, rows] = (n2 * gain_two[...] + bias_two[...]).astype(bf16)

    store(n2_s, n2_out)
    store(f2_s, f2_out)
    store(res_s, res_out)
    for copy in stores:
        copy.wait()
    for copy in started:
        copy.wait_send()


def forward(n_seq, seq, model, queries, lengths, tokens, w_qkv, w_out, w_up, w_down, vectors, rows):
    def sds(shape, dtype):
        return jax.ShapeDtypeStruct(shape, dtype)

    acts = [
        ((n_seq, seq, model), bf16),
        ((4, n_seq, seq, 576), bf16),
        ((4, n_seq, 3, 1, seq), f32),
        ((4, n_seq, seq, 192), bf16),
        ((n_seq, seq, model), f32),
        ((n_seq, seq, 1), f32),
        ((n_seq, seq, model), bf16),
        ((4, n_seq, seq, model), bf16),
        ((4, n_seq, seq, model), bf16),
        ((n_seq, seq, model), f32),
        ((n_seq, seq, 1), f32),
        ((n_seq, seq, model), bf16),
    ]
    weights = [(4,) + w.shape for w in (w_qkv, w_out, w_up, w_down)]
    any_spec = pl.BlockSpec(memory_space=pl.ANY)
    vmem_spec = pl.BlockSpec(memory_space=pltpu.VMEM)
    scratch = [pltpu.VMEM((4, n_seq, seq, model // 4), bf16)]
    scratch += [pltpu.VMEM(*a) for a in acts[:4]]
    scratch += [pltpu.VMEM((n_seq, seq, model), f32)]
    scratch += [pltpu.VMEM(*a) for a in acts[4:]]
    scratch += [pltpu.VMEM(w, bf16) for w in weights]
    scratch += [pltpu.VMEM((4,) + vectors.shape, f32)]
    scratch += [
        pltpu.SemaphoreType.DMA((42,)),
        pltpu.SemaphoreType.DMA((42,)),
        pltpu.SemaphoreType.DMA((6,)),
        pltpu.SemaphoreType.DMA((16,)),
    ]
    return pl.pallas_call(
        functools.partial(forward_kernel, (n_seq, seq, model, queries)),
        out_shape=[sds(*a) for a in acts] + [sds(w, bf16) for w in weights],
        in_specs=[pl.BlockSpec(memory_space=pltpu.SMEM)] + [any_spec] * 6 + [vmem_spec] * 6,
        out_specs=[any_spec] * 16,
        scratch_shapes=scratch,
        compiler_params=pltpu.CompilerParams(
            collective_id=0, has_side_effects=True, vmem_limit_bytes=60 * MIB
        ),
        name="layer_forward",
    )(lengths, tokens, w_qkv, w_out, w_up, w_down, vectors, *rows)


precise = lax.Precision.HIGHEST


def dot_f32(a, b, dims):
    return lax.dot_general(a, b, (dims, ((), ())), precision=precise, preferred_element_type=f32)


def square(block):
    return block.reshape(-1, block.shape[-1])


def norm_back_rows(upstream, normed, factor, gain_row):
    scaled = upstream * gain_row
    mean_one = jnp.mean(scaled, -1, keepdims=True)
    mean_two = jnp.mean(scaled * normed, -1, keepdims=True)
    return factor * (scaled - mean_one - normed * mean_two)


class Reduction:
    def __init__(self, order, bits, remote, send, base, held, hops):
        self.order, self.bits = order, bits
        self.remote, self.send, self.base = remote, send, base
        self.held, self.hops = held, hops
        self.axes = [["x", "z1", "z0", "y"]]
        for name in order:
            self.axes.append([a for a in self.axes[-1] if a != name])

    def buffer(self, hop):
        return self.held if hop == 0 else self.hops[hop - 1]

    def start(self, hop):
        name = self.order[hop]
        bit, peer = self.bits[name]
        place = self.axes[hop].index(name)
        src = self.buffer(hop).at[(slice(None),) * place + (1 - bit,)]
        self.send(self.base + 2 + hop, src, self.buffer(hop + 1), peer)

    def finish(self, hop, out=None):
        name = self.order[hop]
        bit, peer = self.bits[name]
        place = self.axes[hop].index(name)
        src, dst = self.buffer(hop), self.buffer(hop + 1)
        self.remote(self.base + 2 + hop, dst, dst, peer).wait_recv()
        left = len(self.axes[hop + 1])
        if left == 0:
            out[...] = src[(bit,)].astype(f32) + dst[...].astype(f32)
            return

        @pl.loop(0, 2**left)
        def _(i):
            index = []
            for k in range(left):
                index.append(lax.rem(lax.div(i, 2**k), 2))
            index = tuple(index)
            full = index[:place] + (bit,) + index[place:]
            dst[index] = (dst[index].astype(f32) + src[full].astype(f32)).astype(bf16)


def backward_kernel(
    cfg,
    lengths,
    positions,
    targets,
    states,
    doc_ids,
    query_weight,
    doc_table,
    w_query,
    gain_one,
    gain_two,
    vocab,
    out_grad,
    res,
    x_in,
    qkv_in,
    lse_in,
    ctx_in,
    n1_in,
    f1_in,
    hl_in,
    act_in,
    gp_in,
    n2_in,
    f2_in,
    wq_in,
    wo_in,
    wu_in,
    wd_in,
    output,
    nll_out,
    gt_out,
    gs_out,
    gwq_out,
    down_out,
    up_out,
    qk_out,
    vo_out,
    vec_out,
    big,
    head,
    pk,
    lg,
    ut,
    us,
    ur,
    ss,
    sr,
    lb,
    dlog,
    st_all,
    diff,
    og,
    tmp,
    n1,
    n2,
    f1,
    f2,
    dy,
    act,
    gp,
    wq,
    wo,
    wu,
    wd,
    qkv,
    ctx,
    lse,
    d_t,
    x_t,
    d_up,
    dctx,
    dqkv,
    dxb,
    gt,
    sums,
    sums_in,
    qk_send,
    vo_send,
    parts,
    *rest,
):
    n_seq, seq, model, queries, slots, table, docs = cfg
    red_bufs, (send_sem, recv_sem, local_sem) = rest[:-3], rest[-3:]
    m_rows = n_seq * seq
    own_rows = 8 * n_seq
    d = lax.axis_index("doc")
    t = lax.axis_index("tensor")
    t1, t2 = flip(t, 1), flip(t, 2)
    t3 = flip(t1, 2)
    x_bit = lax.div(t, 2)
    bits = {
        "x": (x_bit, {"tensor": t2}),
        "y": (lax.rem(d, 2), {"doc": flip(d, 1)}),
        "z0": (lax.rem(lax.div(d, 2), 2), {"doc": flip(d, 2)}),
        "z1": (lax.div(d, 4), {"doc": flip(d, 4)}),
    }

    barrier = pltpu.get_barrier_semaphore()
    doc_peers = [lax.rem(d + k, docs) for k in range(1, docs)]
    peers = [{"tensor": p} for p in (t1, t2, t3)] + [{"doc": p} for p in doc_peers]
    for peer in peers:
        pl.semaphore_signal(barrier, inc=1, device_id=peer, device_id_type=MESH)
    pl.semaphore_wait(barrier, len(peers))

    def remote(number, src, dst, peer):
        return pltpu.make_async_remote_copy(
            src_ref=src,
            dst_ref=dst,
            send_sem=send_sem.at[number],
            recv_sem=recv_sem.at[number],
            device_id=peer,
            device_id_type=MESH,
        )

    started = []

    def send(number, src, dst, peer):
        copy = remote(number, src, dst, peer)
        copy.start()
        started.append(copy)

    def arrived(number, ref):
        remote(number, ref, ref, {"tensor": t1}).wait_recv()

    loads = {}

    def load(name, src, dst):
        copy = pltpu.make_async_copy(src, dst, local_sem.at[len(loads)])
        copy.start()
        loads[name] = copy

    own = pl.multiple_of(t * n_seq, n_seq)
    load("head", res.at[:, pl.ds(0, 32)], head)
    load("vocab", vocab, big)
    base = 0
    st_all[d] = states[...]
    for k, p in enumerate(doc_peers):
        send(base + k, states, st_all.at[d], {"doc": p})
    states_base = base
    base += docs - 1
    load("og", out_grad.at[pl.ds(own, n_seq)], og)
    load("n2", n2_in, n2)
    load("f2", f2_in, f2)
    order = (t3, t1, t2, t)
    load("act0", act_in.at[order[0]], act.at[0])
    load("act1", act_in.at[order[1]], act.at[1])
    for i in range(2):
        load("wd%d" % i, wd_in.at[order[i]], wd.at[i])
        load("wu%d" % i, wu_in.at[order[i]], wu.at[i])
    load("gp0", gp_in.at[order[0]], gp.at[0])
    load("gp1", gp_in.at[order[1]], gp.at[1])
    load("hl", hl_in, tmp)
    load("n1", n1_in, n1)
    load("f1", f1_in, f1)
    load("wo", wo_in, wo)
    for i in range(2):
        load("wq%d" % i, wq_in.at[order[i]], wq.at[i])
        load("qkv%d" % i, qkv_in.at[order[i]], qkv.at[i])
    load("ctx", ctx_in, ctx)
    load("lse", lse_in, lse)
    first_row = d * (4 * n_seq)
    lane = lax.broadcasted_iota(jnp.int32, (own_rows, 32 * n_seq), 1)
    line = lax.broadcasted_iota(jnp.int32, (own_rows, 32 * n_seq), 0)
    spot = jnp.zeros((own_rows, 32 * n_seq), jnp.int32)
    for b in range(own_rows):
        query = lax.rem(first_row + t * n_seq + b // 8, queries)
        spot = jnp.where(line == b, positions[query, b % 8] + 32 * (b // 8), spot)
    hot = (lane == spot).astype(f32)
    hot_low = hot.astype(bf16)
    loads["head"].wait()
    pk[t] = dot(hot_low, rows_of(head[...])).astype(bf16)
    pick_base = base
    for k, p in enumerate((t1, t2, t3)):
        send(base + k, pk.at[t], pk.at[t], {"tensor": p})
    base += 3
    out_base = base
    base += 3
    send(out_base, res, output.at[pl.ds(own, n_seq)], {"tensor": t2})
    send(out_base + 1, res, output.at[pl.ds(own, n_seq)], {"tensor": t1})
    load("out", res, output.at[pl.ds(own, n_seq)])
    all_rows = 4 * own_rows
    vocab_local = vocab.shape[0] * model
    chunk = model
    tall = lax.broadcasted_iota(jnp.int32, (all_rows, 1), 0)
    goal = jnp.zeros((all_rows, 1), jnp.int32)
    for b in range(all_rows):
        query = lax.rem(first_row + b // 8, queries)
        goal = jnp.where(tall == b, targets[query, b % 8], goal)
    goal = goal - t * vocab_local
    for k, p in enumerate((t1, t2, t3)):
        arrived(pick_base + k, pk.at[p])
    loads["vocab"].wait()

    @pl.loop(0, vocab_local // chunk)
    def _(j):
        start = pl.multiple_of(j * chunk, chunk)
        lg[:, pl.ds(start, chunk)] = dot_nt(rows_of(pk[...]), square(big[j]))

    high = jnp.max(lg[...], 1, keepdims=True)
    ut[...] = jnp.zeros_like(ut)

    def vocab_step(j, carry):
        mass, chosen = carry
        start = pl.multiple_of(j * chunk, chunk)
        values = lg[:, pl.ds(start, chunk)]
        e = jnp.exp(values - high)
        index = lax.broadcasted_iota(jnp.int32, (all_rows, chunk), 1) + start
        hits = (index == goal).astype(f32)
        both = jnp.concatenate([e, hits], 0).astype(bf16)
        ut[...] += dot(both, square(big[j]))
        mass = mass + jnp.sum(e, 1, keepdims=True)
        chosen = chosen + jnp.sum(hits * values, 1, keepdims=True)
        return mass, chosen

    zero = jnp.zeros((all_rows, 1), f32)
    mass, chosen = lax.fori_loop(0, vocab_local // chunk, vocab_step, (zero, zero))
    spread = lax.broadcasted_iota(jnp.int32, (all_rows, 128), 1)
    stats = jnp.where(spread == 0, high, jnp.where(spread == 1, mass, chosen))
    mean_row = (ut[:all_rows] * (1.0 / mass)).astype(bf16)
    goal_row = ut[all_rows:].astype(bf16)
    for j in range(4):
        part = slice(j * own_rows, (j + 1) * own_rows)
        us[j, :, :model] = mean_row[part]
        us[j, :, model:] = goal_row[part]
        ss[j] = stats[part]
    part_base = base
    base += 6
    for k, p in enumerate((t1, t2, t3)):
        send(part_base + k, ss.at[p], sr.at[t], {"tensor": p})
        send(part_base + 3 + k, us.at[p], ur.at[t], {"tensor": p})
    sr[t] = ss[t]
    ur[t] = us[t]
    for k, p in enumerate((t1, t2, t3)):
        arrived(part_base + k, sr.at[p])
    highs = [sr[j, :, 0:1] for j in range(4)]
    top = jnp.maximum(jnp.maximum(highs[0], highs[1]), jnp.maximum(highs[2], highs[3]))
    weights = [sr[j, :, 1:2] * jnp.exp(highs[j] - top) for j in range(4)]
    whole = weights[0] + weights[1] + weights[2] + weights[3]
    picked_logit = sr[0, :, 2:3] + sr[1, :, 2:3] + sr[2, :, 2:3] + sr[3, :, 2:3]
    loglik = picked_logit - (top + jnp.log(whole))
    mine = first_row + t * n_seq
    for s in range(n_seq):
        total = jnp.sum(loglik[8 * s : 8 * s + 8], 0, keepdims=True)
        lb[mine + s] = jnp.broadcast_to(total, (1, 128))
    like_base = base
    base += 3
    mine_ref = lb.at[pl.ds(mine, n_seq)]
    for k, p in enumerate((t1, t2, t3)):
        send(like_base + k, mine_ref, mine_ref, {"tensor": p})
    for k, p in enumerate((t1, t2, t3)):
        arrived(part_base + 3 + k, ur.at[p])
    gap = jnp.zeros((own_rows, model), f32)
    for j in range(4):
        share = weights[j] / whole
        gap = gap + ur[j, :, model:].astype(f32) - share * ur[j, :, :model].astype(f32)
    diff[...] = gap
    for k, p in enumerate((t1, t2, t3)):
        arrived(like_base + k, lb.at[pl.ds(first_row + p * n_seq, n_seq)])
    group_base = base
    base += docs - 1
    group_ref = lb.at[pl.ds(first_row, 4 * n_seq)]
    for k, p in enumerate(doc_peers):
        send(group_base + k, group_ref, group_ref, {"doc": p})
    for k in range(docs - 1):
        source = lax.rem(d + docs - 1 - k, docs)
        arrived(states_base + k, st_all.at[source])
    share_width = model // docs
    emb = jnp.zeros((states.shape[0], 128), f32)
    for j in range(docs):
        emb = emb + dot(st_all[j, :, :share_width], w_query[j])
    emb = emb[:queries]
    table_score = dot_f32(emb, doc_table[...], ((1,), (1,)))
    entry = lax.broadcasted_iota(jnp.int32, (queries, table), 1)
    hot_docs = [(entry == doc_ids[:, k : k + 1]).astype(f32) for k in range(slots)]
    prior = [jnp.sum(hot_docs[k] * table_score, 1, keepdims=True) for k in range(slots)]
    for k in range(docs - 1):
        source = lax.rem(d + docs - 1 - k, docs)
        arrived(group_base + k, lb.at[pl.ds(source * (4 * n_seq), 4 * n_seq)])
    joint = []
    for k in range(slots):
        column = lb[k * queries : (k + 1) * queries].reshape(queries, 128)
        joint.append(prior[k] + column[:, 0:1])

    def log_sum(values):
        largest = functools.reduce(jnp.maximum, values)
        total = functools.reduce(jnp.add, [jnp.exp(v - largest) for v in values])
        return largest + jnp.log(total)

    prior_lse, joint_lse = log_sum(prior), log_sum(joint)
    nll_out[...] = jnp.broadcast_to(prior_lse - joint_lse, (queries, 128))
    spread_docs = jnp.zeros((queries, table), f32)
    for k in range(slots):
        post = jnp.exp(joint[k] - joint_lse)
        before = jnp.exp(prior[k] - prior_lse)
        spread_docs = spread_docs + hot_docs[k] * (query_weight[...] * (before - post))
        value = -query_weight[...] * post
        dlog[k * queries : (k + 1) * queries] = jnp.broadcast_to(value, (queries, 128)).reshape(
            queries, 1, 128
        )
    d_emb = dot_f32(spread_docs, doc_table[...], ((1,), (0,))).astype(bf16)
    gs_out[...] = dot_nt(d_emb, w_query[d])
    gwq_out[...] = dot_tn(st_all[d, :queries, :share_width].astype(f32), d_emb.astype(f32))
    scattered = []
    for s in range(n_seq):
        coefficient = dlog[mine + s]
        rows = diff[8 * s : 8 * s + 8] * coefficient[:, 0:1]
        scattered.append(
            dot_f32(hot[8 * s : 8 * s + 8, 32 * s : 32 * s + 32], rows, ((0,), (0,)))
        )
    sums[0] = jnp.zeros(sums.shape[1:], f32)
    for name in ("og", "n2", "f2"):
        loads[name].wait()
    step_rows = 96

    def add_sum(row, value):
        sums[0, 4, row : row + 1] += jnp.sum(value, 0, keepdims=True)

    def second_norm(s, rows, flat, extra):
        upstream = og[s, rows].astype(f32)
        if extra is not None:
            upstream = upstream + extra
        normed = n2[flat]
        back = norm_back_rows(upstream, normed, f2[flat], gain_two[...])
        add_sum(4, upstream * normed)
        add_sum(5, upstream)
        add_sum(3, back)
        dy[flat] = back
        og[s, rows] = back.astype(bf16)

    for s in range(n_seq):
        extra = jnp.concatenate([scattered[s], jnp.zeros((step_rows - 32, model), f32)], 0)
        second_norm(s, pl.ds(0, step_rows), pl.ds(s * seq, step_rows), extra)

        @pl.loop(1, seq // step_rows)
        def _(i):
            start = pl.multiple_of(i * step_rows, step_rows)
            second_norm(s, pl.ds(start, step_rows), pl.ds(s * seq + start, step_rows), None)

    d_t[...] = rows_of(og[...]).T
    orders = (
        ("y", "z0", "x", "z1"),
        ("z0", "y", "x", "z1"),
        ("y", "z0", "x", "z1"),
        ("z0", "y", "x", "z1"),
    )
    reds = []
    for k, names in enumerate(orders):
        bufs = red_bufs[5 * k : 5 * k + 5]
        reds.append(Reduction(names, bits, remote, send, base, bufs[0], bufs[1:]))
        base += 6
    down, up, qk, vo = reds
    block_shape = (2, 2, 2, model // docs)

    def emit(red, i, sending, shard, lanes, value):
        value = value.reshape(block_shape + (value.shape[-1],))
        which = lax.div(shard, 2)
        if i < 2:
            sending[which, :, :, :, :, lanes] = value.astype(bf16)
        else:
            total = value + red.held[which, :, :, :, :, lanes].astype(f32)
            red.held[which, :, :, :, :, lanes] = total.astype(bf16)

    def before_block(red, i, shard):
        if i >= 2:
            which = lax.div(shard, 2)
            arrived(red.base + (i - 2), red.held.at[which])

    def after_block(red, i, sending, shard):
        if i < 2:
            which = lax.div(shard, 2)
            send(red.base + i, sending.at[which], red.held.at[which], {"tensor": t1})

    down_send, up_send = big.at[0:2], big.at[2:4]
    tiles = model // 256
    for i, shard in enumerate(order):
        loads["act%d" % i].wait()
        before_block(down, i, shard)

        @pl.loop(0, tiles)
        def _(n):
            lanes = pl.ds(pl.multiple_of(n * 256, 256), 256)
            emit(down, i, down_send, shard, lanes, dot(d_t[...], act[i % 2, :, lanes]))

        if i + 2 < 4:
            load("act%d" % (i + 2), act_in.at[order[i + 2]], act.at[i % 2])
        after_block(down, i, down_send, shard)
    down.start(0)
    loads["hl"].wait()
    x_t[...] = tmp[...].T
    load("x", x_in, tmp)
    for i, shard in enumerate(order):
        for name in ("gp", "wd", "wu"):
            loads["%s%d" % (name, i)].wait()
        before_block(up, i, shard)

        @pl.loop(0, tiles)
        def _(n):
            lanes = pl.ds(pl.multiple_of(n * 256, 256), 256)
            value = dot_nt(rows_of(og[...]), wd[i % 2, lanes]) * gp[i % 2, :, lanes].astype(f32)
            low = value.astype(bf16)
            d_up[:, lanes] = low
            sums[0, shard, 0:1, lanes] = jnp.sum(low.astype(f32), 0, keepdims=True)

        if i + 2 < 4:
            load("gp%d" % (i + 2), gp_in.at[order[i + 2]], gp.at[i % 2])
            load("wd%d" % (i + 2), wd_in.at[order[i + 2]], wd.at[i % 2])

        @pl.loop(0, tiles)
        def _(n):
            lanes = pl.ds(pl.multiple_of(n * 256, 256), 256)
            value = dot_nt(d_up[...], wu[i % 2, lanes])
            if i == 0:
                n2[:, lanes] = value
            else:
                n2[:, lanes] += value
            emit(up, i, up_send, shard, lanes, dot(x_t[...], d_up[:, lanes]))

        if i + 2 < 4:
            load("wu%d" % (i + 2), wu_in.at[order[i + 2]], wu.at[i % 2])
        after_block(up, i, up_send, shard)
    up.start(0)
    arrived(out_base, output.at[pl.ds(t2 * n_seq, n_seq)])
    passed = output.at[pl.ds(t2 * n_seq, n_seq)]
    send(out_base + 2, passed, passed, {"tensor": t1})
    loads["n1"].wait()
    loads["f1"].wait()

    @pl.loop(0, m_rows // step_rows)
    def _(i):
        flat = pl.ds(pl.multiple_of(i * step_rows, step_rows), step_rows)
        s, start = lax.div(i, seq // step_rows), lax.rem(i, seq // step_rows) * step_rows
        upstream = dy[flat] + n2[flat]
        normed = n1[flat]
        back = norm_back_rows(upstream, normed, f1[flat], gain_one[...])
        add_sum(1, upstream * normed)
        add_sum(2, upstream)
        add_sum(0, back)
        dy[flat] = back
        og[s, pl.ds(pl.multiple_of(start, step_rows), step_rows)] = back.astype(bf16)

    d_t[...] = rows_of(og[...]).T
    loads["x"].wait()
    x_t[...] = tmp[...].T
    for name in ("wo", "ctx", "lse"):
        loads[name].wait()
    key_index = lax.broadcasted_iota(jnp.int32, (seq, seq), 0)
    for i, shard in enumerate(order):
        loads["qkv%d" % i].wait()
        loads["wq%d" % i].wait()
        dctx[...] = dot_nt(rows_of(og[...]), wo[shard]).astype(bf16)

        @pl.loop(0, n_seq)
        def _(s):
            rows = pl.ds(pl.multiple_of(s * seq, 32), seq)
            row = first_row + t * n_seq + s
            length = lengths[lax.rem(row, queries), lax.div(row, queries)]
            z = qkv[i % 2, s]
            upstream = dctx[rows]
            d_q, d_k, d_v = [], [], []
            for h in range(3):
                qh = z[:, h * 64 : h * 64 + 64]
                kh = z[:, 192 + h * 64 : 256 + h * 64]
                vh = z[:, 384 + h * 64 : 448 + h * 64]
                dc = upstream[:, h * 64 : h * 64 + 64]
                scores = jnp.where(key_index < length, dot_nt(kh, qh * 0.125), -1000000000.0)
                prob = jnp.exp(scores - lse[shard, s, h])
                d_v.append(dot(prob.astype(bf16), dc))
                d_prob = dot_nt(vh, dc)
                inner = jnp.sum(d_prob * prob, 0, keepdims=True)
                d_score = (prob * (d_prob - inner)).astype(bf16)
                d_k.append(dot(d_score, qh) * 0.125)
                d_q.append(dot_tn(kh, d_score) * 0.125)
            first = jnp.concatenate(d_q, 0).T
            both = jnp.concatenate([first] + d_k + d_v, 1).astype(bf16)
            dqkv[rows] = both
            lse_sum = jnp.sum(both.astype(f32), 0, keepdims=True)
            parts[s] = lse_sum

        total = parts[0]
        for s in range(1, n_seq):
            total = total + parts[s]
        sums[0, shard, 1:2, : 3 * 192] = total
        before_block(qk, i, shard)
        emit(qk, i, qk_send, shard, slice(None), dot(x_t[...], dqkv[:, :384]))
        after_block(qk, i, qk_send, shard)
        before_block(vo, i, shard)
        value = jnp.concatenate([dot(x_t[...], dqkv[:, 384:]), dot(d_t[...], ctx[shard])], 1)
        emit(vo, i, vo_send, shard, slice(None), value)
        after_block(vo, i, vo_send, shard)

        @pl.loop(0, tiles)
        def _(n):
            lanes = pl.ds(pl.multiple_of(n * 256, 256), 256)
            value = dot_nt(dqkv[...], wq[i % 2, lanes])
            if i == 0:
                n1[:, lanes] = value
            else:
                n1[:, lanes] += value

        if i + 2 < 4:
            load("qkv%d" % (i + 2), qkv_in.at[order[i + 2]], qkv.at[i % 2])
            load("wq%d" % (i + 2), wq_in.at[order[i + 2]], wq.at[i % 2])

    for j in range(4):
        lanes = slice(j * 192, j * 192 + 192)
        dxb[j] = (n1[:, lanes] + dy[:, lanes]).astype(bf16)
    tok_base = base
    base += 3
    for k, p in enumerate((t2, t3, t1)):
        send(tok_base + k, dxb.at[p], gt.at[t], {"tensor": p})
    gt[t] = dxb[t]
    vec_base = base
    vec_peers = [{"tensor": t1}, bits["y"][1], bits["z0"][1], bits["x"][1], bits["z1"][1]]
    base += len(vec_peers)

    def vec_start(k):
        send(vec_base + k, sums.at[k], sums_in.at[k], vec_peers[k])

    def vec_finish(k):
        arrived(vec_base + k, sums_in.at[k])
        sums[k + 1] = sums[k] + sums_in[k]

    qk.start(0)
    vo.start(0)
    vec_start(0)
    vec_finish(0)
    vec_start(1)
    down.finish(0)
    down.start(1)
    up.finish(0)
    up.start(1)
    vec_finish(1)
    vec_start(2)
    down.finish(1)
    down.start(2)
    up.finish(1)
    up.start(2)
    vec_finish(2)
    vec_start(3)
    qk.finish(0)
    qk.start(1)
    vo.finish(0)
    vo.start(1)
    down.finish(2)
    down.start(3)
    up.finish(2)
    up.start(3)
    vec_finish(3)
    vec_start(4)
    for k, p in enumerate((t2, t3, t1)):
        arrived(tok_base + k, gt.at[p])
    load("gt", gt, gt_out)
    qk.finish(1)
    qk.start(2)
    vo.finish(1)
    vo.start(2)
    down.finish(3, down_out)
    up.finish(3, up_out)
    vec_finish(4)
    vec_out[...] = sums[5]
    qk.finish(2)
    qk.start(3)
    vo.finish(2)
    vo.start(3)
    qk.finish(3, qk_out)
    vo.finish(3, vo_out)
    arrived(out_base + 1, output.at[pl.ds(t1 * n_seq, n_seq)])
    arrived(out_base + 2, output.at[pl.ds(t3 * n_seq, n_seq)])
    loads["out"].wait()
    loads["gt"].wait()
    for copy in started:
        copy.wait_send()


def backward(
    n_seq,
    seq,
    model,
    docs,
    tables,
    vocab,
    out_grad,
    kept,
):
    lengths, positions, targets, states, doc_ids, query_weight, doc_table, w_query = tables[:8]
    queries, slots = doc_ids.shape
    table = doc_table.shape[0]
    m_rows = n_seq * seq
    own_rows = 8 * n_seq
    all_rows = 4 * own_rows
    share = model // docs
    (res, x, qkv, lse, ctx, n1, f1, hl, act, gp, n2, f2, wq, wo, wu, wd) = kept

    def flat(a):
        return a.reshape(a.shape[:-3] + (a.shape[-3] * a.shape[-2], a.shape[-1]))

    kept = [
        res,
        flat(x),
        qkv,
        lse,
        flat(ctx),
        flat(n1),
        flat(f1),
        flat(hl),
        flat(act),
        flat(gp),
        flat(n2),
        flat(f2),
        flat(wq),
        flat(wo),
        flat(wu),
        flat(wd),
    ]
    vocab = vocab.reshape(vocab.shape[0] // model, 2, 2, 2, share, model)

    def sds(shape, dtype):
        return jax.ShapeDtypeStruct(shape, dtype)

    any_spec = pl.BlockSpec(memory_space=pl.ANY)
    vmem_spec = pl.BlockSpec(memory_space=pltpu.VMEM)
    smem_spec = pl.BlockSpec(memory_space=pltpu.SMEM)
    outs = [
        sds((4 * n_seq, seq, model), bf16),
        sds((queries, 128), f32),
        sds((4, m_rows, model // 4), bf16),
        sds((queries, share), f32),
        sds((share, 128), f32),
        sds((share, model), f32),
        sds((share, model), f32),
        sds((share, 384), f32),
        sds((share, 384), f32),
        sds((5, 8, model), f32),
    ]
    out_specs = [any_spec, vmem_spec, any_spec] + [vmem_spec] * 7

    def vm(shape, dtype):
        return pltpu.VMEM(shape, dtype)

    scratch = [
        vm(vocab.shape, bf16),
        vm((n_seq, 32, model), bf16),
        vm((4, own_rows, model), bf16),
        vm((all_rows, vocab.shape[0] * model), f32),
        vm((2 * all_rows, model), f32),
        vm((4, own_rows, 2 * model), bf16),
        vm((4, own_rows, 2 * model), bf16),
        vm((4, own_rows, 128), f32),
        vm((4, own_rows, 128), f32),
        vm((docs * 4 * n_seq, 1, 128), f32),
        vm((docs * 4 * n_seq, 1, 128), f32),
        vm((docs,) + states.shape, bf16),
        vm((own_rows, model), f32),
        vm((n_seq, seq, model), bf16),
        vm((m_rows, model), bf16),
        vm((m_rows, model), f32),
        vm((m_rows, model), f32),
        vm((m_rows, 1), f32),
        vm((m_rows, 1), f32),
        vm((m_rows, model), f32),
        vm((2, m_rows, model), bf16),
        vm((2, m_rows, model), bf16),
        vm((2, model, 576), bf16),
        vm((4, 192, model), bf16),
        vm((2, model, model), bf16),
        vm((2, model, model), bf16),
        vm((2, n_seq, seq, 576), bf16),
        vm((4, m_rows, 192), bf16),
        vm((4, n_seq, 3, 1, seq), f32),
        vm((model, m_rows), bf16),
        vm((model, m_rows), bf16),
        vm((m_rows, model), bf16),
        vm((m_rows, 192), bf16),
        vm((m_rows, 576), bf16),
        vm((4, m_rows, 192), bf16),
        vm((4, m_rows, 192), bf16),
        vm((6, 5, 8, model), f32),
        vm((5, 5, 8, model), f32),
        vm((2, 2, 2, 2, share, 384), bf16),
        vm((2, 2, 2, 2, share, 384), bf16),
        vm((n_seq, 1, 576), f32),
    ]
    for width in (model, model, 384, 384):
        for left in (4, 3, 2, 1, 0):
            scratch.append(vm((2,) * left + (share, width), bf16))
    copies = 2 * (docs - 1) + 3 + 3 + 6 + 3 + 6 * 4 + 3 + 5
    scratch += [
        pltpu.SemaphoreType.DMA((copies,)),
        pltpu.SemaphoreType.DMA((copies,)),
        pltpu.SemaphoreType.DMA((40,)),
    ]
    return pl.pallas_call(
        functools.partial(backward_kernel, (n_seq, seq, model, queries, slots, table, docs)),
        out_shape=outs,
        in_specs=[smem_spec] * 3 + [vmem_spec] * 7 + [any_spec] * 18,
        out_specs=out_specs,
        scratch_shapes=scratch,
        compiler_params=pltpu.CompilerParams(
            collective_id=1, has_side_effects=True, vmem_limit_bytes=60 * MIB
        ),
        name="layer_backward",
    )(*tables, vocab, out_grad, *kept)


def joined(array, axis, combine):
    everything = jax.tree.map(lambda part: lax.all_gather(part, axis), array)
    initial = jax.tree.map(lambda part: part[0], everything)

    def step(k, so_far):
        return combine(so_far, jax.tree.map(lambda part: part[k], everything))

    return lax.fori_loop(1, lax.axis_size(axis), step, initial)


def norm_back(upstream, normed, factor, gain_vec):
    scaled = upstream * gain_vec
    inner = (
        scaled
        - jnp.mean(scaled, -1, keepdims=True)
        - normed * jnp.mean(scaled * normed, -1, keepdims=True)
    )
    return (inner * factor, jnp.sum(upstream * normed, 0), jnp.sum(upstream, 0))


def merge_pair(high_first, mass_first, high_second, mass_second):
    highest = jnp.maximum(high_first, high_second)
    return (
        highest,
        mass_first * jnp.exp(high_first - highest) + mass_second * jnp.exp(high_second - highest),
    )


def vocab_combine(first, second):
    highest, summed = merge_pair(first[0], first[1], second[0], second[1])
    return (highest, summed, first[2] + second[2])


def query_combine(first, second):
    prior_high, prior_mass = merge_pair(first[0], first[1], second[0], second[1])
    joint_high, joint_mass = merge_pair(first[2], first[3], second[2], second[3])
    return (prior_high, prior_mass, joint_high, joint_mass)


def partial_lse(members, values):
    highest = jnp.max(jnp.where(members, values[:, None], -1e30), 0)
    summed = jnp.sum(jnp.where(members, jnp.exp(values[:, None] - highest[None, :]), 0.0), 0)
    return (highest, summed)


def shards(
    tokens,
    query_states,
    w_qkv,
    b_qv,
    w_out,
    b_out,
    ln1_gain,
    ln1_bias,
    w_up,
    b_up,
    w_down,
    b_down,
    ln2_gain,
    ln2_bias,
    w_query,
    doc_table,
    vocab_table,
    doc_ids,
    lengths,
    positions,
    targets,
    out_grad,
    query_weight,
):
    sequences, seq_length, part_width = tokens.shape
    model_width = w_qkv.shape[1]
    n_seq = sequences // 4
    row_count = n_seq * seq_length
    queries = lengths.shape[0]
    t = lax.axis_index("tensor")
    packed_qkv = jnp.concatenate([w_qkv[0], w_qkv[1], w_qkv[2]], 1).reshape(4, 192, 576)
    hidden = w_up.shape[1]
    vectors = jnp.zeros((8, hidden), f32)
    vectors = vectors.at[0].set(b_up).at[1, :192].set(b_qv[0]).at[1, 384:576].set(b_qv[1])
    rows = [v[None, :] for v in (b_out, ln1_gain, ln1_bias, b_down, ln2_gain, ln2_bias)]
    (x, qkv, lse, ctx, n1, f1, hl, act, gp, n2, f2, res, wq, wo, wu, wd) = forward(
        n_seq,
        seq_length,
        model_width,
        queries,
        lengths,
        tokens,
        packed_qkv,
        w_out.reshape(4, 48, model_width),
        w_up.reshape(4, 192, hidden),
        w_down.reshape(4, 192, model_width),
        vectors,
        rows,
    )
    docs = lax.axis_size("doc")
    if docs == 8 and n_seq == 2:
        share = model_width // docs
        states_rows = max(16, -(-queries // 16) * 16)
        states = jnp.zeros((states_rows, 128), bf16).at[:queries, :share].set(query_states)
        tables = (
            lengths,
            positions,
            targets,
            states,
            doc_ids,
            query_weight[:, None],
            doc_table,
            w_query.reshape(docs, share, w_query.shape[1]),
            rows[1],
            rows[4],
        )
        kept = (res, x, qkv, lse, ctx, n1, f1, hl, act, gp, n2, f2, wq, wo, wu, wd)
        (output, nll, gt, gs, gwq, g_down, g_up, g_qk, g_vo, sums) = backward(
            n_seq, seq_length, model_width, docs, tables, vocab_table, out_grad, kept
        )
        d = lax.axis_index("doc")
        six = lax.dynamic_slice_in_dim(sums[4, :6], d * share, share, 1)
        mine = lax.dynamic_index_in_dim(sums[:4], t, 0, keepdims=False)
        return (
            output,
            nll[:, 0],
            gt.reshape(sequences, seq_length, part_width).astype(f32),
            gs,
            jnp.stack([g_qk[:, :192], g_qk[:, 192:], g_vo[:, :192]]),
            jnp.stack([mine[1, :192], mine[1, 384:576]]),
            g_vo[:, 192:].T,
            six[0],
            six[1],
            six[2],
            g_up,
            mine[0],
            g_down.T,
            six[3],
            six[4],
            six[5],
            gwq,
        )
    output = lax.all_gather(res, "tensor", axis=0, tiled=True)
    row_index = lax.axis_index("doc") * sequences + jnp.arange(sequences, dtype=jnp.int32)
    slot_index = row_index // queries
    query_index = row_index % queries
    row_position = positions[query_index]
    row_target = targets[query_index]
    own = lambda a: lax.dynamic_slice_in_dim(a, t * n_seq, n_seq, 0)
    own_position = own(row_position)
    seq_base = jnp.arange(n_seq, dtype=jnp.int32)[:, None]
    picked = lax.all_gather(res[seq_base, own_position], "tensor", axis=0, tiled=True)
    vocab_logits = jnp.einsum("btd,vd->btv", picked, vocab_table, preferred_element_type=f32)
    vocab_local = vocab_table.shape[0]
    vocab_ids = t * vocab_local + jnp.arange(vocab_local, dtype=jnp.int32)
    target_hits = vocab_ids[None, None, :] == row_target[:, :, None]
    local_high = jnp.max(vocab_logits, -1)
    local_mass = jnp.sum(jnp.exp(vocab_logits - local_high[:, :, None]), -1)
    local_chosen = jnp.sum(jnp.where(target_hits, vocab_logits, 0.0), -1)
    vocab_high, vocab_mass, chosen = joined(
        (local_high, local_mass, local_chosen), "tensor", vocab_combine
    )
    vocab_lse = vocab_high + jnp.log(vocab_mass)
    loglik = jnp.sum(chosen - vocab_lse, -1)
    states = lax.all_gather(query_states, "doc", axis=1, tiled=True)
    query_emb = jnp.dot(states, w_query, preferred_element_type=f32)
    members = query_index[:, None] == jnp.arange(queries, dtype=jnp.int32)[None, :]
    member_weights = members.astype(f32)
    own_emb = jnp.dot(member_weights, query_emb, precision=precise)
    embeds = doc_table[doc_ids[query_index, slot_index]]
    retrieval = jnp.sum(own_emb * embeds, -1)
    joint_score = retrieval + loglik
    prior_high, prior_mass = partial_lse(members, retrieval)
    joint_high, joint_mass = partial_lse(members, joint_score)
    prior_high, prior_mass, joint_high, joint_mass = joined(
        (prior_high, prior_mass, joint_high, joint_mass), "doc", query_combine
    )
    prior_lse = prior_high + jnp.log(prior_mass)
    joint_lse = joint_high + jnp.log(joint_mass)
    query_nll = prior_lse - joint_lse
    row_weight = query_weight[query_index]
    posterior = jnp.exp(joint_score - jnp.dot(member_weights, joint_lse, precision=precise))
    prior_prob = jnp.exp(retrieval - jnp.dot(member_weights, prior_lse, precision=precise))
    grad_loglik = -row_weight * posterior
    grad_retrieval = row_weight * (prior_prob - posterior)
    vocab_probs = jnp.exp(vocab_logits - vocab_lse[:, :, None])
    grad_logits = (grad_loglik[:, None, None] * (target_hits.astype(f32) - vocab_probs)).astype(
        bf16
    )
    grad_picked = lax.psum_scatter(
        jnp.einsum("btv,vd->btd", grad_logits, vocab_table, preferred_element_type=f32),
        "tensor",
        scatter_dimension=0,
        tiled=True,
    )
    grad_emb = jnp.dot(
        member_weights.T, grad_retrieval[:, None] * embeds, precision=precise
    ).astype(bf16)
    grad_w_query = jnp.dot(states.T, grad_emb, preferred_element_type=f32)
    grad_states = jnp.dot(grad_emb, w_query.T, preferred_element_type=f32)
    flat = lambda a: a.reshape(row_count, a.shape[-1])
    grad_result = flat(own(out_grad).astype(f32).at[seq_base, own_position].add(grad_picked))
    n1, f1, n2, f2, hl, x = flat(n1), flat(f1), flat(n2), flat(f2), flat(hl), flat(x)
    dy2, dg2, db2 = norm_back(grad_result, n2, f2, ln2_gain)
    d_low = dy2.astype(bf16)
    act, gp = act.reshape(4, row_count, hidden), gp.reshape(4, row_count, hidden)
    wu, wd = wu.reshape(4, model_width, hidden), wd.reshape(4, hidden, model_width)
    wq, wo = wq.reshape(4, model_width, 576), wo.reshape(4, 192, model_width)
    qkv, ctx = qkv.reshape(4, n_seq, seq_length, 576), ctx.reshape(4, row_count, 192)
    g_down = jnp.einsum("tmf,md->tfd", act, d_low, preferred_element_type=f32)
    d_act = jnp.einsum("md,tfd->tmf", d_low, wd, preferred_element_type=f32)
    d_up = (d_act * gp.astype(f32)).astype(bf16)
    g_up = jnp.einsum("md,tmf->tdf", hl, d_up, preferred_element_type=f32)
    g_b_up = jnp.sum(d_up.astype(f32), 1)
    d_hidden = dy2 + jnp.einsum("tmf,tdf->md", d_up, wu, preferred_element_type=f32)
    dy1, dg1, db1 = norm_back(d_hidden, n1, f1, ln1_gain)
    d_att = dy1.astype(bf16)
    g_out = jnp.einsum("tme,md->ted", ctx, d_att, preferred_element_type=f32)
    d_ctx = jnp.einsum("md,ted->tme", d_att, wo, preferred_element_type=f32).astype(bf16)
    d_ctx = d_ctx.reshape(4, n_seq, seq_length, 3, 64)
    heads = qkv.reshape(4, n_seq, seq_length, 3, 3, 64)
    hq, hk, hv = heads[:, :, :, 0], heads[:, :, :, 1], heads[:, :, :, 2]
    row_length = own(lengths[query_index, slot_index])
    key_mask = (jnp.arange(seq_length, dtype=jnp.int32)[None, :] < row_length[:, None])[
        None, :, None, None, :
    ]
    scores = jnp.einsum("tbqhe,tbkhe->tbhqk", hq, hk, preferred_element_type=f32) * 0.125
    scores = jnp.where(key_mask, scores, -1000000000.0)
    prob = jnp.exp(scores - lse.reshape(4, n_seq, 3, seq_length, 1))
    d_v = jnp.einsum("tbhqk,tbqhe->tbkhe", prob.astype(bf16), d_ctx, preferred_element_type=f32)
    d_prob = jnp.einsum("tbqhe,tbkhe->tbhqk", d_ctx, hv, preferred_element_type=f32)
    d_s = (prob * (d_prob - jnp.sum(d_prob * prob, -1, keepdims=True))).astype(bf16)
    d_q = jnp.einsum("tbhqk,tbkhe->tbqhe", d_s, hk, preferred_element_type=f32) * 0.125
    d_k = jnp.einsum("tbhqk,tbqhe->tbkhe", d_s, hq, preferred_element_type=f32) * 0.125
    d_qkv = jnp.stack([d_q, d_k, d_v], 3).reshape(4, row_count, 576).astype(bf16)
    g_b = jnp.sum(d_qkv.astype(f32), 1)
    g_qkv = jnp.einsum("md,tme->tde", x, d_qkv, preferred_element_type=f32)
    d_x = dy1 + jnp.einsum("tme,tde->md", d_qkv, wq, preferred_element_type=f32)
    d_x = d_x.reshape(n_seq, seq_length, 4, part_width).astype(bf16)
    grad_tokens = lax.all_to_all(d_x, "tensor", split_axis=2, concat_axis=0, tiled=True)
    grad_tokens = grad_tokens.reshape(sequences, seq_length, part_width).astype(f32)
    over_t = lambda a: lax.psum_scatter(a, "tensor", scatter_dimension=0, tiled=True)[0]
    docs = lambda a, k: lax.psum_scatter(a, "doc", scatter_dimension=k, tiled=True)
    g_qkv = docs(over_t(g_qkv), 0)
    g_qkv = jnp.stack([g_qkv[:, :192], g_qkv[:, 192:384], g_qkv[:, 384:]])
    g_b = lax.psum(over_t(g_b), "doc")
    small = lambda v: docs(lax.psum(v, "tensor"), 0)
    return (
        output,
        query_nll,
        grad_tokens,
        docs(grad_states, 1),
        g_qkv,
        jnp.stack([g_b[:192], g_b[384:]]),
        docs(over_t(g_out), 1),
        small(jnp.sum(dy1, 0)),
        small(dg1),
        small(db1),
        docs(over_t(g_up), 0),
        lax.psum(over_t(g_b_up), "doc"),
        docs(over_t(g_down), 1),
        small(jnp.sum(dy2, 0)),
        small(dg2),
        small(db2),
        docs(grad_w_query, 0),
    )


def solution(mesh):
    in_specs = (
        P("doc", None, "tensor"),
        P(None, "doc"),
        P(None, None, "tensor"),
        P(None, "tensor"),
        P("tensor", None),
        P(),
        P(),
        P(),
        P(None, "tensor"),
        P("tensor"),
        P("tensor", None),
        P(),
        P(),
        P(),
        P(),
        P(),
        P("tensor", None),
        P(),
        P(),
        P(),
        P(),
        P("doc", None, None),
        P(),
    )
    out_specs = (
        P("doc", None, None),
        P(),
        P("doc", None, "tensor"),
        P(None, "doc"),
        P(None, "doc", "tensor"),
        P(None, "tensor"),
        P("tensor", "doc"),
        P("doc"),
        P("doc"),
        P("doc"),
        P("doc", "tensor"),
        P("tensor"),
        P("tensor", "doc"),
        P("doc"),
        P("doc"),
        P("doc"),
        P("doc", None),
    )
    return jax.shard_map(shards, mesh=mesh, in_specs=in_specs, out_specs=out_specs, check_vma=False)
```

```python
import functools

import jax
import jax.numpy as jnp
from jax import lax
from jax.experimental import pallas as pl
from jax.experimental.pallas import tpu as pltpu
from jax.sharding import PartitionSpec as P

MESH = pl.DeviceIdType.MESH
f32 = jnp.float32
bf16 = jnp.bfloat16
MIB = 1024 * 1024


def flip(index, bit):
    return index + bit * (1 - 2 * lax.rem(lax.div(index, bit), 2))


def dot(a, b):
    return lax.dot_general(a, b, (((1,), (0,)), ((), ())), preferred_element_type=f32)


def dot_nt(a, b):
    return lax.dot_general(a, b, (((1,), (1,)), ((), ())), preferred_element_type=f32)


def dot_tn(a, b):
    return lax.dot_general(a, b, (((0,), (0,)), ((), ())), preferred_element_type=f32)


def rows_of(block):
    return block.reshape(block.shape[0] * block.shape[1], block.shape[2])


def picks(positions, first_row, n_seq, queries):
    shape = (8 * n_seq, 32 * n_seq)
    lane = lax.broadcasted_iota(jnp.int32, shape, 1)
    line = lax.broadcasted_iota(jnp.int32, shape, 0)
    spot = jnp.zeros(shape, jnp.int32)
    for b in range(8 * n_seq):
        query = lax.rem(first_row + b // 8, queries)
        spot = jnp.where(line == b, positions[query, b % 8] + 32 * (b // 8), spot)
    return (lane == spot).astype(f32)


def norm_forward(y):
    centred = y - jnp.mean(y, -1, keepdims=True)
    factor = lax.rsqrt(jnp.mean(centred * centred, -1, keepdims=True) + 1e-12)
    return centred * factor, factor


def forward_kernel(
    cfg,
    lengths,
    positions,
    tokens,
    w_qkv,
    w_out,
    w_up,
    w_down,
    b_qv,
    b_up,
    b_out,
    gain_one,
    bias_one,
    b_down,
    gain_two,
    bias_two,
    x_out,
    qkv_out,
    lse_out,
    ctx_out,
    n1_out,
    f1_out,
    hl_out,
    act_out,
    gp_out,
    n2_out,
    f2_out,
    res_out,
    wq_all,
    wo_all,
    wu_all,
    wd_all,
    pk,
    tok,
    x_s,
    qkv_s,
    lse_s,
    ctx_s,
    att_s,
    n1_s,
    f1_s,
    hl_s,
    act_s,
    gp_s,
    n2_s,
    f2_s,
    res_s,
    wq,
    wo,
    wu,
    wd,
    vec,
    send_sem,
    recv_sem,
    local_sem,
    out_sem,
):
    n_seq, seq, model, queries = cfg
    d = lax.axis_index("doc")
    t = lax.axis_index("tensor")
    t1, t2 = flip(t, 1), flip(t, 2)
    t3 = flip(t1, 2)
    d1, d2 = flip(d, 1), flip(d, 2)
    q = lax.rem(d, 4)
    q1, q2 = flip(q, 1), flip(q, 2)
    q3 = flip(q1, 2)

    def local(number, src, dst):
        copy = pltpu.make_async_copy(src, dst, local_sem.at[number])
        copy.start()
        return copy

    own_q = local(0, w_qkv, wq.at[t])
    barrier = pltpu.get_barrier_semaphore()
    peers = ({"tensor": t1}, {"tensor": t2}, {"tensor": t3}, {"doc": d1}, {"doc": d2})
    for peer in peers:
        pl.semaphore_signal(barrier, inc=1, device_id=peer, device_id_type=MESH)
    pl.semaphore_wait(barrier, len(peers))

    def remote(number, src, dst, peer):
        return pltpu.make_async_remote_copy(
            src_ref=src,
            dst_ref=dst,
            send_sem=send_sem.at[number],
            recv_sem=recv_sem.at[number],
            device_id=peer,
            device_id_type=MESH,
        )

    gathered = (wq, wo, wu, wd)
    inputs = (w_qkv, w_out, w_up, w_down)
    outputs = (wq_all, wo_all, wu_all, wd_all)
    started = []

    def send(number, src, dst, peer):
        copy = remote(number, src, dst, peer)
        copy.start()
        started.append(copy)

    hops = [(({"doc": d1}, q1), ({"doc": d2}, q2))] * 4
    hops[1] = hops[3] = hops[0][::-1]

    def send_x(a, pieces=1):
        count = inputs[a].shape[1] // pieces
        for k in range(pieces):
            rows = pl.ds(k * count, count)
            src, dst = inputs[a].at[q, rows], gathered[a].at[t, q, rows]
            remote(9 * a, src, dst, {"tensor": t2}).start()
        started.append(remote(9 * a, inputs[a].at[q], gathered[a].at[t, q], {"tensor": t2}))

    def send_core(a):
        send(9 * a + 4, inputs[a], gathered[a].at[t], {"tensor": t1})

    def arrived(number, ref):
        remote(number, ref, ref, {"tensor": t1}).wait_recv()

    def piece(a, part):
        return gathered[a].at[t2, part]

    def after_x(a):
        (first, _), (second, _) = hops[a]
        arrived(9 * a, piece(a, q))
        send(9 * a + 1, piece(a, q), piece(a, q), first)
        send(9 * a + 2, piece(a, q), piece(a, q), second)
        send(9 * a + 5, piece(a, q), piece(a, q), {"tensor": t1})

    def after_first(a):
        (_, part), (second, _) = hops[a]
        arrived(9 * a + 1, piece(a, part))
        send(9 * a + 3, piece(a, part), piece(a, part), second)
        send(9 * a + 6, piece(a, part), piece(a, part), {"tensor": t1})

    def after_second(a):
        (_, _), (_, part) = hops[a]
        arrived(9 * a + 2, piece(a, part))
        send(9 * a + 7, piece(a, part), piece(a, part), {"tensor": t1})
        arrived(9 * a + 3, piece(a, q3))
        send(9 * a + 8, piece(a, q3), piece(a, q3), {"tensor": t1})

    def after_core(a):
        (_, one), (_, two) = hops[a]
        for k, part in enumerate((q, one, two, q3)):
            arrived(9 * a + 5 + k, gathered[a].at[t3, part])

    tok_base, vec_base, pick_base = 36, 39, 42
    own = pl.multiple_of(t * n_seq, n_seq)
    own_tok = local(1, tokens.at[pl.ds(own, n_seq)], tok.at[t])

    def send_tokens(k, peer):
        theirs = pl.multiple_of(peer * n_seq, n_seq)
        send(tok_base + k, tokens.at[pl.ds(theirs, n_seq)], tok.at[t], {"tensor": peer})

    send_x(0, 3)
    send_tokens(2, t1)
    send_tokens(0, t2)
    send_tokens(1, t3)
    own_o = local(3, w_out, wo.at[t])
    part_width = model // 4
    gap = jnp.zeros((1, part_width), f32)
    vec[t, 1:2] = jnp.concatenate([b_qv[0:1], gap, b_qv[1:2], gap], 1)
    singles = (b_up, None, b_out, gain_one, bias_one, b_down, gain_two, bias_two)
    for k, ref in enumerate(singles):
        if ref is not None:
            vec[t, k : k + 1] = ref[...].reshape(1, model)
    for a in range(4):
        send_core(a)
    for k, peer in enumerate((t2, t3, t1)):
        send(vec_base + k, vec.at[t], vec.at[t], {"tensor": peer})
    own_u = local(4, w_up, wu.at[t])
    own_d = local(5, w_down, wd.at[t])
    after_x(0)
    send_x(2)
    send_x(1, 3)
    after_first(0)
    own_tok.wait()
    for k, peer in enumerate((t2, t3, t1)):
        arrived(tok_base + k, tok.at[peer])

    def row(k):
        return vec[t, k : k + 1, :]

    stores = []

    def store(src, dst):
        copy = pltpu.make_async_copy(src, dst, out_sem.at[len(stores)])
        copy.start()
        stores.append(copy)

    @pl.loop(0, n_seq)
    def _(s):
        x_s[s] = jnp.concatenate([tok[j, s] for j in range(4)], axis=1)

    store(x_s, x_out)

    key_index = lax.broadcasted_iota(jnp.int32, (seq, seq), 0)

    def attention(part, first):
        @pl.loop(0, n_seq)
        def _(s):
            row = d * (4 * n_seq) + t * n_seq + s
            length = lengths[lax.rem(row, queries), lax.div(row, queries)]
            bias = vec[part, 1:2, :576]
            z = (dot_nt(x_s[s], rows_of(wq[part])) + bias).astype(bf16)
            qkv_s[part, s] = z
            pieces = []
            for h in range(3):
                qh = z[:, h * 64 : h * 64 + 64] * 0.125
                kh = z[:, 192 + h * 64 : 256 + h * 64]
                vh = z[:, 384 + h * 64 : 448 + h * 64]
                st = jnp.where(key_index < length, dot_nt(kh, qh), -1000000000.0)
                high = jnp.max(st, 0, keepdims=True)
                e = jnp.exp(st - high)
                total = jnp.sum(e, 0, keepdims=True)
                prob = (e * (1.0 / total)).astype(bf16)
                lse_s[part, s, h] = high + jnp.log(total)
                pieces.append(dot_tn(vh, prob))
            ctx_s[part, s] = jnp.concatenate(pieces, axis=0).T.astype(bf16)

    def project(part, first):
        @pl.loop(0, n_seq)
        def _(s):
            for n in range(model // 256):
                cols = slice(n * 256, n * 256 + 256)
                term = dot(ctx_s[part, s], rows_of(wo[part, :, :, cols]))
                if first:
                    att_s[s, :, cols] = term
                else:
                    att_s[s, :, cols] += term

    own_q.wait()
    attention(t, True)
    send_x(3)
    after_x(1)
    own_o.wait()
    project(t, True)
    after_x(2)
    for k, peer in enumerate((t2, t3, t1)):
        arrived(vec_base + k, vec.at[peer])
    arrived(4, wq.at[t1])
    arrived(9 + 4, wo.at[t1])
    attention(t1, False)
    after_first(1)
    project(t1, False)
    after_second(0)
    after_x(3)
    attention(t2, False)
    after_second(1)
    project(t2, False)
    after_core(0)
    attention(t3, False)
    after_first(2)
    after_core(1)
    project(t3, False)
    store(qkv_s, qkv_out)
    store(lse_s, lse_out)
    store(ctx_s, ctx_out)
    store(wq, wq_all)
    store(wo, wo_all)

    chunk = 96
    chunks = seq // chunk

    @pl.loop(0, n_seq * chunks)
    def _(i):
        s, r = lax.div(i, chunks), pl.multiple_of(lax.rem(i, chunks) * chunk, chunk)
        rows = pl.ds(r, chunk)
        y = x_s[s, rows].astype(f32) + att_s[s, rows] + row(2)
        n1, f1 = norm_forward(y)
        n1_s[s, rows] = n1
        f1_s[s, rows] = f1
        hl_s[s, rows] = (n1 * row(3) + row(4)).astype(bf16)

    store(n1_s, n1_out)
    store(f1_s, f1_out)
    store(hl_s, hl_out)
    after_first(3)
    own_u.wait()
    own_d.wait()

    def ffn_up(part):
        @pl.loop(0, n_seq * (model // 256))
        def _(i):
            s, n = lax.div(i, model // 256), lax.rem(i, model // 256)
            cols = pl.ds(pl.multiple_of(n * 256, 256), 256)
            u = dot(hl_s[s], rows_of(wu[part, :, :, cols])) + vec[part, 0:1, cols]
            cdf = 0.5 * (1.0 + lax.erf(u * 0.7071067811865476))
            pdf = jnp.exp(u * u * -0.5) * 0.3989422804014327
            act_s[part, s, :, cols] = (u * cdf).astype(bf16)
            gp_s[part, s, :, cols] = (cdf + u * pdf).astype(bf16)

    def ffn_down(part, first):
        @pl.loop(0, n_seq * (model // 256))
        def _(i):
            s, n = lax.div(i, model // 256), lax.rem(i, model // 256)
            cols = pl.ds(pl.multiple_of(n * 256, 256), 256)
            term = dot(act_s[part, s], rows_of(wd[part, :, :, cols]))
            if first:
                att_s[s, :, cols] = term
            else:
                att_s[s, :, cols] += term

    def store_ffn(part):
        store(act_s.at[part], act_out.at[part])
        store(gp_s.at[part], gp_out.at[part])
        store(wu.at[part], wu_all.at[part])
        store(wd.at[part], wd_all.at[part])

    def store_ffn(part):
        store(act_s.at[part], act_out.at[part])
        store(gp_s.at[part], gp_out.at[part])
        store(wu.at[part], wu_all.at[part])
        store(wd.at[part], wd_all.at[part])

    ffn_up(t)
    store_ffn(t)
    ffn_down(t, True)
    arrived(2 * 9 + 4, wu.at[t1])
    ffn_up(t1)
    arrived(3 * 9 + 4, wd.at[t1])
    store_ffn(t1)
    ffn_down(t1, False)
    after_second(2)
    ffn_up(t2)
    after_second(3)
    store_ffn(t2)
    ffn_down(t2, False)
    after_core(2)
    ffn_up(t3)
    after_core(3)
    store_ffn(t3)
    ffn_down(t3, False)

    @pl.loop(0, n_seq * chunks)
    def _(i):
        s, r = lax.div(i, chunks), pl.multiple_of(lax.rem(i, chunks) * chunk, chunk)
        rows = pl.ds(r, chunk)
        y = n1_s[s, rows] * row(3) + row(4) + att_s[s, rows] + row(5)
        n2, f2 = norm_forward(y)
        n2_s[s, rows] = n2
        f2_s[s, rows] = f2
        res_s[s, rows] = (n2 * row(6) + row(7)).astype(bf16)

    store(n2_s, n2_out)
    store(f2_s, f2_out)
    store(res_s, res_out)
    hot = picks(positions, d * (4 * n_seq) + t * n_seq, n_seq, queries).astype(bf16)
    pk[t] = dot(hot, rows_of(res_s[:, :32])).astype(bf16)
    for k, peer in enumerate((t2, t3, t1)):
        send(pick_base + k, pk.at[t], pk.at[t], {"tensor": peer})
    for k, peer in enumerate((t2, t3, t1)):
        arrived(pick_base + k, pk.at[peer])
    for copy in stores:
        copy.wait()
    for copy in started:
        copy.wait_send()


def forward(n_seq, seq, model, queries, tables, tokens, weights_in, vectors):
    def sds(shape, dtype):
        return jax.ShapeDtypeStruct(shape, dtype)

    acts = [
        ((n_seq, seq, model), bf16),
        ((4, n_seq, seq, 576), bf16),
        ((4, n_seq, 3, 1, seq), f32),
        ((4, n_seq, seq, 192), bf16),
        ((n_seq, seq, model), f32),
        ((n_seq, seq, 1), f32),
        ((n_seq, seq, model), bf16),
        ((4, n_seq, seq, model), bf16),
        ((4, n_seq, seq, model), bf16),
        ((n_seq, seq, model), f32),
        ((n_seq, seq, 1), f32),
        ((n_seq, seq, model), bf16),
    ]
    weights = [(4,) + w.shape for w in weights_in]
    any_spec = pl.BlockSpec(memory_space=pl.ANY)
    vmem_spec = pl.BlockSpec(memory_space=pltpu.VMEM)
    scratch = [pltpu.VMEM((4, n_seq, seq, model // 4), bf16)]
    scratch += [pltpu.VMEM(*a) for a in acts[:4]]
    scratch += [pltpu.VMEM((n_seq, seq, model), f32)]
    scratch += [pltpu.VMEM(*a) for a in acts[4:]]
    scratch += [pltpu.VMEM(w, bf16) for w in weights]
    scratch += [pltpu.VMEM((4, 8, model), f32)]
    scratch += [
        pltpu.SemaphoreType.DMA((45,)),
        pltpu.SemaphoreType.DMA((45,)),
        pltpu.SemaphoreType.DMA((6,)),
        pltpu.SemaphoreType.DMA((32,)),
    ]
    return pl.pallas_call(
        functools.partial(forward_kernel, (n_seq, seq, model, queries)),
        out_shape=[sds(*a) for a in acts]
        + [sds(w, bf16) for w in weights]
        + [sds((4, 8 * n_seq, model), bf16)],
        in_specs=[pl.BlockSpec(memory_space=pltpu.SMEM)] * 2 + [any_spec] * 5 + [vmem_spec] * 8,
        out_specs=[any_spec] * 16 + [vmem_spec],
        scratch_shapes=scratch,
        compiler_params=pltpu.CompilerParams(
            collective_id=0, has_side_effects=True, vmem_limit_bytes=60 * MIB
        ),
        name="layer_forward",
    )(*tables, tokens, *weights_in, *vectors)


precise = lax.Precision.HIGHEST


def dot_f32(a, b, dims):
    return lax.dot_general(a, b, (dims, ((), ())), precision=precise, preferred_element_type=f32)


def square(block):
    return block.reshape(-1, block.shape[-1])


def norm_back_rows(upstream, normed, factor, gain_row):
    scaled = upstream * gain_row
    mean_one = jnp.mean(scaled, -1, keepdims=True)
    mean_two = jnp.mean(scaled * normed, -1, keepdims=True)
    return factor * (scaled - mean_one - normed * mean_two)


class Chain:
    def __init__(self, bits, wait, send, base, held, buffers):
        self.wait, self.send, self.base, self.held = wait, send, base, held
        self.one_y, self.one_z, self.two = buffers
        (self.y, self.y_peer), (self.z0, self.z0_peer) = bits["y"], bits["z0"]
        self.width = self.two.shape[-1] // 2

    def lanes(self, half):
        return slice(half * self.width, (half + 1) * self.width)

    def start(self):
        src = self.held.at[:, :, 1 - self.y, :, self.lanes(0)]
        self.send(self.base, src, self.one_y, self.y_peer)
        src = self.held.at[:, 1 - self.z0, :, :, self.lanes(1)]
        self.send(self.base + 1, src, self.one_z, self.z0_peer)

    def middle(self):
        low, high = self.lanes(0), self.lanes(1)
        self.wait(self.base, self.one_y)
        for a in range(2):
            there = self.one_y[a, 1 - self.z0].astype(f32)
            add = self.held[a, 1 - self.z0, self.y, :, low].astype(f32)
            self.one_y[a, 1 - self.z0] = (there + add).astype(bf16)
        src = self.one_y.at[:, 1 - self.z0]
        self.send(self.base + 2, src, self.two.at[:, :, low], self.z0_peer)
        self.wait(self.base + 1, self.one_z)
        for a in range(2):
            there = self.one_z[a, 1 - self.y].astype(f32)
            add = self.held[a, self.z0, 1 - self.y, :, high].astype(f32)
            self.one_z[a, 1 - self.y] = (there + add).astype(bf16)
        src = self.one_z.at[:, 1 - self.y]
        self.send(self.base + 3, src, self.two.at[:, :, high], self.y_peer)

    def finish(self, a):
        low, high = self.lanes(0), self.lanes(1)
        first = self.one_y[a, self.z0].astype(f32) + self.held[a, self.z0, self.y, :, low].astype(f32)
        second = self.one_z[a, self.y].astype(f32) + self.held[a, self.z0, self.y, :, high].astype(f32)
        return self.two[a].astype(f32) + jnp.concatenate([first, second], 1)

    def arrive(self):
        self.wait(self.base + 2, self.two.at[:, :, self.lanes(0)])
        self.wait(self.base + 3, self.two.at[:, :, self.lanes(1)])


class Reduction:
    def __init__(self, bits, wait, send, base, buffers):
        self.wait, self.send, self.base = wait, send, base
        self.held, self.x_in, self.last = buffers[0], buffers[7], buffers[8]
        (self.x, self.x_peer), (self.z1, self.z1_peer) = bits["x"], bits["z1"]
        self.other = Chain(bits, wait, send, base + 2, self.held.at[1 - self.x], buffers[1:4])
        self.mine = Chain(bits, wait, send, base + 6, self.held.at[self.x], buffers[4:7])

    def pass_other(self):
        self.other.arrive()
        for a in range(2):
            self.other.two[a] = self.other.finish(a).astype(bf16)
        self.send(self.base + 10, self.other.two, self.x_in, self.x_peer)

    def pass_mine(self):
        self.mine.arrive()
        self.wait(self.base + 10, self.x_in)
        for k in range(2):
            a = 1 - self.z1 if k == 0 else self.z1
            total = self.mine.finish(a) + self.x_in[a].astype(f32)
            self.mine.two[a] = total.astype(bf16)
            if k == 0:
                self.send(self.base + 11, self.mine.two.at[a], self.last, self.z1_peer)

    def result(self):
        self.wait(self.base + 11, self.last)
        return self.mine.two[self.z1].astype(f32) + self.last[...].astype(f32)


def backward_kernel(
    cfg,
    lengths,
    positions,
    targets,
    query_weight,
    states,
    doc_ids,
    doc_table,
    w_query,
    gain_one,
    gain_two,
    pk,
    vocab,
    out_grad,
    res,
    x_in,
    qkv_in,
    lse_in,
    ctx_in,
    n1_in,
    f1_in,
    hl_in,
    act_in,
    gp_in,
    n2_in,
    f2_in,
    wq_in,
    wo_in,
    wu_in,
    wd_in,
    output,
    nll_out,
    gt_out,
    gs_out,
    gwq_out,
    down_out,
    up_out,
    qkv_out,
    out_out,
    vec_out,
    big,
    shares,
    lg,
    ut,
    us,
    ur,
    sr,
    lb,
    dlog,
    st_all,
    diff,
    og,
    tmp,
    n1,
    n2,
    f1,
    f2,
    dy,
    act,
    gp,
    wq,
    wo,
    wu,
    wd,
    qkv,
    ctx,
    lse,
    d_t,
    x_t,
    d_up,
    dctx,
    dqkv,
    dxb,
    gt,
    sums,
    sums_in,
    own_states,
    attn_send,
    parts,
    *rest,
):
    n_seq, seq, model, queries, slots, table, docs = cfg
    red_bufs, (send_sem, recv_sem, local_sem) = rest[:-3], rest[-3:]
    m_rows = n_seq * seq
    own_rows = 8 * n_seq
    d = lax.axis_index("doc")
    t = lax.axis_index("tensor")
    t1, t2 = flip(t, 1), flip(t, 2)
    t3 = flip(t1, 2)
    x_bit = lax.div(t, 2)
    bits = {
        "x": (x_bit, {"tensor": t2}),
        "y": (lax.rem(d, 2), {"doc": flip(d, 1)}),
        "z0": (lax.rem(lax.div(d, 2), 2), {"doc": flip(d, 2)}),
        "z1": (lax.div(d, 4), {"doc": flip(d, 4)}),
    }

    barrier = pltpu.get_barrier_semaphore()
    doc_peers = [lax.rem(d + k, docs) for k in range(1, docs)]
    peers = [{"tensor": p} for p in (t1, t2, t3)] + [{"doc": p} for p in doc_peers]
    for peer in peers:
        pl.semaphore_signal(barrier, inc=1, device_id=peer, device_id_type=MESH)
    pl.semaphore_wait(barrier, len(peers))

    def remote(number, src, dst, peer):
        return pltpu.make_async_remote_copy(
            src_ref=src,
            dst_ref=dst,
            send_sem=send_sem.at[number],
            recv_sem=recv_sem.at[number],
            device_id=peer,
            device_id_type=MESH,
        )

    started = []

    def send(number, src, dst, peer):
        copy = remote(number, src, dst, peer)
        copy.start()
        started.append(copy)

    def arrived(number, ref):
        remote(number, ref, ref, {"tensor": t1}).wait_recv()

    loads = {}

    def load(name, src, dst):
        copy = pltpu.make_async_copy(src, dst, local_sem.at[len(loads)])
        copy.start()
        loads[name] = copy

    own = pl.multiple_of(t * n_seq, n_seq)
    load("vocab", vocab, big)
    base = 0
    share_width = model // docs
    wide = states[...].astype(f32)
    wide = jnp.concatenate([wide, jnp.zeros((queries, 128 - share_width), f32)], 1)
    fill = own_states.shape[0] - queries
    if fill:
        wide = jnp.concatenate([wide, jnp.zeros((fill, 128), f32)], 0)
    own_states[...] = wide.astype(bf16)
    st_all[d] = own_states[...]
    for k, p in enumerate(doc_peers):
        send(base + k, own_states, st_all.at[d], {"doc": p})
    states_base = base
    base += docs - 1
    load("og", out_grad.at[pl.ds(own, n_seq)], og)
    load("n2", n2_in, n2)
    load("f2", f2_in, f2)
    order = (t3, t2, t1, t)
    load("act0", act_in.at[order[0]], act.at[0])
    load("act1", act_in.at[order[1]], act.at[1])
    for i in range(2):
        load("wd%d" % i, wd_in.at[order[i]], wd.at[i])
        load("wu%d" % i, wu_in.at[order[i]], wu.at[i])
    load("gp0", gp_in.at[order[0]], gp.at[0])
    load("gp1", gp_in.at[order[1]], gp.at[1])
    load("hl", hl_in, tmp)
    load("n1", n1_in, n1)
    load("f1", f1_in, f1)
    load("wo", wo_in, wo)
    for i in range(2):
        load("wq%d" % i, wq_in.at[order[i]], wq.at[i])
        load("qkv%d" % i, qkv_in.at[order[i]], qkv.at[i])
    load("ctx", ctx_in, ctx)
    load("lse", lse_in, lse)
    first_row = d * (4 * n_seq)
    hot = picks(positions, first_row + t * n_seq, n_seq, queries)
    out_base = base
    base += 3
    all_rows = 4 * own_rows
    vocab_local = vocab.shape[0] * model
    chunk = model
    tall = lax.broadcasted_iota(jnp.int32, (all_rows, 1), 0)
    goal = jnp.zeros((all_rows, 1), jnp.int32)
    for b in range(all_rows):
        query = lax.rem(first_row + b // 8, queries)
        goal = jnp.where(tall == b, targets[query, b % 8], goal)
    goal = goal - t * vocab_local
    loads["vocab"].wait()

    @pl.loop(0, vocab_local // chunk)
    def _(j):
        start = pl.multiple_of(j * chunk, chunk)
        lg[:, pl.ds(start, chunk)] = dot_nt(rows_of(pk[...]), square(big[j]))

    high = jnp.max(lg[...], 1, keepdims=True)
    ut[...] = jnp.zeros_like(ut)

    def vocab_step(j, carry):
        mass, chosen = carry
        start = pl.multiple_of(j * chunk, chunk)
        values = lg[:, pl.ds(start, chunk)]
        e = jnp.exp(values - high)
        index = lax.broadcasted_iota(jnp.int32, (all_rows, chunk), 1) + start
        hits = (index == goal).astype(f32)
        both = jnp.concatenate([e, hits], 0).astype(bf16)
        ut[...] += dot(both, square(big[j]))
        mass = mass + jnp.sum(e, 1, keepdims=True)
        chosen = chosen + jnp.sum(hits * values, 1, keepdims=True)
        return mass, chosen

    zero = jnp.zeros((all_rows, 1), f32)
    mass, chosen = lax.fori_loop(0, vocab_local // chunk, vocab_step, (zero, zero))
    spread = lax.broadcasted_iota(jnp.int32, (all_rows, 128), 1)
    stats = jnp.where(spread == 0, high, jnp.where(spread == 1, mass, chosen))
    mean_row = (ut[:all_rows] * (1.0 / mass)).astype(bf16)
    goal_row = ut[all_rows:].astype(bf16)
    for j in range(4):
        part = slice(j * own_rows, (j + 1) * own_rows)
        us[j, :, :model] = mean_row[part]
        us[j, :, model:] = goal_row[part]
    part_base = base
    base += 6
    sr[t] = stats
    for k, p in enumerate((t2, t3, t1)):
        send(part_base + k, sr.at[t], sr.at[t], {"tensor": p})
    for k, p in enumerate((t2, t3, t1)):
        send(part_base + 3 + k, us.at[p], ur.at[t], {"tensor": p})
    ur[t] = us[t]
    sums[0] = jnp.zeros(sums.shape[1:], f32)
    for name in ("og", "n2", "f2"):
        loads[name].wait()
    step_rows = 96

    def add_sum(row, value):
        sums[0, 8 + row] += jnp.sum(value, 0, keepdims=True)

    def second_norm(s, rows, flat, extra):
        upstream = og[s, rows].astype(f32)
        if extra is not None:
            upstream = upstream + extra
        normed = n2[flat]
        back = norm_back_rows(upstream, normed, f2[flat], gain_two[...].reshape(1, model))
        add_sum(4, upstream * normed)
        add_sum(5, upstream)
        add_sum(3, back)
        dy[flat] = back
        og[s, rows] = back.astype(bf16)

    for s in range(n_seq):

        @pl.loop(1, seq // step_rows)
        def _(i):
            start = pl.multiple_of(i * step_rows, step_rows)
            second_norm(s, pl.ds(start, step_rows), pl.ds(s * seq + start, step_rows), None)

    for k, p in enumerate((t2, t3, t1)):
        arrived(part_base + k, sr.at[p])
    highs = [sr[j, :, 0:1] for j in range(4)]
    top = jnp.maximum(jnp.maximum(highs[0], highs[1]), jnp.maximum(highs[2], highs[3]))
    masses = [sr[j, :, 1:2] * jnp.exp(highs[j] - top) for j in range(4)]
    whole = masses[0] + masses[1] + masses[2] + masses[3]
    picked_logit = sr[0, :, 2:3] + sr[1, :, 2:3] + sr[2, :, 2:3] + sr[3, :, 2:3]
    loglik = picked_logit - (top + jnp.log(whole))
    mine = first_row + t * n_seq
    for s in range(4 * n_seq):
        total = jnp.sum(loglik[8 * s : 8 * s + 8], 0, keepdims=True)
        lb[first_row + s] = jnp.broadcast_to(total, (1, 128))
    group_base = base
    base += docs - 1
    group_ref = lb.at[pl.ds(first_row, 4 * n_seq)]
    for k, p in enumerate(doc_peers):
        send(group_base + k, group_ref, group_ref, {"doc": p})
    for j in range(4):
        share = jnp.broadcast_to(masses[j] / whole, (all_rows, 128))
        shares[j] = share.reshape(4, own_rows, 128)
    loads["hl"].wait()
    x_t[...] = tmp[...].T
    load("x", x_in, tmp)
    for k, p in enumerate((t2, t3, t1)):
        arrived(part_base + 3 + k, ur.at[p])
    gap = jnp.zeros((own_rows, model), f32)
    for j in range(4):
        share = shares[j, t][:, 0:1]
        gap = gap + ur[j, :, model:].astype(f32) - share * ur[j, :, :model].astype(f32)
    diff[...] = gap
    for k in range(docs - 1):
        source = lax.rem(d + docs - 1 - k, docs)
        arrived(states_base + k, st_all.at[source])
    emb = jnp.zeros((own_states.shape[0], 128), f32)
    for j in range(docs):
        emb = emb + dot(st_all[j, :, :share_width], w_query[j])
    emb = emb[:queries]
    table_score = dot_f32(emb, doc_table[...], ((1,), (1,)))
    entry = lax.broadcasted_iota(jnp.int32, (queries, table), 1)
    hot_docs = [(entry == doc_ids[:, k : k + 1]).astype(f32) for k in range(slots)]
    prior = [jnp.sum(hot_docs[k] * table_score, 1, keepdims=True) for k in range(slots)]
    for k in range(docs - 1):
        source = lax.rem(d + docs - 1 - k, docs)
        arrived(group_base + k, lb.at[pl.ds(source * (4 * n_seq), 4 * n_seq)])
    joint = []
    for k in range(slots):
        column = lb[k * queries : (k + 1) * queries].reshape(queries, 128)
        joint.append(prior[k] + column[:, 0:1])

    def log_sum(values):
        largest = functools.reduce(jnp.maximum, values)
        total = functools.reduce(jnp.add, [jnp.exp(v - largest) for v in values])
        return largest + jnp.log(total)

    prior_lse, joint_lse = log_sum(prior), log_sum(joint)
    tall = lax.broadcasted_iota(jnp.int32, (queries, 1), 0)
    weight = jnp.zeros((queries, 1), f32)
    for k in range(queries):
        weight = jnp.where(tall == k, query_weight[k], weight)
    nll_out[...] = jnp.broadcast_to(prior_lse - joint_lse, (queries, 128))
    spread_docs = jnp.zeros((queries, table), f32)
    for k in range(slots):
        post = jnp.exp(joint[k] - joint_lse)
        before = jnp.exp(prior[k] - prior_lse)
        spread_docs = spread_docs + hot_docs[k] * (weight * (before - post))
        value = -weight * post
        dlog[k * queries : (k + 1) * queries] = jnp.broadcast_to(value, (queries, 128)).reshape(
            queries, 1, 128
        )
    d_emb = dot_f32(spread_docs, doc_table[...], ((1,), (0,))).astype(bf16)
    gs_out[...] = dot_nt(d_emb, w_query[d])
    gwq_out[...] = dot_tn(st_all[d, :queries, :share_width].astype(f32), d_emb.astype(f32))
    scattered = []
    for s in range(n_seq):
        coefficient = dlog[mine + s]
        rows = diff[8 * s : 8 * s + 8] * coefficient[:, 0:1]
        scattered.append(
            dot_f32(hot[8 * s : 8 * s + 8, 32 * s : 32 * s + 32], rows, ((0,), (0,)))
        )
    mine_out = output.at[pl.ds(own, n_seq)]
    send(out_base, res, mine_out, {"tensor": t2})
    send(out_base + 1, res, mine_out, {"tensor": t1})
    for s in range(n_seq):
        extra = jnp.concatenate([scattered[s], jnp.zeros((step_rows - 32, model), f32)], 0)
        second_norm(s, pl.ds(0, step_rows), pl.ds(s * seq, step_rows), extra)

    d_t[...] = rows_of(og[...]).T
    reds = []
    for k in range(3):
        reds.append(Reduction(bits, arrived, send, base, red_bufs[9 * k : 9 * k + 9]))
        base += 12
    down, up, attn = reds
    block_shape = (2, 2, 2, model // docs)

    def emit(red, i, sending, shard, lanes, value):
        value = value.reshape(block_shape + (value.shape[-1],))
        which = lax.div(shard, 2)
        if i % 2 == 0:
            sending[which, :, :, :, :, lanes] = value.astype(bf16)
        else:
            total = value + red.held[which, :, :, :, :, lanes].astype(f32)
            red.held[which, :, :, :, :, lanes] = total.astype(bf16)

    def before_block(red, i, shard):
        if i % 2 == 1:
            which = lax.div(shard, 2)
            arrived(red.base + i // 2, red.held.at[which])

    def after_block(red, i, sending, shard):
        if i % 2 == 0:
            which = lax.div(shard, 2)
            send(red.base + i // 2, sending.at[which], red.held.at[which], {"tensor": t1})

    down_send, up_send = big.at[0:2], big.at[2:4]
    tiles = model // 256
    for i, shard in enumerate(order):
        loads["act%d" % i].wait()
        before_block(down, i, shard)

        @pl.loop(0, tiles)
        def _(n):
            lanes = pl.ds(pl.multiple_of(n * 256, 256), 256)
            emit(down, i, down_send, shard, lanes, dot(d_t[...], act[i % 2, :, lanes]))

        if i + 2 < 4:
            load("act%d" % (i + 2), act_in.at[order[i + 2]], act.at[i % 2])
        after_block(down, i, down_send, shard)
        if i == 1:
            down.other.start()
    down.mine.start()
    for i, shard in enumerate(order):
        for name in ("gp", "wd", "wu"):
            loads["%s%d" % (name, i)].wait()
        before_block(up, i, shard)

        @pl.loop(0, tiles)
        def _(n):
            lanes = pl.ds(pl.multiple_of(n * 256, 256), 256)
            value = dot_nt(rows_of(og[...]), wd[i % 2, lanes]) * gp[i % 2, :, lanes].astype(f32)
            low = value.astype(bf16)
            d_up[:, lanes] = low
            sums[0, shard, :, lanes] = jnp.sum(low.astype(f32), 0, keepdims=True)

        if i + 2 < 4:
            load("gp%d" % (i + 2), gp_in.at[order[i + 2]], gp.at[i % 2])
            load("wd%d" % (i + 2), wd_in.at[order[i + 2]], wd.at[i % 2])

        @pl.loop(0, tiles)
        def _(n):
            lanes = pl.ds(pl.multiple_of(n * 256, 256), 256)
            value = dot_nt(d_up[...], wu[i % 2, lanes])
            if i == 0:
                n2[:, lanes] = value
            else:
                n2[:, lanes] += value
            emit(up, i, up_send, shard, lanes, dot(x_t[...], d_up[:, lanes]))

        if i + 2 < 4:
            load("wu%d" % (i + 2), wu_in.at[order[i + 2]], wu.at[i % 2])
        after_block(up, i, up_send, shard)
        if i == 1:
            down.other.middle()
            up.other.start()
        if i == 2:
            down.mine.middle()
    up.mine.start()
    down.pass_other()
    arrived(out_base, output.at[pl.ds(t2 * n_seq, n_seq)])
    passed = output.at[pl.ds(t2 * n_seq, n_seq)]
    send(out_base + 2, passed, passed, {"tensor": t1})
    loads["n1"].wait()
    loads["f1"].wait()

    @pl.loop(0, m_rows // step_rows)
    def _(i):
        flat = pl.ds(pl.multiple_of(i * step_rows, step_rows), step_rows)
        s, start = lax.div(i, seq // step_rows), lax.rem(i, seq // step_rows) * step_rows
        upstream = dy[flat] + n2[flat]
        normed = n1[flat]
        back = norm_back_rows(upstream, normed, f1[flat], gain_one[...].reshape(1, model))
        add_sum(1, upstream * normed)
        add_sum(2, upstream)
        add_sum(0, back)
        dy[flat] = back
        og[s, pl.ds(pl.multiple_of(start, step_rows), step_rows)] = back.astype(bf16)

    d_t[...] = rows_of(og[...]).T
    up.other.middle()
    loads["x"].wait()
    x_t[...] = tmp[...].T
    for name in ("wo", "ctx", "lse"):
        loads[name].wait()
    vec_base = base
    vec_peers = [{"tensor": t1}, bits["y"][1], bits["z0"][1], bits["x"][1], bits["z1"][1]]
    base += len(vec_peers)

    def vec_start(k):
        send(vec_base + k, sums.at[k], sums_in.at[k], vec_peers[k])

    def vec_finish(k):
        arrived(vec_base + k, sums_in.at[k])
        sums[k + 1] = sums[k] + sums_in[k]

    key_index = lax.broadcasted_iota(jnp.int32, (seq, seq), 0)
    for i, shard in enumerate(order):
        loads["qkv%d" % i].wait()
        loads["wq%d" % i].wait()
        dctx[...] = dot_nt(rows_of(og[...]), wo[shard]).astype(bf16)

        @pl.loop(0, n_seq)
        def _(s):
            rows = pl.ds(pl.multiple_of(s * seq, 32), seq)
            row = first_row + t * n_seq + s
            length = lengths[lax.rem(row, queries), lax.div(row, queries)]
            z = qkv[i % 2, s]
            upstream = dctx[rows]
            d_q, d_k, d_v = [], [], []
            for h in range(3):
                qh = z[:, h * 64 : h * 64 + 64]
                kh = z[:, 192 + h * 64 : 256 + h * 64]
                vh = z[:, 384 + h * 64 : 448 + h * 64]
                dc = upstream[:, h * 64 : h * 64 + 64]
                scores = jnp.where(key_index < length, dot_nt(kh, qh * 0.125), -1000000000.0)
                prob = jnp.exp(scores - lse[shard, s, h])
                d_v.append(dot(prob.astype(bf16), dc))
                d_prob = dot_nt(vh, dc)
                inner = jnp.sum(d_prob * prob, 0, keepdims=True)
                d_score = (prob * (d_prob - inner)).astype(bf16)
                d_k.append(dot(d_score, qh) * 0.125)
                d_q.append(dot_tn(kh, d_score) * 0.125)
            first = jnp.concatenate(d_q, 0).T
            both = jnp.concatenate([first] + d_k + d_v, 1).astype(bf16)
            dqkv[rows] = both
            lse_sum = jnp.sum(both.astype(f32), 0, keepdims=True)
            parts[s] = lse_sum

        total = parts[0]
        for s in range(1, n_seq):
            total = total + parts[s]
        sums[0, 4 + shard, :, : 3 * 192] = total
        before_block(attn, i, shard)
        value = jnp.concatenate([dot(x_t[...], dqkv[...]), dot(d_t[...], ctx[shard])], 1)
        emit(attn, i, attn_send, shard, slice(None), value)
        after_block(attn, i, attn_send, shard)
        if i == 0:
            down.pass_mine()
            up.mine.middle()
        if i == 1:
            attn.other.start()
            up.pass_other()
        if i == 2:
            down_out[...] = down.result()
            up.pass_mine()
            attn.other.middle()
        if i == 3:
            attn.mine.start()
            vec_start(0)
            up_out[...] = up.result()
            attn.pass_other()

        @pl.loop(0, tiles)
        def _(n):
            lanes = pl.ds(pl.multiple_of(n * 256, 256), 256)
            value = dot(dqkv[...], wq[i % 2, :, lanes])
            if i == 0:
                n1[:, lanes] = value
            else:
                n1[:, lanes] += value

        if i + 2 < 4:
            load("qkv%d" % (i + 2), qkv_in.at[order[i + 2]], qkv.at[i % 2])
            load("wq%d" % (i + 2), wq_in.at[order[i + 2]], wq.at[i % 2])

    for j in range(4):
        lanes = slice(j * 192, j * 192 + 192)
        block = (n1[:, lanes] + dy[:, lanes]).astype(bf16)
        dxb[j] = jnp.concatenate([block[k * seq : (k + 1) * seq] for k in range(n_seq)], 1)
    tok_base = base
    base += 3
    for k, p in enumerate((t2, t3, t1)):
        send(tok_base + k, dxb.at[p], gt.at[t], {"tensor": p})
    gt[t] = dxb[t]
    vec_finish(0)
    vec_start(1)
    attn.mine.middle()
    vec_finish(1)
    vec_start(2)
    vec_finish(2)
    vec_start(3)
    attn.pass_mine()
    vec_finish(3)
    vec_start(4)
    for k, p in enumerate((t2, t3, t1)):
        arrived(tok_base + k, gt.at[p])
    load("gt", gt, gt_out)
    vec_finish(4)
    vec_out[...] = sums[5]
    total = attn.result()
    for k in range(3):
        qkv_out[k] = total[:, k * 192 : k * 192 + 192]
    out_out[...] = total[:, 576:].T
    arrived(out_base + 1, output.at[pl.ds(t1 * n_seq, n_seq)])
    arrived(out_base + 2, output.at[pl.ds(t3 * n_seq, n_seq)])
    loads["gt"].wait()
    for copy in started:
        copy.wait_send()


def backward(
    n_seq,
    seq,
    model,
    docs,
    tables,
    vocab,
    out_grad,
    kept,
):
    states, doc_ids, doc_table, w_query = tables[4:8]
    queries, slots = doc_ids.shape
    table = doc_table.shape[0]
    m_rows = n_seq * seq
    own_rows = 8 * n_seq
    all_rows = 4 * own_rows
    share = model // docs
    states_rows = -(-queries // 16) * 16
    (res, x, qkv, lse, ctx, n1, f1, hl, act, gp, n2, f2, wq, wo, wu, wd) = kept

    def flat(a):
        return a.reshape(a.shape[:-3] + (a.shape[-3] * a.shape[-2], a.shape[-1]))

    kept = [
        res,
        flat(x),
        qkv,
        lse,
        flat(ctx),
        flat(n1),
        flat(f1),
        flat(hl),
        flat(act),
        flat(gp),
        flat(n2),
        flat(f2),
        flat(wq),
        flat(wo),
        flat(wu),
        flat(wd),
    ]
    vocab = vocab.reshape(vocab.shape[0] // model, 2, 2, 2, share, model)

    def sds(shape, dtype):
        return jax.ShapeDtypeStruct(shape, dtype)

    any_spec = pl.BlockSpec(memory_space=pl.ANY)
    vmem_spec = pl.BlockSpec(memory_space=pltpu.VMEM)
    smem_spec = pl.BlockSpec(memory_space=pltpu.SMEM)
    outs = [
        sds((4 * n_seq, seq, model), bf16),
        sds((queries, 128), f32),
        sds((4, seq, n_seq * 192), bf16),
        sds((queries, share), f32),
        sds((share, 128), f32),
        sds((share, model), f32),
        sds((share, model), f32),
        sds((3, share, 192), f32),
        sds((192, share), f32),
        sds((14, 1, model), f32),
    ]
    out_specs = [any_spec, vmem_spec, any_spec] + [vmem_spec] * 7

    def vm(shape, dtype):
        return pltpu.VMEM(shape, dtype)

    scratch = [
        vm(vocab.shape, bf16),
        vm((4, 4, own_rows, 128), f32),
        vm((all_rows, vocab.shape[0] * model), f32),
        vm((2 * all_rows, model), f32),
        vm((4, own_rows, 2 * model), bf16),
        vm((4, own_rows, 2 * model), bf16),
        vm((4, all_rows, 128), f32),
        vm((docs * 4 * n_seq, 1, 128), f32),
        vm((docs * 4 * n_seq, 1, 128), f32),
        vm((docs, states_rows, 128), bf16),
        vm((own_rows, model), f32),
        vm((n_seq, seq, model), bf16),
        vm((m_rows, model), bf16),
        vm((m_rows, model), f32),
        vm((m_rows, model), f32),
        vm((m_rows, 1), f32),
        vm((m_rows, 1), f32),
        vm((m_rows, model), f32),
        vm((2, m_rows, model), bf16),
        vm((2, m_rows, model), bf16),
        vm((2, 576, model), bf16),
        vm((4, 192, model), bf16),
        vm((2, model, model), bf16),
        vm((2, model, model), bf16),
        vm((2, n_seq, seq, 576), bf16),
        vm((4, m_rows, 192), bf16),
        vm((4, n_seq, 3, 1, seq), f32),
        vm((model, m_rows), bf16),
        vm((model, m_rows), bf16),
        vm((m_rows, model), bf16),
        vm((m_rows, 192), bf16),
        vm((m_rows, 576), bf16),
        vm((4, seq, n_seq * 192), bf16),
        vm((4, seq, n_seq * 192), bf16),
        vm((6, 14, 1, model), f32),
        vm((5, 14, 1, model), f32),
        vm((states_rows, 128), bf16),
        vm((2, 2, 2, 2, share, model), bf16),
        vm((n_seq, 1, 576), f32),
    ]
    for _ in range(3):
        scratch.append(vm((2, 2, 2, 2, share, model), bf16))
        for _ in range(2):
            scratch.append(vm((2, 2, share, model // 2), bf16))
            scratch.append(vm((2, 2, share, model // 2), bf16))
            scratch.append(vm((2, share, model), bf16))
        scratch.append(vm((2, share, model), bf16))
        scratch.append(vm((share, model), bf16))
    copies = 2 * (docs - 1) + 3 + 6 + 12 * 3 + 3 + 5
    scratch += [
        pltpu.SemaphoreType.DMA((copies,)),
        pltpu.SemaphoreType.DMA((copies,)),
        pltpu.SemaphoreType.DMA((40,)),
    ]
    return pl.pallas_call(
        functools.partial(backward_kernel, (n_seq, seq, model, queries, slots, table, docs)),
        out_shape=outs,
        in_specs=[smem_spec] * 4 + [vmem_spec] * 7 + [any_spec] * 18,
        out_specs=out_specs,
        scratch_shapes=scratch,
        compiler_params=pltpu.CompilerParams(
            collective_id=1, has_side_effects=True, vmem_limit_bytes=60 * MIB
        ),
        name="layer_backward",
    )(*tables, vocab, out_grad, *kept)


def finish_kernel(cfg, *refs):
    n_seq, docs = cfg
    output, res, gs, gwq, down, up, qkv, out, gt_in, nll_in, sums_in = refs[:11]
    output_out, nll_out, tokens_out, gs_out, qkv_out, b_qv_out, out_out = refs[11:18]
    b_out_out, gain_one_out, bias_one_out, up_out, b_up_out, down_out = refs[18:24]
    b_down_out, gain_two_out, bias_two_out, gwq_out, gt, nll, sums, whole = refs[24:32]
    held, sem, sem_out = refs[32:-2], refs[-2], refs[-1]
    d = lax.axis_index("doc")
    t = lax.axis_index("tensor")
    pairs = [(gt_in, gt), (sums_in, sums), (nll_in, nll), (res, whole.at[pl.ds(t * n_seq, n_seq)])]
    for k in range(1, 4):
        part = pl.ds(lax.rem(t + k, 4) * n_seq, n_seq)
        pairs.append((output.at[part], whole.at[part]))
    passed = ((down, down_out), (up, up_out), (qkv, qkv_out), (out, out_out), (gs, gs_out))
    passed += ((gwq, gwq_out),)
    pairs += [(pair[0], buf) for pair, buf in zip(passed, held)]
    copies = [pltpu.make_async_copy(*pair, sem.at[k]) for k, pair in enumerate(pairs)]
    for copy in copies:
        copy.start()
    ends = []

    def forward_to(number, src, dst):
        copies[number].wait()
        copy = pltpu.make_async_copy(src, dst, sem_out.at[len(ends)])
        copy.start()
        ends.append(copy)

    for k in range(4):
        part = pl.ds(lax.rem(t + k, 4) * n_seq, n_seq)
        forward_to(3 + k, whole.at[part], output_out.at[part])
    for k, (pair, buf) in enumerate(zip(passed, held)):
        forward_to(7 + k, buf, pair[1])
    part_width = gt.shape[-1] // n_seq
    copies[0].wait()
    for j in range(4):
        for s in range(n_seq):
            lanes = slice(s * part_width, (s + 1) * part_width)
            tokens_out[j * n_seq + s] = gt[j, :, lanes].astype(f32)
    copies[1].wait()
    copies[2].wait()
    nll_out[...] = nll[:, 0]
    heads = sums[4 + t]
    b_qv_out[0:1] = heads[:, :part_width]
    b_qv_out[1:2] = heads[:, 2 * part_width : 3 * part_width]
    b_up_out[...] = sums[t].reshape(b_up_out.shape)
    width = b_out_out.shape[0]
    singles = (b_out_out, gain_one_out, bias_one_out, b_down_out, gain_two_out, bias_two_out)
    for k, ref in enumerate(singles):
        row = sums[8 + k]
        own = jnp.zeros((1, width), f32)
        for j in range(docs):
            own = own + jnp.where(d == j, row[:, j * width : (j + 1) * width], 0.0)
        ref[...] = own.reshape(width)
    for copy in ends:
        copy.wait()


def finish(n_seq, docs, parts):
    output, res, gt, nll, gs, gwq, down, up, qkv, out, sums = parts
    model = sums.shape[-1]
    share = model // docs
    part_width = gt.shape[-1] // n_seq

    def sds(*shape):
        return jax.ShapeDtypeStruct(shape, f32)

    outs = [
        jax.ShapeDtypeStruct(output.shape, bf16),
        sds(nll.shape[0]),
        sds(4 * n_seq, gt.shape[1], part_width),
        sds(*gs.shape),
        sds(*qkv.shape),
        sds(2, part_width),
        sds(*out.shape),
        sds(share),
        sds(share),
        sds(share),
        sds(*up.shape),
        sds(model),
        sds(*down.shape),
        sds(share),
        sds(share),
        sds(share),
        sds(*gwq.shape),
    ]
    any_spec = pl.BlockSpec(memory_space=pltpu.HBM)
    vmem_spec = pl.BlockSpec(memory_space=pltpu.VMEM)
    out_specs = [vmem_spec] * 17
    for k in (0, 3, 4, 6, 10, 12, 16):
        out_specs[k] = any_spec
    results = pl.pallas_call(
        functools.partial(finish_kernel, (n_seq, docs)),
        out_shape=outs,
        in_specs=[any_spec] * 11,
        out_specs=out_specs,
        scratch_shapes=[
            pltpu.VMEM(gt.shape, gt.dtype),
            pltpu.VMEM(nll.shape, nll.dtype),
            pltpu.VMEM(sums.shape, sums.dtype),
            pltpu.VMEM(output.shape, output.dtype),
            *(pltpu.VMEM(a.shape, a.dtype) for a in (down, up, qkv, out, gs, gwq)),
            pltpu.SemaphoreType.DMA((13,)),
            pltpu.SemaphoreType.DMA((10,)),
        ],
        compiler_params=pltpu.CompilerParams(vmem_limit_bytes=62 * MIB),
        name="layer_results",
    )(output, res, gs, gwq, down, up, qkv, out, gt, nll, sums)
    results = list(results)
    results[12] = results[12].T
    return results


def joined(array, axis, combine):
    everything = jax.tree.map(lambda part: lax.all_gather(part, axis), array)
    initial = jax.tree.map(lambda part: part[0], everything)

    def step(k, so_far):
        return combine(so_far, jax.tree.map(lambda part: part[k], everything))

    return lax.fori_loop(1, lax.axis_size(axis), step, initial)


def norm_back(upstream, normed, factor, gain_vec):
    scaled = upstream * gain_vec
    inner = (
        scaled
        - jnp.mean(scaled, -1, keepdims=True)
        - normed * jnp.mean(scaled * normed, -1, keepdims=True)
    )
    return (inner * factor, jnp.sum(upstream * normed, 0), jnp.sum(upstream, 0))


def merge_pair(high_first, mass_first, high_second, mass_second):
    highest = jnp.maximum(high_first, high_second)
    return (
        highest,
        mass_first * jnp.exp(high_first - highest) + mass_second * jnp.exp(high_second - highest),
    )


def vocab_combine(first, second):
    highest, summed = merge_pair(first[0], first[1], second[0], second[1])
    return (highest, summed, first[2] + second[2])


def query_combine(first, second):
    prior_high, prior_mass = merge_pair(first[0], first[1], second[0], second[1])
    joint_high, joint_mass = merge_pair(first[2], first[3], second[2], second[3])
    return (prior_high, prior_mass, joint_high, joint_mass)


def partial_lse(members, values):
    highest = jnp.max(jnp.where(members, values[:, None], -1e30), 0)
    summed = jnp.sum(jnp.where(members, jnp.exp(values[:, None] - highest[None, :]), 0.0), 0)
    return (highest, summed)


def shards(
    tokens,
    query_states,
    w_qkv,
    b_qv,
    w_out,
    b_out,
    ln1_gain,
    ln1_bias,
    w_up,
    b_up,
    w_down,
    b_down,
    ln2_gain,
    ln2_bias,
    w_query,
    doc_table,
    vocab_table,
    doc_ids,
    lengths,
    positions,
    targets,
    out_grad,
    query_weight,
):
    sequences, seq_length, part_width = tokens.shape
    model_width = w_qkv.shape[1]
    n_seq = sequences // 4
    row_count = n_seq * seq_length
    queries = lengths.shape[0]
    t = lax.axis_index("tensor")
    hidden = w_up.shape[1]
    vectors = (b_qv, b_up, b_out, ln1_gain, ln1_bias, b_down, ln2_gain, ln2_bias)
    quarter = model_width // 4
    weights_in = (
        w_qkv.transpose(0, 2, 1).reshape(4, 3 * quarter // 4, model_width),
        w_out.reshape(4, quarter // 4, model_width),
        w_up.reshape(4, quarter, hidden),
        w_down.reshape(4, hidden // 4, model_width),
    )
    (x, qkv, lse, ctx, n1, f1, hl, act, gp, n2, f2, res, wq, wo, wu, wd, pk) = forward(
        n_seq,
        seq_length,
        model_width,
        queries,
        (lengths, positions),
        tokens,
        weights_in,
        vectors,
    )
    docs = lax.axis_size("doc")
    if docs == 8 and n_seq == 2:
        share = model_width // docs
        tables = (
            lengths,
            positions,
            targets,
            query_weight,
            query_states,
            doc_ids,
            doc_table,
            w_query.reshape(docs, share, w_query.shape[1]),
            ln1_gain,
            ln2_gain,
            pk,
        )
        kept = (res, x, qkv, lse, ctx, n1, f1, hl, act, gp, n2, f2, wq, wo, wu, wd)
        (output, nll, gt, gs, gwq, g_down, g_up, g_qkv, g_out, sums) = backward(
            n_seq, seq_length, model_width, docs, tables, vocab_table, out_grad, kept
        )
        return tuple(
            finish(n_seq, docs, (output, res, gt, nll, gs, gwq, g_down, g_up, g_qkv, g_out, sums))
        )
    output = lax.all_gather(res, "tensor", axis=0, tiled=True)
    row_index = lax.axis_index("doc") * sequences + jnp.arange(sequences, dtype=jnp.int32)
    slot_index = row_index // queries
    query_index = row_index % queries
    row_position = positions[query_index]
    row_target = targets[query_index]
    own = lambda a: lax.dynamic_slice_in_dim(a, t * n_seq, n_seq, 0)
    own_position = own(row_position)
    seq_base = jnp.arange(n_seq, dtype=jnp.int32)[:, None]
    picked = lax.all_gather(res[seq_base, own_position], "tensor", axis=0, tiled=True)
    vocab_logits = jnp.einsum("btd,vd->btv", picked, vocab_table, preferred_element_type=f32)
    vocab_local = vocab_table.shape[0]
    vocab_ids = t * vocab_local + jnp.arange(vocab_local, dtype=jnp.int32)
    target_hits = vocab_ids[None, None, :] == row_target[:, :, None]
    local_high = jnp.max(vocab_logits, -1)
    local_mass = jnp.sum(jnp.exp(vocab_logits - local_high[:, :, None]), -1)
    local_chosen = jnp.sum(jnp.where(target_hits, vocab_logits, 0.0), -1)
    vocab_high, vocab_mass, chosen = joined(
        (local_high, local_mass, local_chosen), "tensor", vocab_combine
    )
    vocab_lse = vocab_high + jnp.log(vocab_mass)
    loglik = jnp.sum(chosen - vocab_lse, -1)
    states = lax.all_gather(query_states, "doc", axis=1, tiled=True)
    query_emb = jnp.dot(states, w_query, preferred_element_type=f32)
    members = query_index[:, None] == jnp.arange(queries, dtype=jnp.int32)[None, :]
    member_weights = members.astype(f32)
    own_emb = jnp.dot(member_weights, query_emb, precision=precise)
    embeds = doc_table[doc_ids[query_index, slot_index]]
    retrieval = jnp.sum(own_emb * embeds, -1)
    joint_score = retrieval + loglik
    prior_high, prior_mass = partial_lse(members, retrieval)
    joint_high, joint_mass = partial_lse(members, joint_score)
    prior_high, prior_mass, joint_high, joint_mass = joined(
        (prior_high, prior_mass, joint_high, joint_mass), "doc", query_combine
    )
    prior_lse = prior_high + jnp.log(prior_mass)
    joint_lse = joint_high + jnp.log(joint_mass)
    query_nll = prior_lse - joint_lse
    row_weight = query_weight[query_index]
    posterior = jnp.exp(joint_score - jnp.dot(member_weights, joint_lse, precision=precise))
    prior_prob = jnp.exp(retrieval - jnp.dot(member_weights, prior_lse, precision=precise))
    grad_loglik = -row_weight * posterior
    grad_retrieval = row_weight * (prior_prob - posterior)
    vocab_probs = jnp.exp(vocab_logits - vocab_lse[:, :, None])
    grad_logits = (grad_loglik[:, None, None] * (target_hits.astype(f32) - vocab_probs)).astype(
        bf16
    )
    grad_picked = lax.psum_scatter(
        jnp.einsum("btv,vd->btd", grad_logits, vocab_table, preferred_element_type=f32),
        "tensor",
        scatter_dimension=0,
        tiled=True,
    )
    grad_emb = jnp.dot(
        member_weights.T, grad_retrieval[:, None] * embeds, precision=precise
    ).astype(bf16)
    grad_w_query = jnp.dot(states.T, grad_emb, preferred_element_type=f32)
    grad_states = jnp.dot(grad_emb, w_query.T, preferred_element_type=f32)
    flat = lambda a: a.reshape(row_count, a.shape[-1])
    grad_result = flat(own(out_grad).astype(f32).at[seq_base, own_position].add(grad_picked))
    n1, f1, n2, f2, hl, x = flat(n1), flat(f1), flat(n2), flat(f2), flat(hl), flat(x)
    dy2, dg2, db2 = norm_back(grad_result, n2, f2, ln2_gain)
    d_low = dy2.astype(bf16)
    act, gp = act.reshape(4, row_count, hidden), gp.reshape(4, row_count, hidden)
    wu, wd = wu.reshape(4, model_width, hidden), wd.reshape(4, hidden, model_width)
    wq, wo = wq.reshape(4, 576, model_width).transpose(0, 2, 1), wo.reshape(4, 192, model_width)
    qkv, ctx = qkv.reshape(4, n_seq, seq_length, 576), ctx.reshape(4, row_count, 192)
    g_down = jnp.einsum("tmf,md->tfd", act, d_low, preferred_element_type=f32)
    d_act = jnp.einsum("md,tfd->tmf", d_low, wd, preferred_element_type=f32)
    d_up = (d_act * gp.astype(f32)).astype(bf16)
    g_up = jnp.einsum("md,tmf->tdf", hl, d_up, preferred_element_type=f32)
    g_b_up = jnp.sum(d_up.astype(f32), 1)
    d_hidden = dy2 + jnp.einsum("tmf,tdf->md", d_up, wu, preferred_element_type=f32)
    dy1, dg1, db1 = norm_back(d_hidden, n1, f1, ln1_gain)
    d_att = dy1.astype(bf16)
    g_out = jnp.einsum("tme,md->ted", ctx, d_att, preferred_element_type=f32)
    d_ctx = jnp.einsum("md,ted->tme", d_att, wo, preferred_element_type=f32).astype(bf16)
    d_ctx = d_ctx.reshape(4, n_seq, seq_length, 3, 64)
    heads = qkv.reshape(4, n_seq, seq_length, 3, 3, 64)
    hq, hk, hv = heads[:, :, :, 0], heads[:, :, :, 1], heads[:, :, :, 2]
    row_length = own(lengths[query_index, slot_index])
    key_mask = (jnp.arange(seq_length, dtype=jnp.int32)[None, :] < row_length[:, None])[
        None, :, None, None, :
    ]
    scores = jnp.einsum("tbqhe,tbkhe->tbhqk", hq, hk, preferred_element_type=f32) * 0.125
    scores = jnp.where(key_mask, scores, -1000000000.0)
    prob = jnp.exp(scores - lse.reshape(4, n_seq, 3, seq_length, 1))
    d_v = jnp.einsum("tbhqk,tbqhe->tbkhe", prob.astype(bf16), d_ctx, preferred_element_type=f32)
    d_prob = jnp.einsum("tbqhe,tbkhe->tbhqk", d_ctx, hv, preferred_element_type=f32)
    d_s = (prob * (d_prob - jnp.sum(d_prob * prob, -1, keepdims=True))).astype(bf16)
    d_q = jnp.einsum("tbhqk,tbkhe->tbqhe", d_s, hk, preferred_element_type=f32) * 0.125
    d_k = jnp.einsum("tbhqk,tbqhe->tbkhe", d_s, hq, preferred_element_type=f32) * 0.125
    d_qkv = jnp.stack([d_q, d_k, d_v], 3).reshape(4, row_count, 576).astype(bf16)
    g_b = jnp.sum(d_qkv.astype(f32), 1)
    g_qkv = jnp.einsum("md,tme->tde", x, d_qkv, preferred_element_type=f32)
    d_x = dy1 + jnp.einsum("tme,tde->md", d_qkv, wq, preferred_element_type=f32)
    d_x = d_x.reshape(n_seq, seq_length, 4, part_width).astype(bf16)
    grad_tokens = lax.all_to_all(d_x, "tensor", split_axis=2, concat_axis=0, tiled=True)
    grad_tokens = grad_tokens.reshape(sequences, seq_length, part_width).astype(f32)
    over_t = lambda a: lax.psum_scatter(a, "tensor", scatter_dimension=0, tiled=True)[0]
    docs = lambda a, k: lax.psum_scatter(a, "doc", scatter_dimension=k, tiled=True)
    g_qkv = docs(over_t(g_qkv), 0)
    g_qkv = jnp.stack([g_qkv[:, :192], g_qkv[:, 192:384], g_qkv[:, 384:]])
    g_b = lax.psum(over_t(g_b), "doc")
    small = lambda v: docs(lax.psum(v, "tensor"), 0)
    return (
        output,
        query_nll,
        grad_tokens,
        docs(grad_states, 1),
        g_qkv,
        jnp.stack([g_b[:192], g_b[384:]]),
        docs(over_t(g_out), 1),
        small(jnp.sum(dy1, 0)),
        small(dg1),
        small(db1),
        docs(over_t(g_up), 0),
        lax.psum(over_t(g_b_up), "doc"),
        docs(over_t(g_down), 1),
        small(jnp.sum(dy2, 0)),
        small(dg2),
        small(db2),
        docs(grad_w_query, 0),
    )


def solution(mesh):
    in_specs = (
        P("doc", None, "tensor"),
        P(None, "doc"),
        P(None, None, "tensor"),
        P(None, "tensor"),
        P("tensor", None),
        P(),
        P(),
        P(),
        P(None, "tensor"),
        P("tensor"),
        P("tensor", None),
        P(),
        P(),
        P(),
        P(),
        P(),
        P("tensor", None),
        P(),
        P(),
        P(),
        P(),
        P("doc", None, None),
        P(),
    )
    out_specs = (
        P("doc", None, None),
        P(),
        P("doc", None, "tensor"),
        P(None, "doc"),
        P(None, "doc", "tensor"),
        P(None, "tensor"),
        P("tensor", "doc"),
        P("doc"),
        P("doc"),
        P("doc"),
        P("doc", "tensor"),
        P("tensor"),
        P("tensor", "doc"),
        P("doc"),
        P("doc"),
        P("doc"),
        P("doc", None),
    )
    return jax.shard_map(shards, mesh=mesh, in_specs=in_specs, out_specs=out_specs, check_vma=False)
```

```python
import functools

import jax
import jax.numpy as jnp
from jax import lax
from jax.experimental import pallas as pl
from jax.experimental.pallas import tpu as pltpu
from jax.sharding import PartitionSpec as P

MESH = pl.DeviceIdType.MESH
f32 = jnp.float32
bf16 = jnp.bfloat16
MIB = 1024 * 1024


def flip(index, bit):
    return index + bit * (1 - 2 * lax.rem(lax.div(index, bit), 2))


def dot(a, b):
    return lax.dot_general(a, b, (((1,), (0,)), ((), ())), preferred_element_type=f32)


def dot_nt(a, b):
    return lax.dot_general(a, b, (((1,), (1,)), ((), ())), preferred_element_type=f32)


def dot_tn(a, b):
    return lax.dot_general(a, b, (((0,), (0,)), ((), ())), preferred_element_type=f32)


def rows_of(block):
    return block.reshape(block.shape[0] * block.shape[1], block.shape[2])


def picks(positions, first_row, n_seq, queries):
    shape = (8 * n_seq, 32 * n_seq)
    lane = lax.broadcasted_iota(jnp.int32, shape, 1)
    line = lax.broadcasted_iota(jnp.int32, shape, 0)
    spot = jnp.zeros(shape, jnp.int32)
    for b in range(8 * n_seq):
        query = lax.rem(first_row + b // 8, queries)
        spot = jnp.where(line == b, positions[query, b % 8] + 32 * (b // 8), spot)
    return (lane == spot).astype(f32)


def norm_forward(y):
    centred = y - jnp.mean(y, -1, keepdims=True)
    factor = lax.rsqrt(jnp.mean(centred * centred, -1, keepdims=True) + 1e-12)
    return centred * factor, factor


def forward_kernel(
    cfg,
    lengths,
    positions,
    tokens,
    w_qkv,
    w_out,
    w_up,
    w_down,
    b_qv,
    b_up,
    b_out,
    gain_one,
    bias_one,
    b_down,
    gain_two,
    bias_two,
    x_out,
    qkv_out,
    lse_out,
    ctx_out,
    n1_out,
    f1_out,
    hl_out,
    act_out,
    gp_out,
    n2_out,
    f2_out,
    res_out,
    wq_all,
    wo_all,
    wu_all,
    wd_all,
    pk,
    raw,
    packed,
    tok,
    x_s,
    qkv_s,
    lse_s,
    ctx_s,
    att_s,
    n1_s,
    f1_s,
    hl_s,
    act_s,
    gp_s,
    n2_s,
    f2_s,
    res_s,
    wq,
    wo,
    wu,
    wd,
    vec,
    send_sem,
    recv_sem,
    local_sem,
    out_sem,
):
    n_seq, seq, model, queries = cfg
    d = lax.axis_index("doc")
    t = lax.axis_index("tensor")
    t1, t2 = flip(t, 1), flip(t, 2)
    t3 = flip(t1, 2)
    d1, d2 = flip(d, 1), flip(d, 2)
    q = lax.rem(d, 4)
    q1, q2 = flip(q, 1), flip(q, 2)
    q3 = flip(q1, 2)

    def local(number, src, dst):
        copy = pltpu.make_async_copy(src, dst, local_sem.at[number])
        copy.start()
        return copy

    own_tok = local(1, tokens, raw)
    own_q = local(0, w_qkv, wq.at[t])
    barrier = pltpu.get_barrier_semaphore()
    peers = ({"tensor": t1}, {"tensor": t2}, {"tensor": t3}, {"doc": d1}, {"doc": d2})
    for peer in peers:
        pl.semaphore_signal(barrier, inc=1, device_id=peer, device_id_type=MESH)
    pl.semaphore_wait(barrier, len(peers))

    def remote(number, src, dst, peer):
        return pltpu.make_async_remote_copy(
            src_ref=src,
            dst_ref=dst,
            send_sem=send_sem.at[number],
            recv_sem=recv_sem.at[number],
            device_id=peer,
            device_id_type=MESH,
        )

    gathered = (wq, wo, wu, wd)
    inputs = (w_qkv, w_out, w_up, w_down)
    started = []

    def send(number, src, dst, peer):
        copy = remote(number, src, dst, peer)
        copy.start()
        started.append(copy)

    half = model // 8
    sources = ((0, None), (1, None), (2, 0), (2, 1), (3, 0), (3, 1))
    hops = (({"doc": d1}, q1), ({"doc": d2}, q2))

    def rows_view(ref, k, begin=0, count=None):
        if k is None and count is None:
            return ref
        begin = begin + (0 if k is None else k * half)
        return ref.at[pl.ds(begin, half if count is None else count)]

    def piece(a, part, shard=None):
        which, k = sources[a]
        return rows_view(gathered[which].at[t2 if shard is None else shard, part], k)

    def send_x(a, pieces):
        which, k = sources[a]
        src, dst = inputs[which].at[q], gathered[which].at[t, q]
        count = (src.shape[0] if k is None else half) // pieces
        for n in range(pieces):
            part = rows_view(src, k, n * count, count)
            remote(8 * a, part, rows_view(dst, k, n * count, count), {"tensor": t2}).start()
        started.append(remote(8 * a, rows_view(src, k), rows_view(dst, k), {"tensor": t2}))

    def send_core(which):
        send(core_base + which, inputs[which], gathered[which].at[t], {"tensor": t1})

    def arrived(number, ref):
        remote(number, ref, ref, {"tensor": t1}).wait_recv()

    def own_core(which):
        arrived(core_base + which, gathered[which].at[t1])

    def after_x(a):
        (first, _), (second, _) = hops[:: -1 if a % 2 else 1]
        arrived(8 * a, piece(a, q))
        send(8 * a + 1, piece(a, q), piece(a, q), first)
        send(8 * a + 2, piece(a, q), piece(a, q), second)
        send(8 * a + 4, piece(a, q), piece(a, q), {"tensor": t1})

    def after_first(a):
        (_, part), (second, _) = hops[:: -1 if a % 2 else 1]
        arrived(8 * a + 1, piece(a, part))
        send(8 * a + 3, piece(a, part), piece(a, part), second)
        send(8 * a + 5, piece(a, part), piece(a, part), {"tensor": t1})

    def after_second(a):
        (_, _), (_, part) = hops[:: -1 if a % 2 else 1]
        arrived(8 * a + 2, piece(a, part))
        send(8 * a + 6, piece(a, part), piece(a, part), {"tensor": t1})
        arrived(8 * a + 3, piece(a, q3))
        send(8 * a + 7, piece(a, q3), piece(a, q3), {"tensor": t1})

    def after_core(a):
        (_, one), (_, two) = hops[:: -1 if a % 2 else 1]
        for k, part in enumerate((q, one, two, q3)):
            arrived(8 * a + 4 + k, piece(a, part, t3))

    core_base, tok_base, vec_base, pick_base = 48, 52, 55, 58
    own = pl.multiple_of(t * n_seq, n_seq)
    def send_tokens(k, peer):
        send(tok_base + k, packed.at[peer], tok.at[t], {"tensor": peer})

    send_x(0, 3)
    own_tok.wait()
    part_width = model // 4
    for j in range(4):
        packed[j] = jnp.concatenate([raw[j * n_seq + s] for s in range(n_seq)], 1)
    tok[t] = packed[t]
    send_tokens(2, t1)
    send_tokens(0, t2)
    send_tokens(1, t3)
    own_o = local(3, w_out, wo.at[t])
    gap = jnp.zeros((1, part_width), f32)
    vec[t, 1:2] = jnp.concatenate([b_qv[0:1], gap, b_qv[1:2], gap], 1)
    singles = (b_up, None, b_out, gain_one, bias_one, b_down, gain_two, bias_two)
    for k, ref in enumerate(singles):
        if ref is not None:
            vec[t, k : k + 1] = ref[...].reshape(1, model)
    for a in range(4):
        send_core(a)
    for k, peer in enumerate((t2, t3, t1)):
        send(vec_base + k, vec.at[t], vec.at[t], {"tensor": peer})
    own_u = local(4, w_up, wu.at[t])
    own_d = local(5, w_down, wd.at[t])
    after_x(0)
    send_x(1, 3)
    after_x(1)
    send_x(3, 2)
    for k, peer in enumerate((t2, t3, t1)):
        arrived(tok_base + k, tok.at[peer])

    def row(k):
        return vec[t, k : k + 1, :]

    stores = []

    def store(src, dst):
        copy = pltpu.make_async_copy(src, dst, out_sem.at[len(stores)])
        copy.start()
        stores.append(copy)

    for s in range(n_seq):
        lanes = slice(s * part_width, (s + 1) * part_width)
        x_s[s] = jnp.concatenate([tok[j, :, lanes] for j in range(4)], axis=1)

    store(x_s, x_out)

    key_index = lax.broadcasted_iota(jnp.int32, (seq, seq), 0)

    def attention(part, first):
        @pl.loop(0, n_seq)
        def _(s):
            row = d * (4 * n_seq) + t * n_seq + s
            length = lengths[lax.rem(row, queries), lax.div(row, queries)]
            bias = vec[part, 1:2, :576]
            z = (dot_nt(x_s[s], rows_of(wq[part])) + bias).astype(bf16)
            qkv_s[part, s] = z
            pieces = []
            for h in range(3):
                qh = z[:, h * 64 : h * 64 + 64] * 0.125
                kh = z[:, 192 + h * 64 : 256 + h * 64]
                vh = z[:, 384 + h * 64 : 448 + h * 64]
                st = jnp.where(key_index < length, dot_nt(kh, qh), -1000000000.0)
                high = jnp.max(st, 0, keepdims=True)
                e = jnp.exp(st - high)
                total = jnp.sum(e, 0, keepdims=True)
                prob = (e * (1.0 / total)).astype(bf16)
                lse_s[part, s, h] = high + jnp.log(total)
                pieces.append(dot_tn(vh, prob))
            ctx_s[part, s] = jnp.concatenate(pieces, axis=0).T.astype(bf16)

    def project(part, first):
        @pl.loop(0, n_seq)
        def _(s):
            for n in range(model // 256):
                cols = slice(n * 256, n * 256 + 256)
                term = dot(ctx_s[part, s], rows_of(wo[part, :, :, cols]))
                if first:
                    att_s[s, :, cols] = term
                else:
                    att_s[s, :, cols] += term

    own_q.wait()
    after_first(0)
    send_x(2, 2)
    attention(t, True)
    send_x(4, 3)
    after_first(1)
    own_o.wait()
    project(t, True)
    for k, peer in enumerate((t2, t3, t1)):
        arrived(vec_base + k, vec.at[peer])
    own_core(0)
    own_core(1)
    after_x(3)
    attention(t1, False)
    send_x(5, 3)
    project(t1, False)
    after_x(2)
    after_second(0)
    attention(t2, False)
    after_second(1)
    project(t2, False)
    after_x(4)
    after_core(0)
    attention(t3, False)
    after_x(5)
    after_core(1)
    project(t3, False)
    store(qkv_s, qkv_out)
    store(lse_s, lse_out)
    store(ctx_s, ctx_out)
    store(wq, wq_all)
    store(wo, wo_all)

    after_first(3)
    chunk = 96
    chunks = seq // chunk

    @pl.loop(0, n_seq * chunks)
    def _(i):
        s, r = lax.div(i, chunks), pl.multiple_of(lax.rem(i, chunks) * chunk, chunk)
        rows = pl.ds(r, chunk)
        y = x_s[s, rows].astype(f32) + att_s[s, rows] + row(2)
        n1, f1 = norm_forward(y)
        n1_s[s, rows] = n1
        f1_s[s, rows] = f1
        hl_s[s, rows] = (n1 * row(3) + row(4)).astype(bf16)

    store(n1_s, n1_out)
    store(f1_s, f1_out)
    store(hl_s, hl_out)
    after_first(2)
    own_u.wait()
    own_d.wait()

    def ffn_up(part):
        @pl.loop(0, n_seq * (model // 256))
        def _(i):
            s, n = lax.div(i, model // 256), lax.rem(i, model // 256)
            cols = pl.ds(pl.multiple_of(n * 256, 256), 256)
            u = dot(hl_s[s], rows_of(wu[part, :, :, cols])) + vec[part, 0:1, cols]
            cdf = 0.5 * (1.0 + lax.erf(u * 0.7071067811865476))
            pdf = jnp.exp(u * u * -0.5) * 0.3989422804014327
            act_s[part, s, :, cols] = (u * cdf).astype(bf16)
            gp_s[part, s, :, cols] = (cdf + u * pdf).astype(bf16)

    def ffn_down(part, first):
        @pl.loop(0, n_seq * (model // 256))
        def _(i):
            s, n = lax.div(i, model // 256), lax.rem(i, model // 256)
            cols = pl.ds(pl.multiple_of(n * 256, 256), 256)
            term = dot(act_s[part, s], rows_of(wd[part, :, :, cols]))
            if first:
                att_s[s, :, cols] = term
            else:
                att_s[s, :, cols] += term

    def store_ffn(part):
        store(act_s.at[part], act_out.at[part])
        store(gp_s.at[part], gp_out.at[part])
        store(wu.at[part], wu_all.at[part])
        store(wd.at[part], wd_all.at[part])

    def store_ffn(part):
        store(act_s.at[part], act_out.at[part])
        store(gp_s.at[part], gp_out.at[part])
        store(wu.at[part], wu_all.at[part])
        store(wd.at[part], wd_all.at[part])

    ffn_up(t)
    store_ffn(t)
    after_first(4)
    ffn_down(t, True)
    after_first(5)
    own_core(2)
    ffn_up(t1)
    own_core(3)
    store_ffn(t1)
    ffn_down(t1, False)
    after_second(3)
    after_second(2)
    ffn_up(t2)
    after_second(4)
    after_second(5)
    store_ffn(t2)
    ffn_down(t2, False)
    after_core(3)
    after_core(2)
    ffn_up(t3)
    after_core(4)
    after_core(5)
    store_ffn(t3)
    ffn_down(t3, False)

    @pl.loop(0, n_seq * chunks)
    def _(i):
        s, r = lax.div(i, chunks), pl.multiple_of(lax.rem(i, chunks) * chunk, chunk)
        rows = pl.ds(r, chunk)
        y = n1_s[s, rows] * row(3) + row(4) + att_s[s, rows] + row(5)
        n2, f2 = norm_forward(y)
        n2_s[s, rows] = n2
        f2_s[s, rows] = f2
        res_s[s, rows] = (n2 * row(6) + row(7)).astype(bf16)

    store(n2_s, n2_out)
    store(f2_s, f2_out)
    store(res_s, res_out)
    hot = picks(positions, d * (4 * n_seq) + t * n_seq, n_seq, queries).astype(bf16)
    pk[t] = dot(hot, rows_of(res_s[:, :32])).astype(bf16)
    for k, peer in enumerate((t2, t3, t1)):
        send(pick_base + k, pk.at[t], pk.at[t], {"tensor": peer})
    for k, peer in enumerate((t2, t3, t1)):
        arrived(pick_base + k, pk.at[peer])
    for copy in stores:
        copy.wait()
    for copy in started:
        copy.wait_send()


def forward(n_seq, seq, model, queries, tables, tokens, weights_in, vectors):
    def sds(shape, dtype):
        return jax.ShapeDtypeStruct(shape, dtype)

    acts = [
        ((n_seq, seq, model), bf16),
        ((4, n_seq, seq, 576), bf16),
        ((4, n_seq, 3, 1, seq), f32),
        ((4, n_seq, seq, 192), bf16),
        ((n_seq, seq, model), f32),
        ((n_seq, seq, 1), f32),
        ((n_seq, seq, model), bf16),
        ((4, n_seq, seq, model), bf16),
        ((4, n_seq, seq, model), bf16),
        ((n_seq, seq, model), f32),
        ((n_seq, seq, 1), f32),
        ((n_seq, seq, model), bf16),
    ]
    weights = [(4,) + w.shape for w in weights_in]
    any_spec = pl.BlockSpec(memory_space=pl.ANY)
    vmem_spec = pl.BlockSpec(memory_space=pltpu.VMEM)
    packed = (4, seq, n_seq * model // 4)
    scratch = [pltpu.VMEM(tokens.shape, bf16), pltpu.VMEM(packed, bf16), pltpu.VMEM(packed, bf16)]
    scratch += [pltpu.VMEM(*a) for a in acts[:4]]
    scratch += [pltpu.VMEM((n_seq, seq, model), f32)]
    scratch += [pltpu.VMEM(*a) for a in acts[4:]]
    scratch += [pltpu.VMEM(w, bf16) for w in weights]
    scratch += [pltpu.VMEM((4, 8, model), f32)]
    scratch += [
        pltpu.SemaphoreType.DMA((61,)),
        pltpu.SemaphoreType.DMA((61,)),
        pltpu.SemaphoreType.DMA((6,)),
        pltpu.SemaphoreType.DMA((32,)),
    ]
    return pl.pallas_call(
        functools.partial(forward_kernel, (n_seq, seq, model, queries)),
        out_shape=[sds(*a) for a in acts]
        + [sds(w, bf16) for w in weights]
        + [sds((4, 8 * n_seq, model), bf16)],
        in_specs=[pl.BlockSpec(memory_space=pltpu.SMEM)] * 2 + [any_spec] * 5 + [vmem_spec] * 8,
        out_specs=[any_spec] * 16 + [vmem_spec],
        scratch_shapes=scratch,
        compiler_params=pltpu.CompilerParams(
            collective_id=0, has_side_effects=True, vmem_limit_bytes=60 * MIB
        ),
        name="layer_forward",
    )(*tables, tokens, *weights_in, *vectors)


precise = lax.Precision.HIGHEST


def dot_f32(a, b, dims):
    return lax.dot_general(a, b, (dims, ((), ())), precision=precise, preferred_element_type=f32)


def square(block):
    return block.reshape(-1, block.shape[-1])


def norm_back_rows(upstream, normed, factor, gain_row):
    scaled = upstream * gain_row
    mean_one = jnp.mean(scaled, -1, keepdims=True)
    mean_two = jnp.mean(scaled * normed, -1, keepdims=True)
    return factor * (scaled - mean_one - normed * mean_two)


class Chain:
    def __init__(self, bits, wait, send, base, held, buffers):
        self.wait, self.send, self.base, self.held = wait, send, base, held
        self.one_y, self.one_z, self.two = buffers
        (self.y, self.y_peer), (self.z0, self.z0_peer) = bits["y"], bits["z0"]
        self.width = self.two.shape[-1] // 2

    def lanes(self, half):
        return slice(half * self.width, (half + 1) * self.width)

    def start(self):
        src = self.held.at[:, :, 1 - self.y, :, self.lanes(0)]
        self.send(self.base, src, self.one_y, self.y_peer)
        src = self.held.at[:, 1 - self.z0, :, :, self.lanes(1)]
        self.send(self.base + 1, src, self.one_z, self.z0_peer)

    def middle(self):
        low, high = self.lanes(0), self.lanes(1)
        self.wait(self.base, self.one_y)
        for a in range(2):
            there = self.one_y[a, 1 - self.z0].astype(f32)
            add = self.held[a, 1 - self.z0, self.y, :, low].astype(f32)
            self.one_y[a, 1 - self.z0] = (there + add).astype(bf16)
        src = self.one_y.at[:, 1 - self.z0]
        self.send(self.base + 2, src, self.two.at[:, :, low], self.z0_peer)
        self.wait(self.base + 1, self.one_z)
        for a in range(2):
            there = self.one_z[a, 1 - self.y].astype(f32)
            add = self.held[a, self.z0, 1 - self.y, :, high].astype(f32)
            self.one_z[a, 1 - self.y] = (there + add).astype(bf16)
        src = self.one_z.at[:, 1 - self.y]
        self.send(self.base + 3, src, self.two.at[:, :, high], self.y_peer)

    def finish(self, a):
        low, high = self.lanes(0), self.lanes(1)
        first = self.one_y[a, self.z0].astype(f32) + self.held[a, self.z0, self.y, :, low].astype(f32)
        second = self.one_z[a, self.y].astype(f32) + self.held[a, self.z0, self.y, :, high].astype(f32)
        return self.two[a].astype(f32) + jnp.concatenate([first, second], 1)

    def arrive(self):
        self.wait(self.base + 2, self.two.at[:, :, self.lanes(0)])
        self.wait(self.base + 3, self.two.at[:, :, self.lanes(1)])


class Reduction:
    def __init__(self, bits, wait, send, base, buffers):
        self.wait, self.send, self.base = wait, send, base
        self.held, self.x_in, self.last = buffers[0], buffers[7], buffers[8]
        (self.x, self.x_peer), (self.z1, self.z1_peer) = bits["x"], bits["z1"]
        self.other = Chain(bits, wait, send, base + 2, self.held.at[1 - self.x], buffers[1:4])
        self.mine = Chain(bits, wait, send, base + 6, self.held.at[self.x], buffers[4:7])

    def pass_other(self):
        self.other.arrive()
        for a in range(2):
            self.other.two[a] = self.other.finish(a).astype(bf16)
        self.send(self.base + 10, self.other.two, self.x_in, self.x_peer)

    def pass_mine(self):
        self.mine.arrive()
        self.wait(self.base + 10, self.x_in)
        for k in range(2):
            a = 1 - self.z1 if k == 0 else self.z1
            total = self.mine.finish(a) + self.x_in[a].astype(f32)
            self.mine.two[a] = total.astype(bf16)
            if k == 0:
                self.send(self.base + 11, self.mine.two.at[a], self.last, self.z1_peer)

    def result(self):
        self.wait(self.base + 11, self.last)
        return self.mine.two[self.z1].astype(f32) + self.last[...].astype(f32)


def backward_kernel(
    cfg,
    lengths,
    positions,
    targets,
    query_weight,
    states,
    doc_ids,
    doc_table,
    w_query,
    gain_one,
    gain_two,
    pk,
    vocab,
    out_grad,
    res,
    x_in,
    qkv_in,
    lse_in,
    ctx_in,
    n1_in,
    f1_in,
    hl_in,
    act_in,
    gp_in,
    n2_in,
    f2_in,
    wq_in,
    wo_in,
    wu_in,
    wd_in,
    output,
    nll_out,
    gt_out,
    gs_out,
    gwq_out,
    down_out,
    up_out,
    qkv_out,
    out_out,
    vec_out,
    big,
    shares,
    lg,
    ut,
    us,
    ur,
    sr,
    lb,
    dlog,
    st_all,
    diff,
    og,
    tmp,
    n1,
    n2,
    f1,
    f2,
    dy,
    act,
    gp,
    wq,
    wo,
    wu,
    wd,
    qkv,
    ctx,
    lse,
    d_t,
    x_t,
    d_up,
    dctx,
    dqkv,
    dxb,
    gt,
    sums,
    sums_in,
    own_states,
    attn_send,
    parts,
    *rest,
):
    n_seq, seq, model, queries, slots, table, docs = cfg
    red_bufs, (send_sem, recv_sem, local_sem) = rest[:-3], rest[-3:]
    m_rows = n_seq * seq
    own_rows = 8 * n_seq
    d = lax.axis_index("doc")
    t = lax.axis_index("tensor")
    t1, t2 = flip(t, 1), flip(t, 2)
    t3 = flip(t1, 2)
    x_bit = lax.div(t, 2)
    bits = {
        "x": (x_bit, {"tensor": t2}),
        "y": (lax.rem(d, 2), {"doc": flip(d, 1)}),
        "z0": (lax.rem(lax.div(d, 2), 2), {"doc": flip(d, 2)}),
        "z1": (lax.div(d, 4), {"doc": flip(d, 4)}),
    }

    barrier = pltpu.get_barrier_semaphore()
    doc_peers = [lax.rem(d + k, docs) for k in range(1, docs)]
    peers = [{"tensor": p} for p in (t1, t2, t3)] + [{"doc": p} for p in doc_peers]
    for peer in peers:
        pl.semaphore_signal(barrier, inc=1, device_id=peer, device_id_type=MESH)
    pl.semaphore_wait(barrier, len(peers))

    def remote(number, src, dst, peer):
        return pltpu.make_async_remote_copy(
            src_ref=src,
            dst_ref=dst,
            send_sem=send_sem.at[number],
            recv_sem=recv_sem.at[number],
            device_id=peer,
            device_id_type=MESH,
        )

    started = []

    def send(number, src, dst, peer):
        copy = remote(number, src, dst, peer)
        copy.start()
        started.append(copy)

    def arrived(number, ref):
        remote(number, ref, ref, {"tensor": t1}).wait_recv()

    loads = {}

    def load(name, src, dst):
        copy = pltpu.make_async_copy(src, dst, local_sem.at[len(loads)])
        copy.start()
        loads[name] = copy

    own = pl.multiple_of(t * n_seq, n_seq)
    for j in range(vocab.shape[0]):
        load("vocab%d" % j, vocab.at[j], big.at[j])
    base = 0
    share_width = model // docs
    wide = states[...].astype(f32)
    wide = jnp.concatenate([wide, jnp.zeros((queries, 128 - share_width), f32)], 1)
    fill = own_states.shape[0] - queries
    if fill:
        wide = jnp.concatenate([wide, jnp.zeros((fill, 128), f32)], 0)
    own_states[...] = wide.astype(bf16)
    st_all[d] = own_states[...]
    for k, p in enumerate(doc_peers):
        send(base + k, own_states, st_all.at[d], {"doc": p})
    states_base = base
    base += docs - 1
    order = (t3, t2, t1, t)
    first_row = d * (4 * n_seq)
    hot = picks(positions, first_row + t * n_seq, n_seq, queries)
    out_base = base
    base += 3
    all_rows = 4 * own_rows
    vocab_local = vocab.shape[0] * model
    chunk = model
    tall = lax.broadcasted_iota(jnp.int32, (all_rows, 1), 0)
    goal = jnp.zeros((all_rows, 1), jnp.int32)
    for b in range(all_rows):
        query = lax.rem(first_row + b // 8, queries)
        goal = jnp.where(tall == b, targets[query, b % 8], goal)
    goal = goal - t * vocab_local
    picked = rows_of(pk[...])
    for j in range(vocab_local // chunk):
        loads["vocab%d" % j].wait()
        lg[:, j * chunk : (j + 1) * chunk] = dot_nt(picked, square(big[j]))
    load("og", out_grad.at[pl.ds(own, n_seq)], og)
    load("n2", n2_in, n2)
    load("f2", f2_in, f2)
    load("hl", hl_in, tmp)

    high = jnp.max(lg[...], 1, keepdims=True)
    ut[...] = jnp.zeros_like(ut)

    def vocab_step(j, carry):
        mass, chosen = carry
        start = pl.multiple_of(j * chunk, chunk)
        values = lg[:, pl.ds(start, chunk)]
        e = jnp.exp(values - high)
        index = lax.broadcasted_iota(jnp.int32, (all_rows, chunk), 1) + start
        hits = (index == goal).astype(f32)
        both = jnp.concatenate([e, hits], 0).astype(bf16)
        ut[...] += dot(both, square(big[j]))
        mass = mass + jnp.sum(e, 1, keepdims=True)
        chosen = chosen + jnp.sum(hits * values, 1, keepdims=True)
        return mass, chosen

    zero = jnp.zeros((all_rows, 1), f32)
    mass, chosen = lax.fori_loop(0, vocab_local // chunk, vocab_step, (zero, zero))
    spread = lax.broadcasted_iota(jnp.int32, (all_rows, 128), 1)
    stats = jnp.where(spread == 0, high, jnp.where(spread == 1, mass, chosen))
    mean_row = (ut[:all_rows] * (1.0 / mass)).astype(bf16)
    goal_row = ut[all_rows:].astype(bf16)
    for j in range(4):
        part = slice(j * own_rows, (j + 1) * own_rows)
        us[j, :, :model] = mean_row[part]
        us[j, :, model:] = goal_row[part]
    part_base = base
    base += 6
    sr[t] = stats
    for k, p in enumerate((t2, t3, t1)):
        send(part_base + k, sr.at[t], sr.at[t], {"tensor": p})
    for k, p in enumerate((t2, t3, t1)):
        send(part_base + 3 + k, us.at[p], ur.at[t], {"tensor": p})
    ur[t] = us[t]
    for i in range(2):
        load("act%d" % i, act_in.at[order[i]], act.at[i])
    sums[0] = jnp.zeros(sums.shape[1:], f32)
    for name in ("og", "n2", "f2"):
        loads[name].wait()
    step_rows = 96

    def add_sum(row, value):
        sums[0, 8 + row] += jnp.sum(value, 0, keepdims=True)

    def second_norm(s, rows, flat, extra):
        upstream = og[s, rows].astype(f32)
        if extra is not None:
            upstream = upstream + extra
        normed = n2[flat]
        back = norm_back_rows(upstream, normed, f2[flat], gain_two[...].reshape(1, model))
        add_sum(4, upstream * normed)
        add_sum(5, upstream)
        add_sum(3, back)
        dy[flat] = back
        og[s, rows] = back.astype(bf16)

    for s in range(n_seq):

        @pl.loop(1, seq // step_rows)
        def _(i):
            start = pl.multiple_of(i * step_rows, step_rows)
            second_norm(s, pl.ds(start, step_rows), pl.ds(s * seq + start, step_rows), None)

    for k, p in enumerate((t2, t3, t1)):
        arrived(part_base + k, sr.at[p])
    highs = [sr[j, :, 0:1] for j in range(4)]
    top = jnp.maximum(jnp.maximum(highs[0], highs[1]), jnp.maximum(highs[2], highs[3]))
    masses = [sr[j, :, 1:2] * jnp.exp(highs[j] - top) for j in range(4)]
    whole = masses[0] + masses[1] + masses[2] + masses[3]
    picked_logit = sr[0, :, 2:3] + sr[1, :, 2:3] + sr[2, :, 2:3] + sr[3, :, 2:3]
    loglik = picked_logit - (top + jnp.log(whole))
    mine = first_row + t * n_seq
    for s in range(4 * n_seq):
        total = jnp.sum(loglik[8 * s : 8 * s + 8], 0, keepdims=True)
        lb[first_row + s] = jnp.broadcast_to(total, (1, 128))
    group_base = base
    base += docs - 1
    group_ref = lb.at[pl.ds(first_row, 4 * n_seq)]
    for k, p in enumerate(doc_peers):
        send(group_base + k, group_ref, group_ref, {"doc": p})
    for j in range(4):
        share = jnp.broadcast_to(masses[j] / whole, (all_rows, 128))
        shares[j] = share.reshape(4, own_rows, 128)
    loads["hl"].wait()
    x_t[...] = tmp[...].T
    load("x", x_in, tmp)
    for i in range(2):
        load("wd%d" % i, wd_in.at[order[i]], wd.at[i])
        load("gp%d" % i, gp_in.at[order[i]], gp.at[i])
        load("wu%d" % i, wu_in.at[order[i]], wu.at[i])
    for k, p in enumerate((t2, t3, t1)):
        arrived(part_base + 3 + k, ur.at[p])
    gap = jnp.zeros((own_rows, model), f32)
    for j in range(4):
        share = shares[j, t][:, 0:1]
        gap = gap + ur[j, :, model:].astype(f32) - share * ur[j, :, :model].astype(f32)
    diff[...] = gap
    for k in range(docs - 1):
        source = lax.rem(d + docs - 1 - k, docs)
        arrived(states_base + k, st_all.at[source])
    emb = jnp.zeros((own_states.shape[0], 128), f32)
    for j in range(docs):
        emb = emb + dot(st_all[j, :, :share_width], w_query[j])
    emb = emb[:queries]
    table_score = dot_f32(emb, doc_table[...], ((1,), (1,)))
    entry = lax.broadcasted_iota(jnp.int32, (queries, table), 1)
    hot_docs = [(entry == doc_ids[:, k : k + 1]).astype(f32) for k in range(slots)]
    prior = [jnp.sum(hot_docs[k] * table_score, 1, keepdims=True) for k in range(slots)]
    for k in range(docs - 1):
        source = lax.rem(d + docs - 1 - k, docs)
        arrived(group_base + k, lb.at[pl.ds(source * (4 * n_seq), 4 * n_seq)])
    joint = []
    for k in range(slots):
        column = lb[k * queries : (k + 1) * queries].reshape(queries, 128)
        joint.append(prior[k] + column[:, 0:1])

    def log_sum(values):
        largest = functools.reduce(jnp.maximum, values)
        total = functools.reduce(jnp.add, [jnp.exp(v - largest) for v in values])
        return largest + jnp.log(total)

    prior_lse, joint_lse = log_sum(prior), log_sum(joint)
    tall = lax.broadcasted_iota(jnp.int32, (queries, 1), 0)
    weight = jnp.zeros((queries, 1), f32)
    for k in range(queries):
        weight = jnp.where(tall == k, query_weight[k], weight)
    nll_out[...] = jnp.broadcast_to(prior_lse - joint_lse, (queries, 128))
    spread_docs = jnp.zeros((queries, table), f32)
    for k in range(slots):
        post = jnp.exp(joint[k] - joint_lse)
        before = jnp.exp(prior[k] - prior_lse)
        spread_docs = spread_docs + hot_docs[k] * (weight * (before - post))
        value = -weight * post
        dlog[k * queries : (k + 1) * queries] = jnp.broadcast_to(value, (queries, 128)).reshape(
            queries, 1, 128
        )
    d_emb = dot_f32(spread_docs, doc_table[...], ((1,), (0,))).astype(bf16)
    gs_out[...] = dot_nt(d_emb, w_query[d])
    gwq_out[...] = dot_tn(st_all[d, :queries, :share_width].astype(f32), d_emb.astype(f32))
    scattered = []
    for s in range(n_seq):
        coefficient = dlog[mine + s]
        rows = diff[8 * s : 8 * s + 8] * coefficient[:, 0:1]
        scattered.append(
            dot_f32(hot[8 * s : 8 * s + 8, 32 * s : 32 * s + 32], rows, ((0,), (0,)))
        )
    mine_out = output.at[pl.ds(own, n_seq)]
    send(out_base, res, mine_out, {"tensor": t2})
    send(out_base + 1, res, mine_out, {"tensor": t1})
    for s in range(n_seq):
        extra = jnp.concatenate([scattered[s], jnp.zeros((step_rows - 32, model), f32)], 0)
        second_norm(s, pl.ds(0, step_rows), pl.ds(s * seq, step_rows), extra)

    d_t[...] = rows_of(og[...]).T
    reds = []
    for k in range(3):
        reds.append(Reduction(bits, arrived, send, base, red_bufs[9 * k : 9 * k + 9]))
        base += 12
    down, up, attn = reds
    block_shape = (2, 2, 2, model // docs)

    def emit(red, i, sending, shard, lanes, value):
        value = value.reshape(block_shape + (value.shape[-1],))
        which = lax.div(shard, 2)
        if i % 2 == 0:
            sending[which, :, :, :, :, lanes] = value.astype(bf16)
        else:
            total = value + red.held[which, :, :, :, :, lanes].astype(f32)
            red.held[which, :, :, :, :, lanes] = total.astype(bf16)

    def before_block(red, i, shard):
        if i % 2 == 1:
            which = lax.div(shard, 2)
            arrived(red.base + i // 2, red.held.at[which])

    def after_block(red, i, sending, shard):
        if i % 2 == 0:
            which = lax.div(shard, 2)
            send(red.base + i // 2, sending.at[which], red.held.at[which], {"tensor": t1})

    down_send, up_send = big.at[0:2], big.at[2:4]
    tiles = model // 256
    for i, shard in enumerate(order):
        loads["act%d" % i].wait()
        before_block(down, i, shard)

        @pl.loop(0, tiles)
        def _(n):
            lanes = pl.ds(pl.multiple_of(n * 256, 256), 256)
            emit(down, i, down_send, shard, lanes, dot(d_t[...], act[i % 2, :, lanes]))

        if i + 2 < 4:
            load("act%d" % (i + 2), act_in.at[order[i + 2]], act.at[i % 2])
        after_block(down, i, down_send, shard)
        if i == 1:
            down.other.start()
    down.mine.start()
    load("n1", n1_in, n1)
    load("f1", f1_in, f1)
    load("wo", wo_in, wo)
    load("ctx", ctx_in, ctx)
    load("lse", lse_in, lse)
    for i in range(2):
        load("qkv%d" % i, qkv_in.at[order[i]], qkv.at[i])
        load("wq%d" % i, wq_in.at[order[i]], wq.at[i])
    for i, shard in enumerate(order):
        for name in ("gp", "wd", "wu"):
            loads["%s%d" % (name, i)].wait()
        before_block(up, i, shard)

        @pl.loop(0, tiles)
        def _(n):
            lanes = pl.ds(pl.multiple_of(n * 256, 256), 256)
            value = dot_nt(rows_of(og[...]), wd[i % 2, lanes]) * gp[i % 2, :, lanes].astype(f32)
            low = value.astype(bf16)
            d_up[:, lanes] = low
            sums[0, shard, :, lanes] = jnp.sum(low.astype(f32), 0, keepdims=True)

        if i + 2 < 4:
            load("gp%d" % (i + 2), gp_in.at[order[i + 2]], gp.at[i % 2])
            load("wd%d" % (i + 2), wd_in.at[order[i + 2]], wd.at[i % 2])

        @pl.loop(0, tiles)
        def _(n):
            lanes = pl.ds(pl.multiple_of(n * 256, 256), 256)
            value = dot_nt(d_up[...], wu[i % 2, lanes])
            if i == 0:
                n2[:, lanes] = value
            else:
                n2[:, lanes] += value
            emit(up, i, up_send, shard, lanes, dot(x_t[...], d_up[:, lanes]))

        if i + 2 < 4:
            load("wu%d" % (i + 2), wu_in.at[order[i + 2]], wu.at[i % 2])
        after_block(up, i, up_send, shard)
        if i == 1:
            down.other.middle()
            up.other.start()
        if i == 2:
            down.mine.middle()
    up.mine.start()
    down.pass_other()
    arrived(out_base, output.at[pl.ds(t2 * n_seq, n_seq)])
    passed = output.at[pl.ds(t2 * n_seq, n_seq)]
    send(out_base + 2, passed, passed, {"tensor": t1})
    loads["n1"].wait()
    loads["f1"].wait()

    @pl.loop(0, m_rows // step_rows)
    def _(i):
        flat = pl.ds(pl.multiple_of(i * step_rows, step_rows), step_rows)
        s, start = lax.div(i, seq // step_rows), lax.rem(i, seq // step_rows) * step_rows
        upstream = dy[flat] + n2[flat]
        normed = n1[flat]
        back = norm_back_rows(upstream, normed, f1[flat], gain_one[...].reshape(1, model))
        add_sum(1, upstream * normed)
        add_sum(2, upstream)
        add_sum(0, back)
        dy[flat] = back
        og[s, pl.ds(pl.multiple_of(start, step_rows), step_rows)] = back.astype(bf16)

    d_t[...] = rows_of(og[...]).T
    up.other.middle()
    loads["x"].wait()
    x_t[...] = tmp[...].T
    for name in ("wo", "ctx", "lse"):
        loads[name].wait()
    vec_base = base
    vec_peers = [{"tensor": t1}, bits["y"][1], bits["z0"][1], bits["x"][1], bits["z1"][1]]
    base += len(vec_peers)

    def vec_start(k):
        send(vec_base + k, sums.at[k], sums_in.at[k], vec_peers[k])

    def vec_finish(k):
        arrived(vec_base + k, sums_in.at[k])
        sums[k + 1] = sums[k] + sums_in[k]

    key_index = lax.broadcasted_iota(jnp.int32, (seq, seq), 0)
    for i, shard in enumerate(order):
        loads["qkv%d" % i].wait()
        loads["wq%d" % i].wait()
        dctx[...] = dot_nt(rows_of(og[...]), wo[shard]).astype(bf16)

        @pl.loop(0, n_seq)
        def _(s):
            rows = pl.ds(pl.multiple_of(s * seq, 32), seq)
            row = first_row + t * n_seq + s
            length = lengths[lax.rem(row, queries), lax.div(row, queries)]
            z = qkv[i % 2, s]
            upstream = dctx[rows]
            d_q, d_k, d_v = [], [], []
            for h in range(3):
                qh = z[:, h * 64 : h * 64 + 64]
                kh = z[:, 192 + h * 64 : 256 + h * 64]
                vh = z[:, 384 + h * 64 : 448 + h * 64]
                dc = upstream[:, h * 64 : h * 64 + 64]
                scores = jnp.where(key_index < length, dot_nt(kh, qh * 0.125), -1000000000.0)
                prob = jnp.exp(scores - lse[shard, s, h])
                d_v.append(dot(prob.astype(bf16), dc))
                d_prob = dot_nt(vh, dc)
                inner = jnp.sum(d_prob * prob, 0, keepdims=True)
                d_score = (prob * (d_prob - inner)).astype(bf16)
                d_k.append(dot(d_score, qh) * 0.125)
                d_q.append(dot_tn(kh, d_score) * 0.125)
            first = jnp.concatenate(d_q, 0).T
            both = jnp.concatenate([first] + d_k + d_v, 1).astype(bf16)
            dqkv[rows] = both
            lse_sum = jnp.sum(both.astype(f32), 0, keepdims=True)
            parts[s] = lse_sum

        total = parts[0]
        for s in range(1, n_seq):
            total = total + parts[s]
        sums[0, 4 + shard, :, : 3 * 192] = total
        before_block(attn, i, shard)
        value = jnp.concatenate([dot(x_t[...], dqkv[...]), dot(d_t[...], ctx[shard])], 1)
        emit(attn, i, attn_send, shard, slice(None), value)
        after_block(attn, i, attn_send, shard)
        if i == 0:
            down.pass_mine()
            up.mine.middle()
        if i == 1:
            attn.other.start()
            up.pass_other()
        if i == 2:
            down_out[...] = down.result()
            up.pass_mine()
            attn.other.middle()
        if i == 3:
            attn.mine.start()
            vec_start(0)
            up_out[...] = up.result()
            attn.pass_other()

        @pl.loop(0, tiles)
        def _(n):
            lanes = pl.ds(pl.multiple_of(n * 256, 256), 256)
            value = dot(dqkv[...], wq[i % 2, :, lanes])
            if i == 0:
                n1[:, lanes] = value
            else:
                n1[:, lanes] += value

        if i + 2 < 4:
            load("qkv%d" % (i + 2), qkv_in.at[order[i + 2]], qkv.at[i % 2])
            load("wq%d" % (i + 2), wq_in.at[order[i + 2]], wq.at[i % 2])

    for j in range(4):
        lanes = slice(j * 192, j * 192 + 192)
        block = (n1[:, lanes] + dy[:, lanes]).astype(bf16)
        dxb[j] = jnp.concatenate([block[k * seq : (k + 1) * seq] for k in range(n_seq)], 1)
    tok_base = base
    base += 3
    for k, p in enumerate((t2, t3, t1)):
        send(tok_base + k, dxb.at[p], gt.at[t], {"tensor": p})
    gt[t] = dxb[t]
    vec_finish(0)
    vec_start(1)
    attn.mine.middle()
    vec_finish(1)
    vec_start(2)
    vec_finish(2)
    vec_start(3)
    attn.pass_mine()
    vec_finish(3)
    vec_start(4)
    for k, p in enumerate((t2, t3, t1)):
        arrived(tok_base + k, gt.at[p])
    load("gt", gt, gt_out)
    vec_finish(4)
    vec_out[...] = sums[5]
    total = attn.result()
    for k in range(3):
        qkv_out[k] = total[:, k * 192 : k * 192 + 192]
    out_out[...] = total[:, 576:].T
    arrived(out_base + 1, output.at[pl.ds(t1 * n_seq, n_seq)])
    arrived(out_base + 2, output.at[pl.ds(t3 * n_seq, n_seq)])
    loads["gt"].wait()
    for copy in started:
        copy.wait_send()


def backward(
    n_seq,
    seq,
    model,
    docs,
    tables,
    vocab,
    out_grad,
    kept,
):
    states, doc_ids, doc_table, w_query = tables[4:8]
    queries, slots = doc_ids.shape
    table = doc_table.shape[0]
    m_rows = n_seq * seq
    own_rows = 8 * n_seq
    all_rows = 4 * own_rows
    share = model // docs
    states_rows = -(-queries // 16) * 16
    (res, x, qkv, lse, ctx, n1, f1, hl, act, gp, n2, f2, wq, wo, wu, wd) = kept

    def flat(a):
        return a.reshape(a.shape[:-3] + (a.shape[-3] * a.shape[-2], a.shape[-1]))

    kept = [
        res,
        flat(x),
        qkv,
        lse,
        flat(ctx),
        flat(n1),
        flat(f1),
        flat(hl),
        flat(act),
        flat(gp),
        flat(n2),
        flat(f2),
        flat(wq),
        flat(wo),
        flat(wu),
        flat(wd),
    ]
    vocab = vocab.reshape(vocab.shape[0] // model, 2, 2, 2, share, model)

    def sds(shape, dtype):
        return jax.ShapeDtypeStruct(shape, dtype)

    any_spec = pl.BlockSpec(memory_space=pl.ANY)
    vmem_spec = pl.BlockSpec(memory_space=pltpu.VMEM)
    smem_spec = pl.BlockSpec(memory_space=pltpu.SMEM)
    outs = [
        sds((4 * n_seq, seq, model), bf16),
        sds((queries, 128), f32),
        sds((4, seq, n_seq * 192), bf16),
        sds((queries, share), f32),
        sds((share, 128), f32),
        sds((share, model), f32),
        sds((share, model), f32),
        sds((3, share, 192), f32),
        sds((192, share), f32),
        sds((14, 1, model), f32),
    ]
    out_specs = [any_spec, vmem_spec, any_spec] + [vmem_spec] * 7

    def vm(shape, dtype):
        return pltpu.VMEM(shape, dtype)

    scratch = [
        vm(vocab.shape, bf16),
        vm((4, 4, own_rows, 128), f32),
        vm((all_rows, vocab.shape[0] * model), f32),
        vm((2 * all_rows, model), f32),
        vm((4, own_rows, 2 * model), bf16),
        vm((4, own_rows, 2 * model), bf16),
        vm((4, all_rows, 128), f32),
        vm((docs * 4 * n_seq, 1, 128), f32),
        vm((docs * 4 * n_seq, 1, 128), f32),
        vm((docs, states_rows, 128), bf16),
        vm((own_rows, model), f32),
        vm((n_seq, seq, model), bf16),
        vm((m_rows, model), bf16),
        vm((m_rows, model), f32),
        vm((m_rows, model), f32),
        vm((m_rows, 1), f32),
        vm((m_rows, 1), f32),
        vm((m_rows, model), f32),
        vm((2, m_rows, model), bf16),
        vm((2, m_rows, model), bf16),
        vm((2, 576, model), bf16),
        vm((4, 192, model), bf16),
        vm((2, model, model), bf16),
        vm((2, model, model), bf16),
        vm((2, n_seq, seq, 576), bf16),
        vm((4, m_rows, 192), bf16),
        vm((4, n_seq, 3, 1, seq), f32),
        vm((model, m_rows), bf16),
        vm((model, m_rows), bf16),
        vm((m_rows, model), bf16),
        vm((m_rows, 192), bf16),
        vm((m_rows, 576), bf16),
        vm((4, seq, n_seq * 192), bf16),
        vm((4, seq, n_seq * 192), bf16),
        vm((6, 14, 1, model), f32),
        vm((5, 14, 1, model), f32),
        vm((states_rows, 128), bf16),
        vm((2, 2, 2, 2, share, model), bf16),
        vm((n_seq, 1, 576), f32),
    ]
    for _ in range(3):
        scratch.append(vm((2, 2, 2, 2, share, model), bf16))
        for _ in range(2):
            scratch.append(vm((2, 2, share, model // 2), bf16))
            scratch.append(vm((2, 2, share, model // 2), bf16))
            scratch.append(vm((2, share, model), bf16))
        scratch.append(vm((2, share, model), bf16))
        scratch.append(vm((share, model), bf16))
    copies = 2 * (docs - 1) + 3 + 6 + 12 * 3 + 3 + 5
    scratch += [
        pltpu.SemaphoreType.DMA((copies,)),
        pltpu.SemaphoreType.DMA((copies,)),
        pltpu.SemaphoreType.DMA((48,)),
    ]
    return pl.pallas_call(
        functools.partial(backward_kernel, (n_seq, seq, model, queries, slots, table, docs)),
        out_shape=outs,
        in_specs=[smem_spec] * 4 + [vmem_spec] * 7 + [any_spec] * 18,
        out_specs=out_specs,
        scratch_shapes=scratch,
        compiler_params=pltpu.CompilerParams(
            collective_id=1, has_side_effects=True, vmem_limit_bytes=60 * MIB
        ),
        name="layer_backward",
    )(*tables, vocab, out_grad, *kept)


def finish_kernel(cfg, *refs):
    n_seq, docs = cfg
    output, res, gs, gwq, down, up, qkv, out, gt_in, nll_in, sums_in = refs[:11]
    output_out, nll_out, tokens_out, gs_out, qkv_out, b_qv_out, out_out = refs[11:18]
    b_out_out, gain_one_out, bias_one_out, up_out, b_up_out, down_out = refs[18:24]
    b_down_out, gain_two_out, bias_two_out, gwq_out, gt, nll, sums, whole = refs[24:32]
    held, sem, sem_out = refs[32:-2], refs[-2], refs[-1]
    d = lax.axis_index("doc")
    t = lax.axis_index("tensor")
    pairs = [(gt_in, gt), (sums_in, sums), (nll_in, nll), (res, whole.at[pl.ds(t * n_seq, n_seq)])]
    for k in range(1, 4):
        part = pl.ds(lax.rem(t + k, 4) * n_seq, n_seq)
        pairs.append((output.at[part], whole.at[part]))
    passed = ((down, down_out), (up, up_out), (qkv, qkv_out), (out, out_out), (gs, gs_out))
    passed += ((gwq, gwq_out),)
    pairs += [(pair[0], buf) for pair, buf in zip(passed, held)]
    copies = [pltpu.make_async_copy(*pair, sem.at[k]) for k, pair in enumerate(pairs)]
    for copy in copies:
        copy.start()
    ends = []

    def forward_to(number, src, dst):
        copies[number].wait()
        copy = pltpu.make_async_copy(src, dst, sem_out.at[len(ends)])
        copy.start()
        ends.append(copy)

    for k in range(4):
        part = pl.ds(lax.rem(t + k, 4) * n_seq, n_seq)
        forward_to(3 + k, whole.at[part], output_out.at[part])
    for k, (pair, buf) in enumerate(zip(passed, held)):
        forward_to(7 + k, buf, pair[1])
    part_width = gt.shape[-1] // n_seq
    copies[0].wait()
    for j in range(4):
        for s in range(n_seq):
            lanes = slice(s * part_width, (s + 1) * part_width)
            tokens_out[j * n_seq + s] = gt[j, :, lanes].astype(f32)
    copies[1].wait()
    copies[2].wait()
    nll_out[...] = nll[:, 0]
    heads = sums[4 + t]
    b_qv_out[0:1] = heads[:, :part_width]
    b_qv_out[1:2] = heads[:, 2 * part_width : 3 * part_width]
    b_up_out[...] = sums[t].reshape(b_up_out.shape)
    width = b_out_out.shape[0]
    singles = (b_out_out, gain_one_out, bias_one_out, b_down_out, gain_two_out, bias_two_out)
    for k, ref in enumerate(singles):
        row = sums[8 + k]
        own = jnp.zeros((1, width), f32)
        for j in range(docs):
            own = own + jnp.where(d == j, row[:, j * width : (j + 1) * width], 0.0)
        ref[...] = own.reshape(width)
    for copy in ends:
        copy.wait()


def finish(n_seq, docs, parts):
    output, res, gt, nll, gs, gwq, down, up, qkv, out, sums = parts
    model = sums.shape[-1]
    share = model // docs
    part_width = gt.shape[-1] // n_seq

    def sds(*shape):
        return jax.ShapeDtypeStruct(shape, f32)

    outs = [
        jax.ShapeDtypeStruct(output.shape, bf16),
        sds(nll.shape[0]),
        sds(4 * n_seq, gt.shape[1], part_width),
        sds(*gs.shape),
        sds(*qkv.shape),
        sds(2, part_width),
        sds(*out.shape),
        sds(share),
        sds(share),
        sds(share),
        sds(*up.shape),
        sds(model),
        sds(*down.shape),
        sds(share),
        sds(share),
        sds(share),
        sds(*gwq.shape),
    ]
    any_spec = pl.BlockSpec(memory_space=pltpu.HBM)
    vmem_spec = pl.BlockSpec(memory_space=pltpu.VMEM)
    out_specs = [vmem_spec] * 17
    for k in (0, 3, 4, 6, 10, 12, 16):
        out_specs[k] = any_spec
    results = pl.pallas_call(
        functools.partial(finish_kernel, (n_seq, docs)),
        out_shape=outs,
        in_specs=[any_spec] * 11,
        out_specs=out_specs,
        scratch_shapes=[
            pltpu.VMEM(gt.shape, gt.dtype),
            pltpu.VMEM(nll.shape, nll.dtype),
            pltpu.VMEM(sums.shape, sums.dtype),
            pltpu.VMEM(output.shape, output.dtype),
            *(pltpu.VMEM(a.shape, a.dtype) for a in (down, up, qkv, out, gs, gwq)),
            pltpu.SemaphoreType.DMA((13,)),
            pltpu.SemaphoreType.DMA((10,)),
        ],
        compiler_params=pltpu.CompilerParams(vmem_limit_bytes=62 * MIB),
        name="layer_results",
    )(output, res, gs, gwq, down, up, qkv, out, gt, nll, sums)
    results = list(results)
    results[12] = results[12].T
    return results


def joined(array, axis, combine):
    everything = jax.tree.map(lambda part: lax.all_gather(part, axis), array)
    initial = jax.tree.map(lambda part: part[0], everything)

    def step(k, so_far):
        return combine(so_far, jax.tree.map(lambda part: part[k], everything))

    return lax.fori_loop(1, lax.axis_size(axis), step, initial)


def norm_back(upstream, normed, factor, gain_vec):
    scaled = upstream * gain_vec
    inner = (
        scaled
        - jnp.mean(scaled, -1, keepdims=True)
        - normed * jnp.mean(scaled * normed, -1, keepdims=True)
    )
    return (inner * factor, jnp.sum(upstream * normed, 0), jnp.sum(upstream, 0))


def merge_pair(high_first, mass_first, high_second, mass_second):
    highest = jnp.maximum(high_first, high_second)
    return (
        highest,
        mass_first * jnp.exp(high_first - highest) + mass_second * jnp.exp(high_second - highest),
    )


def vocab_combine(first, second):
    highest, summed = merge_pair(first[0], first[1], second[0], second[1])
    return (highest, summed, first[2] + second[2])


def query_combine(first, second):
    prior_high, prior_mass = merge_pair(first[0], first[1], second[0], second[1])
    joint_high, joint_mass = merge_pair(first[2], first[3], second[2], second[3])
    return (prior_high, prior_mass, joint_high, joint_mass)


def partial_lse(members, values):
    highest = jnp.max(jnp.where(members, values[:, None], -1e30), 0)
    summed = jnp.sum(jnp.where(members, jnp.exp(values[:, None] - highest[None, :]), 0.0), 0)
    return (highest, summed)


def shards(
    tokens,
    query_states,
    w_qkv,
    b_qv,
    w_out,
    b_out,
    ln1_gain,
    ln1_bias,
    w_up,
    b_up,
    w_down,
    b_down,
    ln2_gain,
    ln2_bias,
    w_query,
    doc_table,
    vocab_table,
    doc_ids,
    lengths,
    positions,
    targets,
    out_grad,
    query_weight,
):
    sequences, seq_length, part_width = tokens.shape
    model_width = w_qkv.shape[1]
    n_seq = sequences // 4
    row_count = n_seq * seq_length
    queries = lengths.shape[0]
    t = lax.axis_index("tensor")
    hidden = w_up.shape[1]
    vectors = (b_qv, b_up, b_out, ln1_gain, ln1_bias, b_down, ln2_gain, ln2_bias)
    quarter = model_width // 4
    weights_in = (
        w_qkv.transpose(0, 2, 1).reshape(4, 3 * quarter // 4, model_width),
        w_out.reshape(4, quarter // 4, model_width),
        w_up.reshape(4, quarter, hidden),
        w_down.reshape(4, hidden // 4, model_width),
    )
    (x, qkv, lse, ctx, n1, f1, hl, act, gp, n2, f2, res, wq, wo, wu, wd, pk) = forward(
        n_seq,
        seq_length,
        model_width,
        queries,
        (lengths, positions),
        tokens,
        weights_in,
        vectors,
    )
    docs = lax.axis_size("doc")
    if docs == 8 and n_seq == 2:
        share = model_width // docs
        tables = (
            lengths,
            positions,
            targets,
            query_weight,
            query_states,
            doc_ids,
            doc_table,
            w_query.reshape(docs, share, w_query.shape[1]),
            ln1_gain,
            ln2_gain,
            pk,
        )
        kept = (res, x, qkv, lse, ctx, n1, f1, hl, act, gp, n2, f2, wq, wo, wu, wd)
        (output, nll, gt, gs, gwq, g_down, g_up, g_qkv, g_out, sums) = backward(
            n_seq, seq_length, model_width, docs, tables, vocab_table, out_grad, kept
        )
        return tuple(
            finish(n_seq, docs, (output, res, gt, nll, gs, gwq, g_down, g_up, g_qkv, g_out, sums))
        )
    output = lax.all_gather(res, "tensor", axis=0, tiled=True)
    row_index = lax.axis_index("doc") * sequences + jnp.arange(sequences, dtype=jnp.int32)
    slot_index = row_index // queries
    query_index = row_index % queries
    row_position = positions[query_index]
    row_target = targets[query_index]
    own = lambda a: lax.dynamic_slice_in_dim(a, t * n_seq, n_seq, 0)
    own_position = own(row_position)
    seq_base = jnp.arange(n_seq, dtype=jnp.int32)[:, None]
    picked = lax.all_gather(res[seq_base, own_position], "tensor", axis=0, tiled=True)
    vocab_logits = jnp.einsum("btd,vd->btv", picked, vocab_table, preferred_element_type=f32)
    vocab_local = vocab_table.shape[0]
    vocab_ids = t * vocab_local + jnp.arange(vocab_local, dtype=jnp.int32)
    target_hits = vocab_ids[None, None, :] == row_target[:, :, None]
    local_high = jnp.max(vocab_logits, -1)
    local_mass = jnp.sum(jnp.exp(vocab_logits - local_high[:, :, None]), -1)
    local_chosen = jnp.sum(jnp.where(target_hits, vocab_logits, 0.0), -1)
    vocab_high, vocab_mass, chosen = joined(
        (local_high, local_mass, local_chosen), "tensor", vocab_combine
    )
    vocab_lse = vocab_high + jnp.log(vocab_mass)
    loglik = jnp.sum(chosen - vocab_lse, -1)
    states = lax.all_gather(query_states, "doc", axis=1, tiled=True)
    query_emb = jnp.dot(states, w_query, preferred_element_type=f32)
    members = query_index[:, None] == jnp.arange(queries, dtype=jnp.int32)[None, :]
    member_weights = members.astype(f32)
    own_emb = jnp.dot(member_weights, query_emb, precision=precise)
    embeds = doc_table[doc_ids[query_index, slot_index]]
    retrieval = jnp.sum(own_emb * embeds, -1)
    joint_score = retrieval + loglik
    prior_high, prior_mass = partial_lse(members, retrieval)
    joint_high, joint_mass = partial_lse(members, joint_score)
    prior_high, prior_mass, joint_high, joint_mass = joined(
        (prior_high, prior_mass, joint_high, joint_mass), "doc", query_combine
    )
    prior_lse = prior_high + jnp.log(prior_mass)
    joint_lse = joint_high + jnp.log(joint_mass)
    query_nll = prior_lse - joint_lse
    row_weight = query_weight[query_index]
    posterior = jnp.exp(joint_score - jnp.dot(member_weights, joint_lse, precision=precise))
    prior_prob = jnp.exp(retrieval - jnp.dot(member_weights, prior_lse, precision=precise))
    grad_loglik = -row_weight * posterior
    grad_retrieval = row_weight * (prior_prob - posterior)
    vocab_probs = jnp.exp(vocab_logits - vocab_lse[:, :, None])
    grad_logits = (grad_loglik[:, None, None] * (target_hits.astype(f32) - vocab_probs)).astype(
        bf16
    )
    grad_picked = lax.psum_scatter(
        jnp.einsum("btv,vd->btd", grad_logits, vocab_table, preferred_element_type=f32),
        "tensor",
        scatter_dimension=0,
        tiled=True,
    )
    grad_emb = jnp.dot(
        member_weights.T, grad_retrieval[:, None] * embeds, precision=precise
    ).astype(bf16)
    grad_w_query = jnp.dot(states.T, grad_emb, preferred_element_type=f32)
    grad_states = jnp.dot(grad_emb, w_query.T, preferred_element_type=f32)
    flat = lambda a: a.reshape(row_count, a.shape[-1])
    grad_result = flat(own(out_grad).astype(f32).at[seq_base, own_position].add(grad_picked))
    n1, f1, n2, f2, hl, x = flat(n1), flat(f1), flat(n2), flat(f2), flat(hl), flat(x)
    dy2, dg2, db2 = norm_back(grad_result, n2, f2, ln2_gain)
    d_low = dy2.astype(bf16)
    act, gp = act.reshape(4, row_count, hidden), gp.reshape(4, row_count, hidden)
    wu, wd = wu.reshape(4, model_width, hidden), wd.reshape(4, hidden, model_width)
    wq, wo = wq.reshape(4, 576, model_width).transpose(0, 2, 1), wo.reshape(4, 192, model_width)
    qkv, ctx = qkv.reshape(4, n_seq, seq_length, 576), ctx.reshape(4, row_count, 192)
    g_down = jnp.einsum("tmf,md->tfd", act, d_low, preferred_element_type=f32)
    d_act = jnp.einsum("md,tfd->tmf", d_low, wd, preferred_element_type=f32)
    d_up = (d_act * gp.astype(f32)).astype(bf16)
    g_up = jnp.einsum("md,tmf->tdf", hl, d_up, preferred_element_type=f32)
    g_b_up = jnp.sum(d_up.astype(f32), 1)
    d_hidden = dy2 + jnp.einsum("tmf,tdf->md", d_up, wu, preferred_element_type=f32)
    dy1, dg1, db1 = norm_back(d_hidden, n1, f1, ln1_gain)
    d_att = dy1.astype(bf16)
    g_out = jnp.einsum("tme,md->ted", ctx, d_att, preferred_element_type=f32)
    d_ctx = jnp.einsum("md,ted->tme", d_att, wo, preferred_element_type=f32).astype(bf16)
    d_ctx = d_ctx.reshape(4, n_seq, seq_length, 3, 64)
    heads = qkv.reshape(4, n_seq, seq_length, 3, 3, 64)
    hq, hk, hv = heads[:, :, :, 0], heads[:, :, :, 1], heads[:, :, :, 2]
    row_length = own(lengths[query_index, slot_index])
    key_mask = (jnp.arange(seq_length, dtype=jnp.int32)[None, :] < row_length[:, None])[
        None, :, None, None, :
    ]
    scores = jnp.einsum("tbqhe,tbkhe->tbhqk", hq, hk, preferred_element_type=f32) * 0.125
    scores = jnp.where(key_mask, scores, -1000000000.0)
    prob = jnp.exp(scores - lse.reshape(4, n_seq, 3, seq_length, 1))
    d_v = jnp.einsum("tbhqk,tbqhe->tbkhe", prob.astype(bf16), d_ctx, preferred_element_type=f32)
    d_prob = jnp.einsum("tbqhe,tbkhe->tbhqk", d_ctx, hv, preferred_element_type=f32)
    d_s = (prob * (d_prob - jnp.sum(d_prob * prob, -1, keepdims=True))).astype(bf16)
    d_q = jnp.einsum("tbhqk,tbkhe->tbqhe", d_s, hk, preferred_element_type=f32) * 0.125
    d_k = jnp.einsum("tbhqk,tbqhe->tbkhe", d_s, hq, preferred_element_type=f32) * 0.125
    d_qkv = jnp.stack([d_q, d_k, d_v], 3).reshape(4, row_count, 576).astype(bf16)
    g_b = jnp.sum(d_qkv.astype(f32), 1)
    g_qkv = jnp.einsum("md,tme->tde", x, d_qkv, preferred_element_type=f32)
    d_x = dy1 + jnp.einsum("tme,tde->md", d_qkv, wq, preferred_element_type=f32)
    d_x = d_x.reshape(n_seq, seq_length, 4, part_width).astype(bf16)
    grad_tokens = lax.all_to_all(d_x, "tensor", split_axis=2, concat_axis=0, tiled=True)
    grad_tokens = grad_tokens.reshape(sequences, seq_length, part_width).astype(f32)
    over_t = lambda a: lax.psum_scatter(a, "tensor", scatter_dimension=0, tiled=True)[0]
    docs = lambda a, k: lax.psum_scatter(a, "doc", scatter_dimension=k, tiled=True)
    g_qkv = docs(over_t(g_qkv), 0)
    g_qkv = jnp.stack([g_qkv[:, :192], g_qkv[:, 192:384], g_qkv[:, 384:]])
    g_b = lax.psum(over_t(g_b), "doc")
    small = lambda v: docs(lax.psum(v, "tensor"), 0)
    return (
        output,
        query_nll,
        grad_tokens,
        docs(grad_states, 1),
        g_qkv,
        jnp.stack([g_b[:192], g_b[384:]]),
        docs(over_t(g_out), 1),
        small(jnp.sum(dy1, 0)),
        small(dg1),
        small(db1),
        docs(over_t(g_up), 0),
        lax.psum(over_t(g_b_up), "doc"),
        docs(over_t(g_down), 1),
        small(jnp.sum(dy2, 0)),
        small(dg2),
        small(db2),
        docs(grad_w_query, 0),
    )


def solution(mesh):
    in_specs = (
        P("doc", None, "tensor"),
        P(None, "doc"),
        P(None, None, "tensor"),
        P(None, "tensor"),
        P("tensor", None),
        P(),
        P(),
        P(),
        P(None, "tensor"),
        P("tensor"),
        P("tensor", None),
        P(),
        P(),
        P(),
        P(),
        P(),
        P("tensor", None),
        P(),
        P(),
        P(),
        P(),
        P("doc", None, None),
        P(),
    )
    out_specs = (
        P("doc", None, None),
        P(),
        P("doc", None, "tensor"),
        P(None, "doc"),
        P(None, "doc", "tensor"),
        P(None, "tensor"),
        P("tensor", "doc"),
        P("doc"),
        P("doc"),
        P("doc"),
        P("doc", "tensor"),
        P("tensor"),
        P("tensor", "doc"),
        P("doc"),
        P("doc"),
        P("doc"),
        P("doc", None),
    )
    return jax.shard_map(shards, mesh=mesh, in_specs=in_specs, out_specs=out_specs, check_vma=False)
```

```python
import functools

import jax
import jax.numpy as jnp
from jax import lax
from jax.experimental import pallas as pl
from jax.experimental.pallas import tpu as pltpu
from jax.sharding import PartitionSpec as P

MESH = pl.DeviceIdType.MESH
f32 = jnp.float32
bf16 = jnp.bfloat16
MIB = 1024 * 1024


def flip(index, bit):
    return index + bit * (1 - 2 * lax.rem(lax.div(index, bit), 2))


def dot(a, b):
    return lax.dot_general(a, b, (((1,), (0,)), ((), ())), preferred_element_type=f32)


def dot_nt(a, b):
    return lax.dot_general(a, b, (((1,), (1,)), ((), ())), preferred_element_type=f32)


def dot_tn(a, b):
    return lax.dot_general(a, b, (((0,), (0,)), ((), ())), preferred_element_type=f32)


def rows_of(block):
    return block.reshape(block.shape[0] * block.shape[1], block.shape[2])


def picks(positions, first_row, n_seq, queries):
    shape = (8 * n_seq, 32 * n_seq)
    lane = lax.broadcasted_iota(jnp.int32, shape, 1)
    line = lax.broadcasted_iota(jnp.int32, shape, 0)
    spot = jnp.zeros(shape, jnp.int32)
    for b in range(8 * n_seq):
        query = lax.rem(first_row + b // 8, queries)
        spot = jnp.where(line == b, positions[query, b % 8] + 32 * (b // 8), spot)
    return (lane == spot).astype(f32)


def norm_forward(y):
    centred = y - jnp.mean(y, -1, keepdims=True)
    factor = lax.rsqrt(jnp.mean(centred * centred, -1, keepdims=True) + 1e-12)
    return centred * factor, factor


def forward_kernel(
    cfg,
    lengths,
    positions,
    tokens,
    w_qkv,
    w_out,
    w_up,
    w_down,
    b_qv,
    b_up,
    b_out,
    gain_one,
    bias_one,
    b_down,
    gain_two,
    bias_two,
    x_out,
    qkv_out,
    lse_out,
    ctx_out,
    n1_out,
    f1_out,
    hl_out,
    act_out,
    gp_out,
    n2_out,
    f2_out,
    res_out,
    wq_all,
    wo_all,
    wu_all,
    wd_all,
    pk,
    raw,
    packed,
    tok,
    x_s,
    qkv_s,
    lse_s,
    ctx_s,
    att_s,
    n1_s,
    f1_s,
    hl_s,
    act_s,
    gp_s,
    n2_s,
    f2_s,
    res_s,
    wq,
    wo,
    wu,
    wd,
    vec,
    send_sem,
    recv_sem,
    local_sem,
    out_sem,
):
    n_seq, seq, model, queries = cfg
    d = lax.axis_index("doc")
    t = lax.axis_index("tensor")
    t1, t2 = flip(t, 1), flip(t, 2)
    t3 = flip(t1, 2)
    d1, d2 = flip(d, 1), flip(d, 2)
    q = lax.rem(d, 4)
    q1, q2 = flip(q, 1), flip(q, 2)
    q3 = flip(q1, 2)

    def local(number, src, dst):
        copy = pltpu.make_async_copy(src, dst, local_sem.at[number])
        copy.start()
        return copy

    own_tok = local(1, tokens, raw)
    own_q = local(0, w_qkv, wq.at[t])
    barrier = pltpu.get_barrier_semaphore()
    peers = ({"tensor": t1}, {"tensor": t2}, {"tensor": t3}, {"doc": d1}, {"doc": d2})
    for peer in peers:
        pl.semaphore_signal(barrier, inc=1, device_id=peer, device_id_type=MESH)
    pl.semaphore_wait(barrier, len(peers))

    def remote(number, src, dst, peer):
        return pltpu.make_async_remote_copy(
            src_ref=src,
            dst_ref=dst,
            send_sem=send_sem.at[number],
            recv_sem=recv_sem.at[number],
            device_id=peer,
            device_id_type=MESH,
        )

    gathered = (wq, wo, wu, wd)
    inputs = (w_qkv, w_out, w_up, w_down)
    started = []

    def send(number, src, dst, peer):
        copy = remote(number, src, dst, peer)
        copy.start()
        started.append(copy)

    half = model // 8
    sources = ((0, None), (1, None), (2, 0), (2, 1), (3, 0), (3, 1))
    hops = (({"doc": d1}, q1), ({"doc": d2}, q2))

    def rows_view(ref, k, begin=0, count=None):
        if k is None and count is None:
            return ref
        begin = begin + (0 if k is None else k * half)
        return ref.at[pl.ds(begin, half if count is None else count)]

    def piece(a, part, shard=None):
        which, k = sources[a]
        return rows_view(gathered[which].at[t2 if shard is None else shard, part], k)

    def send_x(a, pieces):
        which, k = sources[a]
        src, dst = inputs[which].at[q], gathered[which].at[t, q]
        count = (src.shape[0] if k is None else half) // pieces
        for n in range(pieces):
            part = rows_view(src, k, n * count, count)
            remote(8 * a, part, rows_view(dst, k, n * count, count), {"tensor": t2}).start()
        started.append(remote(8 * a, rows_view(src, k), rows_view(dst, k), {"tensor": t2}))

    def send_core(which):
        send(core_base + which, inputs[which], gathered[which].at[t], {"tensor": t1})

    def arrived(number, ref):
        remote(number, ref, ref, {"tensor": t1}).wait_recv()

    def own_core(which):
        arrived(core_base + which, gathered[which].at[t1])

    def after_x(a):
        (first, _), (second, _) = hops[:: -1 if a % 2 else 1]
        arrived(8 * a, piece(a, q))
        send(8 * a + 1, piece(a, q), piece(a, q), first)
        send(8 * a + 2, piece(a, q), piece(a, q), second)
        send(8 * a + 4, piece(a, q), piece(a, q), {"tensor": t1})

    def after_first(a):
        (_, part), (second, _) = hops[:: -1 if a % 2 else 1]
        arrived(8 * a + 1, piece(a, part))
        send(8 * a + 3, piece(a, part), piece(a, part), second)
        send(8 * a + 5, piece(a, part), piece(a, part), {"tensor": t1})

    def after_second(a):
        (_, _), (_, part) = hops[:: -1 if a % 2 else 1]
        arrived(8 * a + 2, piece(a, part))
        send(8 * a + 6, piece(a, part), piece(a, part), {"tensor": t1})
        arrived(8 * a + 3, piece(a, q3))
        send(8 * a + 7, piece(a, q3), piece(a, q3), {"tensor": t1})

    def after_core(a):
        (_, one), (_, two) = hops[:: -1 if a % 2 else 1]
        for k, part in enumerate((q, one, two, q3)):
            arrived(8 * a + 4 + k, piece(a, part, t3))

    core_base, tok_base, vec_base, pick_base = 48, 52, 55, 58
    own = pl.multiple_of(t * n_seq, n_seq)
    def send_tokens(k, peer):
        send(tok_base + k, packed.at[peer], tok.at[t], {"tensor": peer})

    send_x(0, 3)
    own_tok.wait()
    part_width = model // 4
    for j in range(4):
        packed[j] = jnp.concatenate([raw[j * n_seq + s] for s in range(n_seq)], 1)
    tok[t] = packed[t]
    send_tokens(2, t1)
    send_tokens(0, t2)
    send_tokens(1, t3)
    own_o = local(3, w_out, wo.at[t])
    gap = jnp.zeros((1, part_width), f32)
    vec[t, 1:2] = jnp.concatenate([b_qv[0:1], gap, b_qv[1:2], gap], 1)
    singles = (b_up, None, b_out, gain_one, bias_one, b_down, gain_two, bias_two)
    for k, ref in enumerate(singles):
        if ref is not None:
            vec[t, k : k + 1] = ref[...].reshape(1, model)
    for a in range(4):
        send_core(a)
    for k, peer in enumerate((t2, t3, t1)):
        send(vec_base + k, vec.at[t], vec.at[t], {"tensor": peer})
    own_u = local(4, w_up, wu.at[t])
    own_d = local(5, w_down, wd.at[t])
    after_x(0)
    send_x(1, 3)
    after_x(1)
    send_x(3, 2)
    for k, peer in enumerate((t2, t3, t1)):
        arrived(tok_base + k, tok.at[peer])

    def row(k):
        return vec[t, k : k + 1, :]

    stores = []

    def store(src, dst):
        copy = pltpu.make_async_copy(src, dst, out_sem.at[len(stores)])
        copy.start()
        stores.append(copy)

    for s in range(n_seq):
        lanes = slice(s * part_width, (s + 1) * part_width)
        x_s[s] = jnp.concatenate([tok[j, :, lanes] for j in range(4)], axis=1)

    store(x_s, x_out)

    key_index = lax.broadcasted_iota(jnp.int32, (seq, seq), 0)

    def attention(part, first):
        @pl.loop(0, n_seq)
        def _(s):
            row = d * (4 * n_seq) + t * n_seq + s
            length = lengths[lax.rem(row, queries), lax.div(row, queries)]
            bias = vec[part, 1:2, :576]
            z = (dot_nt(x_s[s], rows_of(wq[part])) + bias).astype(bf16)
            qkv_s[part, s] = z
            pieces = []
            for h in range(3):
                qh = z[:, h * 64 : h * 64 + 64] * 0.125
                kh = z[:, 192 + h * 64 : 256 + h * 64]
                vh = z[:, 384 + h * 64 : 448 + h * 64]
                st = jnp.where(key_index < length, dot_nt(kh, qh), -1000000000.0)
                high = jnp.max(st, 0, keepdims=True)
                e = jnp.exp(st - high)
                total = jnp.sum(e, 0, keepdims=True)
                prob = (e * (1.0 / total)).astype(bf16)
                lse_s[part, s, h] = high + jnp.log(total)
                pieces.append(dot_tn(vh, prob))
            ctx_s[part, s] = jnp.concatenate(pieces, axis=0).T.astype(bf16)

    def project(part, first):
        @pl.loop(0, n_seq)
        def _(s):
            for n in range(model // 256):
                cols = slice(n * 256, n * 256 + 256)
                term = dot(ctx_s[part, s], rows_of(wo[part, :, :, cols]))
                if first:
                    att_s[s, :, cols] = term
                else:
                    att_s[s, :, cols] += term

    own_q.wait()
    after_first(0)
    send_x(2, 2)
    attention(t, True)
    send_x(4, 3)
    after_first(1)
    own_o.wait()
    project(t, True)
    for k, peer in enumerate((t2, t3, t1)):
        arrived(vec_base + k, vec.at[peer])
    own_core(0)
    own_core(1)
    after_x(3)
    attention(t1, False)
    send_x(5, 3)
    project(t1, False)
    after_x(2)
    after_second(0)
    attention(t2, False)
    after_second(1)
    project(t2, False)
    after_x(4)
    after_core(0)
    attention(t3, False)
    after_x(5)
    after_core(1)
    project(t3, False)
    store(qkv_s, qkv_out)
    store(lse_s, lse_out)
    store(ctx_s, ctx_out)
    store(wq, wq_all)
    store(wo, wo_all)

    after_first(3)
    chunk = 96
    chunks = seq // chunk

    @pl.loop(0, n_seq * chunks)
    def _(i):
        s, r = lax.div(i, chunks), pl.multiple_of(lax.rem(i, chunks) * chunk, chunk)
        rows = pl.ds(r, chunk)
        y = x_s[s, rows].astype(f32) + att_s[s, rows] + row(2)
        n1, f1 = norm_forward(y)
        n1_s[s, rows] = n1
        f1_s[s, rows] = f1
        hl_s[s, rows] = (n1 * row(3) + row(4)).astype(bf16)

    store(n1_s, n1_out)
    store(f1_s, f1_out)
    store(hl_s, hl_out)
    after_first(2)
    own_u.wait()
    own_d.wait()

    def ffn_up(part):
        @pl.loop(0, n_seq * (model // 256))
        def _(i):
            s, n = lax.div(i, model // 256), lax.rem(i, model // 256)
            cols = pl.ds(pl.multiple_of(n * 256, 256), 256)
            u = dot(hl_s[s], rows_of(wu[part, :, :, cols])) + vec[part, 0:1, cols]
            cdf = 0.5 * (1.0 + lax.erf(u * 0.7071067811865476))
            pdf = jnp.exp(u * u * -0.5) * 0.3989422804014327
            act_s[part, s, :, cols] = (u * cdf).astype(bf16)
            gp_s[part, s, :, cols] = (cdf + u * pdf).astype(bf16)

    def ffn_down(part, first):
        @pl.loop(0, n_seq * (model // 256))
        def _(i):
            s, n = lax.div(i, model // 256), lax.rem(i, model // 256)
            cols = pl.ds(pl.multiple_of(n * 256, 256), 256)
            term = dot(act_s[part, s], rows_of(wd[part, :, :, cols]))
            if first:
                att_s[s, :, cols] = term
            else:
                att_s[s, :, cols] += term

    def store_ffn(part):
        store(act_s.at[part], act_out.at[part])
        store(gp_s.at[part], gp_out.at[part])
        store(wu.at[part], wu_all.at[part])
        store(wd.at[part], wd_all.at[part])

    def store_ffn(part):
        store(act_s.at[part], act_out.at[part])
        store(gp_s.at[part], gp_out.at[part])
        store(wu.at[part], wu_all.at[part])
        store(wd.at[part], wd_all.at[part])

    ffn_up(t)
    store_ffn(t)
    after_first(4)
    ffn_down(t, True)
    after_first(5)
    own_core(2)
    ffn_up(t1)
    own_core(3)
    store_ffn(t1)
    ffn_down(t1, False)
    after_second(3)
    after_second(2)
    ffn_up(t2)
    after_second(4)
    after_second(5)
    store_ffn(t2)
    ffn_down(t2, False)
    after_core(3)
    after_core(2)
    ffn_up(t3)
    after_core(4)
    after_core(5)
    store_ffn(t3)
    ffn_down(t3, False)

    @pl.loop(0, n_seq * chunks)
    def _(i):
        s, r = lax.div(i, chunks), pl.multiple_of(lax.rem(i, chunks) * chunk, chunk)
        rows = pl.ds(r, chunk)
        y = n1_s[s, rows] * row(3) + row(4) + att_s[s, rows] + row(5)
        n2, f2 = norm_forward(y)
        n2_s[s, rows] = n2
        f2_s[s, rows] = f2
        res_s[s, rows] = (n2 * row(6) + row(7)).astype(bf16)

    store(n2_s, n2_out)
    store(f2_s, f2_out)
    store(res_s, res_out)
    hot = picks(positions, d * (4 * n_seq) + t * n_seq, n_seq, queries).astype(bf16)
    pk[t] = dot(hot, rows_of(res_s[:, :32])).astype(bf16)
    for k, peer in enumerate((t2, t3, t1)):
        send(pick_base + k, pk.at[t], pk.at[t], {"tensor": peer})
    for k, peer in enumerate((t2, t3, t1)):
        arrived(pick_base + k, pk.at[peer])
    for copy in stores:
        copy.wait()
    for copy in started:
        copy.wait_send()


def forward(n_seq, seq, model, queries, tables, tokens, weights_in, vectors):
    def sds(shape, dtype):
        return jax.ShapeDtypeStruct(shape, dtype)

    acts = [
        ((n_seq, seq, model), bf16),
        ((4, n_seq, seq, 576), bf16),
        ((4, n_seq, 3, 1, seq), f32),
        ((4, n_seq, seq, 192), bf16),
        ((n_seq, seq, model), f32),
        ((n_seq, seq, 1), f32),
        ((n_seq, seq, model), bf16),
        ((4, n_seq, seq, model), bf16),
        ((4, n_seq, seq, model), bf16),
        ((n_seq, seq, model), f32),
        ((n_seq, seq, 1), f32),
        ((n_seq, seq, model), bf16),
    ]
    weights = [(4,) + w.shape for w in weights_in]
    any_spec = pl.BlockSpec(memory_space=pl.ANY)
    vmem_spec = pl.BlockSpec(memory_space=pltpu.VMEM)
    packed = (4, seq, n_seq * model // 4)
    scratch = [pltpu.VMEM(tokens.shape, bf16), pltpu.VMEM(packed, bf16), pltpu.VMEM(packed, bf16)]
    scratch += [pltpu.VMEM(*a) for a in acts[:4]]
    scratch += [pltpu.VMEM((n_seq, seq, model), f32)]
    scratch += [pltpu.VMEM(*a) for a in acts[4:]]
    scratch += [pltpu.VMEM(w, bf16) for w in weights]
    scratch += [pltpu.VMEM((4, 8, model), f32)]
    scratch += [
        pltpu.SemaphoreType.DMA((61,)),
        pltpu.SemaphoreType.DMA((61,)),
        pltpu.SemaphoreType.DMA((6,)),
        pltpu.SemaphoreType.DMA((32,)),
    ]
    return pl.pallas_call(
        functools.partial(forward_kernel, (n_seq, seq, model, queries)),
        out_shape=[sds(*a) for a in acts]
        + [sds(w, bf16) for w in weights]
        + [sds((4, 8 * n_seq, model), bf16)],
        in_specs=[pl.BlockSpec(memory_space=pltpu.SMEM)] * 2 + [any_spec] * 5 + [vmem_spec] * 8,
        out_specs=[any_spec] * 16 + [vmem_spec],
        scratch_shapes=scratch,
        compiler_params=pltpu.CompilerParams(
            collective_id=0, has_side_effects=True, vmem_limit_bytes=60 * MIB
        ),
        name="layer_forward",
    )(*tables, tokens, *weights_in, *vectors)


precise = lax.Precision.HIGHEST


def dot_f32(a, b, dims):
    return lax.dot_general(a, b, (dims, ((), ())), precision=precise, preferred_element_type=f32)


def square(block):
    return block.reshape(-1, block.shape[-1])


def norm_back_rows(upstream, normed, factor, gain_row):
    scaled = upstream * gain_row
    mean_one = jnp.mean(scaled, -1, keepdims=True)
    mean_two = jnp.mean(scaled * normed, -1, keepdims=True)
    return factor * (scaled - mean_one - normed * mean_two)


class Chain:
    def __init__(self, bits, wait, send, base, held, buffers):
        self.wait, self.send, self.base, self.held = wait, send, base, held
        self.one_y, self.one_z, self.two = buffers
        (self.y, self.y_peer), (self.z0, self.z0_peer) = bits["y"], bits["z0"]
        self.width = self.two.shape[-1] // 2

    def lanes(self, half):
        return slice(half * self.width, (half + 1) * self.width)

    def start(self):
        src = self.held.at[:, :, 1 - self.y, :, self.lanes(0)]
        self.send(self.base, src, self.one_y, self.y_peer)
        src = self.held.at[:, 1 - self.z0, :, :, self.lanes(1)]
        self.send(self.base + 1, src, self.one_z, self.z0_peer)

    def middle(self):
        low, high = self.lanes(0), self.lanes(1)
        self.wait(self.base, self.one_y)
        for a in range(2):
            there = self.one_y[a, 1 - self.z0].astype(f32)
            add = self.held[a, 1 - self.z0, self.y, :, low].astype(f32)
            self.one_y[a, 1 - self.z0] = (there + add).astype(bf16)
        src = self.one_y.at[:, 1 - self.z0]
        self.send(self.base + 2, src, self.two.at[:, :, low], self.z0_peer)
        self.wait(self.base + 1, self.one_z)
        for a in range(2):
            there = self.one_z[a, 1 - self.y].astype(f32)
            add = self.held[a, self.z0, 1 - self.y, :, high].astype(f32)
            self.one_z[a, 1 - self.y] = (there + add).astype(bf16)
        src = self.one_z.at[:, 1 - self.y]
        self.send(self.base + 3, src, self.two.at[:, :, high], self.y_peer)

    def finish(self, a):
        low, high = self.lanes(0), self.lanes(1)
        first = self.one_y[a, self.z0].astype(f32) + self.held[a, self.z0, self.y, :, low].astype(f32)
        second = self.one_z[a, self.y].astype(f32) + self.held[a, self.z0, self.y, :, high].astype(f32)
        return self.two[a].astype(f32) + jnp.concatenate([first, second], 1)

    def arrive(self):
        self.wait(self.base + 2, self.two.at[:, :, self.lanes(0)])
        self.wait(self.base + 3, self.two.at[:, :, self.lanes(1)])


class Reduction:
    def __init__(self, bits, wait, send, base, buffers):
        self.wait, self.send, self.base = wait, send, base
        self.held, self.x_in, self.last = buffers[0], buffers[7], buffers[8]
        (self.x, self.x_peer), (self.z1, self.z1_peer) = bits["x"], bits["z1"]
        self.other = Chain(bits, wait, send, base + 2, self.held.at[1 - self.x], buffers[1:4])
        self.mine = Chain(bits, wait, send, base + 6, self.held.at[self.x], buffers[4:7])

    def pass_other(self):
        self.other.arrive()
        for a in range(2):
            self.other.two[a] = self.other.finish(a).astype(bf16)
        self.send(self.base + 10, self.other.two, self.x_in, self.x_peer)

    def pass_mine(self):
        self.mine.arrive()
        self.wait(self.base + 10, self.x_in)
        for k in range(2):
            a = 1 - self.z1 if k == 0 else self.z1
            total = self.mine.finish(a) + self.x_in[a].astype(f32)
            self.mine.two[a] = total.astype(bf16)
            if k == 0:
                self.send(self.base + 11, self.mine.two.at[a], self.last, self.z1_peer)

    def result(self):
        self.wait(self.base + 11, self.last)
        return self.mine.two[self.z1].astype(f32) + self.last[...].astype(f32)


def backward_kernel(
    cfg,
    lengths,
    positions,
    targets,
    query_weight,
    states,
    doc_ids,
    doc_table,
    w_query,
    gain_one,
    gain_two,
    pk,
    vocab,
    out_grad,
    res,
    x_in,
    qkv_in,
    lse_in,
    ctx_in,
    n1_in,
    f1_in,
    hl_in,
    act_in,
    gp_in,
    n2_in,
    f2_in,
    wq_in,
    wo_in,
    wu_in,
    wd_in,
    output,
    nll_out,
    gt_out,
    gs_out,
    gwq_out,
    down_out,
    up_out,
    qkv_out,
    out_out,
    vec_out,
    big,
    shares,
    lg,
    ut,
    us,
    ur,
    sr,
    lb,
    dlog,
    st_all,
    diff,
    og,
    tmp,
    n1,
    n2,
    f1,
    f2,
    dy,
    act,
    gp,
    wq,
    wo,
    wu,
    wd,
    qkv,
    ctx,
    lse,
    d_t,
    x_t,
    d_up,
    dctx,
    dqkv,
    dxb,
    gt,
    sums,
    sums_in,
    own_states,
    attn_send,
    parts,
    *rest,
):
    n_seq, seq, model, queries, slots, table, docs = cfg
    red_bufs, (send_sem, recv_sem, local_sem) = rest[:-3], rest[-3:]
    m_rows = n_seq * seq
    own_rows = 8 * n_seq
    d = lax.axis_index("doc")
    t = lax.axis_index("tensor")
    t1, t2 = flip(t, 1), flip(t, 2)
    t3 = flip(t1, 2)
    x_bit = lax.div(t, 2)
    bits = {
        "x": (x_bit, {"tensor": t2}),
        "y": (lax.rem(d, 2), {"doc": flip(d, 1)}),
        "z0": (lax.rem(lax.div(d, 2), 2), {"doc": flip(d, 2)}),
        "z1": (lax.div(d, 4), {"doc": flip(d, 4)}),
    }

    loads = {}

    def load(name, src, dst):
        copy = pltpu.make_async_copy(src, dst, local_sem.at[len(loads)])
        copy.start()
        loads[name] = copy

    for j in range(vocab.shape[0]):
        load("vocab%d" % j, vocab.at[j], big.at[j])
    barrier = pltpu.get_barrier_semaphore()
    doc_peers = [lax.rem(d + k, docs) for k in range(1, docs)]
    peers = [{"tensor": p} for p in (t1, t2, t3)] + [{"doc": p} for p in doc_peers]
    for peer in peers:
        pl.semaphore_signal(barrier, inc=1, device_id=peer, device_id_type=MESH)
    pl.semaphore_wait(barrier, len(peers))

    def remote(number, src, dst, peer):
        return pltpu.make_async_remote_copy(
            src_ref=src,
            dst_ref=dst,
            send_sem=send_sem.at[number],
            recv_sem=recv_sem.at[number],
            device_id=peer,
            device_id_type=MESH,
        )

    started = []

    def send(number, src, dst, peer):
        copy = remote(number, src, dst, peer)
        copy.start()
        started.append(copy)

    def arrived(number, ref):
        remote(number, ref, ref, {"tensor": t1}).wait_recv()

    own = pl.multiple_of(t * n_seq, n_seq)
    base = 0
    share_width = model // docs
    wide = states[...].astype(f32)
    wide = jnp.concatenate([wide, jnp.zeros((queries, 128 - share_width), f32)], 1)
    fill = own_states.shape[0] - queries
    if fill:
        wide = jnp.concatenate([wide, jnp.zeros((fill, 128), f32)], 0)
    own_states[...] = wide.astype(bf16)
    st_all[d] = own_states[...]
    for k, p in enumerate(doc_peers):
        send(base + k, own_states, st_all.at[d], {"doc": p})
    states_base = base
    base += docs - 1
    order = (t3, t2, t1, t)
    down_order = (t3, t1, t2, t)
    first_row = d * (4 * n_seq)
    hot = picks(positions, first_row + t * n_seq, n_seq, queries)
    out_base = base
    base += 3
    all_rows = 4 * own_rows
    vocab_local = vocab.shape[0] * model
    chunk = model
    tall = lax.broadcasted_iota(jnp.int32, (all_rows, 1), 0)
    goal = jnp.zeros((all_rows, 1), jnp.int32)
    for b in range(all_rows):
        query = lax.rem(first_row + b // 8, queries)
        goal = jnp.where(tall == b, targets[query, b % 8], goal)
    goal = goal - t * vocab_local
    picked = rows_of(pk[...])
    for j in range(vocab_local // chunk):
        loads["vocab%d" % j].wait()
        lg[:, j * chunk : (j + 1) * chunk] = dot_nt(picked, square(big[j]))
    load("og", out_grad.at[pl.ds(own, n_seq)], og)
    load("n2", n2_in, n2)
    load("f2", f2_in, f2)
    load("hl", hl_in, tmp)

    high = jnp.max(lg[...], 1, keepdims=True)
    ut[...] = jnp.zeros_like(ut)

    def vocab_step(j, carry):
        mass, chosen = carry
        start = pl.multiple_of(j * chunk, chunk)
        values = lg[:, pl.ds(start, chunk)]
        e = jnp.exp(values - high)
        index = lax.broadcasted_iota(jnp.int32, (all_rows, chunk), 1) + start
        hits = (index == goal).astype(f32)
        both = jnp.concatenate([e, hits], 0).astype(bf16)
        ut[...] += dot(both, square(big[j]))
        mass = mass + jnp.sum(e, 1, keepdims=True)
        chosen = chosen + jnp.sum(hits * values, 1, keepdims=True)
        return mass, chosen

    zero = jnp.zeros((all_rows, 1), f32)
    mass, chosen = lax.fori_loop(0, vocab_local // chunk, vocab_step, (zero, zero))
    spread = lax.broadcasted_iota(jnp.int32, (all_rows, 128), 1)
    stats = jnp.where(spread == 0, high, jnp.where(spread == 1, mass, chosen))
    mean_row = (ut[:all_rows] * (1.0 / mass)).astype(bf16)
    goal_row = ut[all_rows:].astype(bf16)
    for j in range(4):
        part = slice(j * own_rows, (j + 1) * own_rows)
        us[j, :, :model] = mean_row[part]
        us[j, :, model:] = goal_row[part]
    part_base = base
    base += 6
    sr[t] = stats
    for k, p in enumerate((t2, t3, t1)):
        send(part_base + k, sr.at[t], sr.at[t], {"tensor": p})
    for k, p in enumerate((t2, t3, t1)):
        send(part_base + 3 + k, us.at[p], ur.at[t], {"tensor": p})
    ur[t] = us[t]
    for i in range(2):
        load("act%d" % i, act_in.at[down_order[i]], act.at[i])
    sums[0] = jnp.zeros(sums.shape[1:], f32)
    for name in ("og", "n2", "f2"):
        loads[name].wait()
    step_rows = 96

    def add_sum(row, value):
        sums[0, 8 + row] += jnp.sum(value, 0, keepdims=True)

    def second_norm(s, rows, flat, extra):
        upstream = og[s, rows].astype(f32)
        if extra is not None:
            upstream = upstream + extra
        normed = n2[flat]
        back = norm_back_rows(upstream, normed, f2[flat], gain_two[...].reshape(1, model))
        add_sum(4, upstream * normed)
        add_sum(5, upstream)
        add_sum(3, back)
        dy[flat] = back
        og[s, rows] = back.astype(bf16)

    for s in range(n_seq):

        @pl.loop(1, seq // step_rows)
        def _(i):
            start = pl.multiple_of(i * step_rows, step_rows)
            second_norm(s, pl.ds(start, step_rows), pl.ds(s * seq + start, step_rows), None)

    for k, p in enumerate((t2, t3, t1)):
        arrived(part_base + k, sr.at[p])
    highs = [sr[j, :, 0:1] for j in range(4)]
    top = jnp.maximum(jnp.maximum(highs[0], highs[1]), jnp.maximum(highs[2], highs[3]))
    masses = [sr[j, :, 1:2] * jnp.exp(highs[j] - top) for j in range(4)]
    whole = masses[0] + masses[1] + masses[2] + masses[3]
    picked_logit = sr[0, :, 2:3] + sr[1, :, 2:3] + sr[2, :, 2:3] + sr[3, :, 2:3]
    loglik = picked_logit - (top + jnp.log(whole))
    mine = first_row + t * n_seq
    for s in range(4 * n_seq):
        total = jnp.sum(loglik[8 * s : 8 * s + 8], 0, keepdims=True)
        lb[first_row + s] = jnp.broadcast_to(total, (1, 128))
    group_base = base
    base += docs - 1
    group_ref = lb.at[pl.ds(first_row, 4 * n_seq)]
    for k, p in enumerate(doc_peers):
        send(group_base + k, group_ref, group_ref, {"doc": p})
    for j in range(4):
        share = jnp.broadcast_to(masses[j] / whole, (all_rows, 128))
        shares[j] = share.reshape(4, own_rows, 128)
    loads["hl"].wait()
    x_t[...] = tmp[...].T
    load("x", x_in, tmp)
    for i in range(2):
        load("wd%d" % i, wd_in.at[order[i]], wd.at[i])
        load("gp%d" % i, gp_in.at[order[i]], gp.at[i])
        load("wu%d" % i, wu_in.at[order[i]], wu.at[i])
    for k, p in enumerate((t2, t3, t1)):
        arrived(part_base + 3 + k, ur.at[p])
    gap = jnp.zeros((own_rows, model), f32)
    for j in range(4):
        share = shares[j, t][:, 0:1]
        gap = gap + ur[j, :, model:].astype(f32) - share * ur[j, :, :model].astype(f32)
    diff[...] = gap
    for k in range(docs - 1):
        source = lax.rem(d + docs - 1 - k, docs)
        arrived(states_base + k, st_all.at[source])
    emb = jnp.zeros((own_states.shape[0], 128), f32)
    for j in range(docs):
        emb = emb + dot(st_all[j, :, :share_width], w_query[j])
    emb = emb[:queries]
    table_score = dot_f32(emb, doc_table[...], ((1,), (1,)))
    entry = lax.broadcasted_iota(jnp.int32, (queries, table), 1)
    hot_docs = [(entry == doc_ids[:, k : k + 1]).astype(f32) for k in range(slots)]
    prior = [jnp.sum(hot_docs[k] * table_score, 1, keepdims=True) for k in range(slots)]
    for k in range(docs - 1):
        source = lax.rem(d + docs - 1 - k, docs)
        arrived(group_base + k, lb.at[pl.ds(source * (4 * n_seq), 4 * n_seq)])
    joint = []
    for k in range(slots):
        column = lb[k * queries : (k + 1) * queries].reshape(queries, 128)
        joint.append(prior[k] + column[:, 0:1])

    def log_sum(values):
        largest = functools.reduce(jnp.maximum, values)
        total = functools.reduce(jnp.add, [jnp.exp(v - largest) for v in values])
        return largest + jnp.log(total)

    prior_lse, joint_lse = log_sum(prior), log_sum(joint)
    tall = lax.broadcasted_iota(jnp.int32, (queries, 1), 0)
    weight = jnp.zeros((queries, 1), f32)
    for k in range(queries):
        weight = jnp.where(tall == k, query_weight[k], weight)
    nll_out[...] = jnp.broadcast_to(prior_lse - joint_lse, (queries, 128))
    spread_docs = jnp.zeros((queries, table), f32)
    for k in range(slots):
        post = jnp.exp(joint[k] - joint_lse)
        before = jnp.exp(prior[k] - prior_lse)
        spread_docs = spread_docs + hot_docs[k] * (weight * (before - post))
        value = -weight * post
        dlog[k * queries : (k + 1) * queries] = jnp.broadcast_to(value, (queries, 128)).reshape(
            queries, 1, 128
        )
    d_emb = dot_f32(spread_docs, doc_table[...], ((1,), (0,))).astype(bf16)
    gs_out[...] = dot_nt(d_emb, w_query[d])
    gwq_out[...] = dot_tn(st_all[d, :queries, :share_width].astype(f32), d_emb.astype(f32))
    scattered = []
    for s in range(n_seq):
        coefficient = dlog[mine + s]
        rows = diff[8 * s : 8 * s + 8] * coefficient[:, 0:1]
        scattered.append(
            dot_f32(hot[8 * s : 8 * s + 8, 32 * s : 32 * s + 32], rows, ((0,), (0,)))
        )
    mine_out = output.at[pl.ds(own, n_seq)]
    send(out_base, res, mine_out, {"tensor": t2})
    send(out_base + 1, res, mine_out, {"tensor": t1})
    for s in range(n_seq):
        extra = jnp.concatenate([scattered[s], jnp.zeros((step_rows - 32, model), f32)], 0)
        second_norm(s, pl.ds(0, step_rows), pl.ds(s * seq, step_rows), extra)

    d_t[...] = rows_of(og[...]).T
    reds = []
    for k in range(3):
        reds.append(Reduction(bits, arrived, send, base, red_bufs[9 * k : 9 * k + 9]))
        base += 12
    down, up, attn = reds
    block_shape = (2, 2, 2, model // docs)

    def emit(red, shard, sending, lanes, value):
        value = value.reshape(block_shape + (value.shape[-1],))
        which = lax.div(shard, 2)
        if sending is not None:
            sending[which, :, :, :, :, lanes] = value.astype(bf16)
        else:
            total = value + red.held[which, :, :, :, :, lanes].astype(f32)
            red.held[which, :, :, :, :, lanes] = total.astype(bf16)

    def before_block(red, number, shard):
        arrived(red.base + number, red.held.at[lax.div(shard, 2)])

    def after_block(red, number, sending, shard):
        which = lax.div(shard, 2)
        send(red.base + number, sending.at[which], red.held.at[which], {"tensor": t1})

    down_send, up_send = big.at[0:2], big.at[2:4]
    tiles = model // 256
    for i, shard in enumerate(down_order):
        loads["act%d" % i].wait()
        if i >= 2:
            before_block(down, i - 2, shard)

        @pl.loop(0, tiles)
        def _(n):
            lanes = pl.ds(pl.multiple_of(n * 256, 256), 256)
            value = dot(d_t[...], act[i % 2, :, lanes])
            emit(down, shard, down_send if i < 2 else None, lanes, value)

        if i + 2 < 4:
            load("act%d" % (i + 2), act_in.at[down_order[i + 2]], act.at[i % 2])
        if i < 2:
            after_block(down, i, down_send, shard)
        if i == 2:
            down.other.start()
    load("n1", n1_in, n1)
    load("f1", f1_in, f1)
    load("wo", wo_in, wo)
    load("ctx", ctx_in, ctx)
    load("lse", lse_in, lse)
    for i in range(2):
        load("qkv%d" % i, qkv_in.at[order[i]], qkv.at[i])
        load("wq%d" % i, wq_in.at[order[i]], wq.at[i])
    for i, shard in enumerate(order):
        for name in ("gp", "wd", "wu"):
            loads["%s%d" % (name, i)].wait()

        @pl.loop(0, tiles)
        def _(n):
            lanes = pl.ds(pl.multiple_of(n * 256, 256), 256)
            value = dot_nt(rows_of(og[...]), wd[i % 2, lanes]) * gp[i % 2, :, lanes].astype(f32)
            low = value.astype(bf16)
            d_up[:, lanes] = low
            sums[0, 4 + shard, :, lanes] = jnp.sum(low.astype(f32), 0, keepdims=True)

        if i + 2 < 4:
            load("gp%d" % (i + 2), gp_in.at[order[i + 2]], gp.at[i % 2])
            load("wd%d" % (i + 2), wd_in.at[order[i + 2]], wd.at[i % 2])
        if i % 2:
            before_block(up, i // 2, shard)

        @pl.loop(0, tiles)
        def _(n):
            lanes = pl.ds(pl.multiple_of(n * 256, 256), 256)
            value = dot_nt(d_up[...], wu[i % 2, lanes])
            if i == 0:
                n2[:, lanes] = value
            else:
                n2[:, lanes] += value
            value = dot(x_t[...], d_up[:, lanes])
            emit(up, shard, None if i % 2 else up_send, lanes, value)

        if i + 2 < 4:
            load("wu%d" % (i + 2), wu_in.at[order[i + 2]], wu.at[i % 2])
        if i % 2 == 0:
            after_block(up, i // 2, up_send, shard)
        if i == 0:
            down.mine.start()
        if i == 2:
            up.other.start()
    arrived(out_base, output.at[pl.ds(t2 * n_seq, n_seq)])
    passed = output.at[pl.ds(t2 * n_seq, n_seq)]
    send(out_base + 2, passed, passed, {"tensor": t1})
    loads["n1"].wait()
    loads["f1"].wait()

    @pl.loop(0, m_rows // step_rows)
    def _(i):
        flat = pl.ds(pl.multiple_of(i * step_rows, step_rows), step_rows)
        s, start = lax.div(i, seq // step_rows), lax.rem(i, seq // step_rows) * step_rows
        upstream = dy[flat] + n2[flat]
        normed = n1[flat]
        back = norm_back_rows(upstream, normed, f1[flat], gain_one[...].reshape(1, model))
        add_sum(1, upstream * normed)
        add_sum(2, upstream)
        add_sum(0, back)
        dy[flat] = back
        og[s, pl.ds(pl.multiple_of(start, step_rows), step_rows)] = back.astype(bf16)

    d_t[...] = rows_of(og[...]).T
    up.mine.start()
    loads["x"].wait()
    x_t[...] = tmp[...].T
    for name in ("wo", "ctx", "lse"):
        loads[name].wait()
    vec_base = base
    vec_peers = [{"tensor": t1}, bits["y"][1], bits["z0"][1], bits["x"][1], bits["z1"][1]]
    base += 2 * len(vec_peers)
    early, late = pl.ds(4, 10), pl.ds(0, 4)

    def vec_start(k, rows):
        number = vec_base + k + (5 if rows is late else 0)
        send(number, sums.at[k, rows], sums_in.at[k, rows], vec_peers[k])

    def vec_finish(k, rows):
        number = vec_base + k + (5 if rows is late else 0)
        arrived(number, sums_in.at[k, rows])
        sums[k + 1, rows] = sums[k, rows] + sums_in[k, rows]

    def vec_next(k, rows):
        vec_finish(k, rows)
        vec_start(k + 1, rows)

    vec_start(0, early)

    def add_dx(i, first):
        @pl.loop(0, tiles)
        def _(n):
            lanes = pl.ds(pl.multiple_of(n * 256, 256), 256)
            value = dot(dqkv[i % 2], wq[i % 2, :, lanes])
            if first:
                n1[:, lanes] = value
            else:
                n1[:, lanes] += value

    key_index = lax.broadcasted_iota(jnp.int32, (seq, seq), 0)
    for i, shard in enumerate(order):
        loads["qkv%d" % i].wait()
        loads["wq%d" % i].wait()
        dctx[...] = dot_nt(rows_of(og[...]), wo[shard]).astype(bf16)

        @pl.loop(0, n_seq)
        def _(s):
            rows = pl.ds(pl.multiple_of(s * seq, 32), seq)
            row = first_row + t * n_seq + s
            length = lengths[lax.rem(row, queries), lax.div(row, queries)]
            z = qkv[i % 2, s]
            upstream = dctx[rows]
            d_q, d_k, d_v = [], [], []
            for h in range(3):
                qh = z[:, h * 64 : h * 64 + 64]
                kh = z[:, 192 + h * 64 : 256 + h * 64]
                vh = z[:, 384 + h * 64 : 448 + h * 64]
                dc = upstream[:, h * 64 : h * 64 + 64]
                scores = jnp.where(key_index < length, dot_nt(kh, qh * 0.125), -1000000000.0)
                prob = jnp.exp(scores - lse[shard, s, h])
                d_v.append(dot(prob.astype(bf16), dc))
                d_prob = dot_nt(vh, dc)
                inner = jnp.sum(d_prob * prob, 0, keepdims=True)
                d_score = (prob * (d_prob - inner)).astype(bf16)
                d_k.append(dot(d_score, qh) * 0.125)
                d_q.append(dot_tn(kh, d_score) * 0.125)
            first = jnp.concatenate(d_q, 0).T
            both = jnp.concatenate([first] + d_k + d_v, 1).astype(bf16)
            dqkv[i % 2, rows] = both
            lse_sum = jnp.sum(both.astype(f32), 0, keepdims=True)
            parts[s] = lse_sum

        total = parts[0]
        for s in range(1, n_seq):
            total = total + parts[s]
        sums[0, shard, :, : 3 * 192] = total
        if i % 2:
            before_block(attn, i // 2, shard)
        value = jnp.concatenate([dot(x_t[...], dqkv[i % 2]), dot(d_t[...], ctx[shard])], 1)
        emit(attn, shard, None if i % 2 else attn_send, slice(None), value)
        if i % 2 == 0:
            after_block(attn, i // 2, attn_send, shard)
        if i == 0:
            down.other.middle()
            down.mine.middle()
            up.other.middle()
            down.pass_other()
        if i == 1:
            attn.other.start()
            up.mine.middle()
            up.pass_other()
        if i == 2:
            down.pass_mine()
            attn.other.middle()
        if i == 3:
            attn.mine.start()
            vec_start(0, late)
            up.pass_mine()
        if i < 4:
            vec_next(i, early)
        if i < 2:
            add_dx(i, i == 0)
            load("qkv%d" % (i + 2), qkv_in.at[order[i + 2]], qkv.at[i])
            load("wq%d" % (i + 2), wq_in.at[order[i + 2]], wq.at[i])

    add_dx(2, False)
    add_dx(3, False)
    vec_next(0, late)
    attn.pass_other()
    for j in range(4):
        lanes = slice(j * 192, j * 192 + 192)
        block = (n1[:, lanes] + dy[:, lanes]).astype(bf16)
        dxb[j] = jnp.concatenate([block[k * seq : (k + 1) * seq] for k in range(n_seq)], 1)
    tok_base = base
    base += 3
    for k, p in enumerate((t2, t3, t1)):
        send(tok_base + k, dxb.at[p], gt.at[t], {"tensor": p})
    gt[t] = dxb[t]
    vec_next(1, late)
    down_out[...] = down.result()
    attn.mine.middle()
    vec_next(2, late)
    vec_finish(4, early)
    attn.pass_mine()
    vec_next(3, late)
    up_out[...] = up.result()
    vec_finish(4, late)
    vec_out[...] = sums[5]
    for k, p in enumerate((t2, t3, t1)):
        arrived(tok_base + k, gt.at[p])
    load("gt", gt, gt_out)
    total = attn.result()
    for k in range(3):
        qkv_out[k] = total[:, k * 192 : k * 192 + 192]
    out_out[...] = total[:, 576:].T
    arrived(out_base + 1, output.at[pl.ds(t1 * n_seq, n_seq)])
    arrived(out_base + 2, output.at[pl.ds(t3 * n_seq, n_seq)])
    loads["gt"].wait()
    for copy in started:
        copy.wait_send()


def backward(
    n_seq,
    seq,
    model,
    docs,
    tables,
    vocab,
    out_grad,
    kept,
):
    states, doc_ids, doc_table, w_query = tables[4:8]
    queries, slots = doc_ids.shape
    table = doc_table.shape[0]
    m_rows = n_seq * seq
    own_rows = 8 * n_seq
    all_rows = 4 * own_rows
    share = model // docs
    states_rows = -(-queries // 16) * 16
    (res, x, qkv, lse, ctx, n1, f1, hl, act, gp, n2, f2, wq, wo, wu, wd) = kept

    def flat(a):
        return a.reshape(a.shape[:-3] + (a.shape[-3] * a.shape[-2], a.shape[-1]))

    kept = [
        res,
        flat(x),
        qkv,
        lse,
        flat(ctx),
        flat(n1),
        flat(f1),
        flat(hl),
        flat(act),
        flat(gp),
        flat(n2),
        flat(f2),
        flat(wq),
        flat(wo),
        flat(wu),
        flat(wd),
    ]
    vocab = vocab.reshape(vocab.shape[0] // model, 2, 2, 2, share, model)

    def sds(shape, dtype):
        return jax.ShapeDtypeStruct(shape, dtype)

    any_spec = pl.BlockSpec(memory_space=pl.ANY)
    vmem_spec = pl.BlockSpec(memory_space=pltpu.VMEM)
    smem_spec = pl.BlockSpec(memory_space=pltpu.SMEM)
    outs = [
        sds((4 * n_seq, seq, model), bf16),
        sds((queries, 128), f32),
        sds((4, seq, n_seq * 192), bf16),
        sds((queries, share), f32),
        sds((share, 128), f32),
        sds((share, model), f32),
        sds((share, model), f32),
        sds((3, share, 192), f32),
        sds((192, share), f32),
        sds((14, 1, model), f32),
    ]
    out_specs = [any_spec, vmem_spec, any_spec] + [vmem_spec] * 7

    def vm(shape, dtype):
        return pltpu.VMEM(shape, dtype)

    scratch = [
        vm(vocab.shape, bf16),
        vm((4, 4, own_rows, 128), f32),
        vm((all_rows, vocab.shape[0] * model), f32),
        vm((2 * all_rows, model), f32),
        vm((4, own_rows, 2 * model), bf16),
        vm((4, own_rows, 2 * model), bf16),
        vm((4, all_rows, 128), f32),
        vm((docs * 4 * n_seq, 1, 128), f32),
        vm((docs * 4 * n_seq, 1, 128), f32),
        vm((docs, states_rows, 128), bf16),
        vm((own_rows, model), f32),
        vm((n_seq, seq, model), bf16),
        vm((m_rows, model), bf16),
        vm((m_rows, model), f32),
        vm((m_rows, model), f32),
        vm((m_rows, 1), f32),
        vm((m_rows, 1), f32),
        vm((m_rows, model), f32),
        vm((2, m_rows, model), bf16),
        vm((2, m_rows, model), bf16),
        vm((2, 576, model), bf16),
        vm((4, 192, model), bf16),
        vm((2, model, model), bf16),
        vm((2, model, model), bf16),
        vm((2, n_seq, seq, 576), bf16),
        vm((4, m_rows, 192), bf16),
        vm((4, n_seq, 3, 1, seq), f32),
        vm((model, m_rows), bf16),
        vm((model, m_rows), bf16),
        vm((m_rows, model), bf16),
        vm((m_rows, 192), bf16),
        vm((2, m_rows, 576), bf16),
        vm((4, seq, n_seq * 192), bf16),
        vm((4, seq, n_seq * 192), bf16),
        vm((6, 14, 1, model), f32),
        vm((5, 14, 1, model), f32),
        vm((states_rows, 128), bf16),
        vm((2, 2, 2, 2, share, model), bf16),
        vm((n_seq, 1, 576), f32),
    ]
    for _ in range(3):
        scratch.append(vm((2, 2, 2, 2, share, model), bf16))
        for _ in range(2):
            scratch.append(vm((2, 2, share, model // 2), bf16))
            scratch.append(vm((2, 2, share, model // 2), bf16))
            scratch.append(vm((2, share, model), bf16))
        scratch.append(vm((2, share, model), bf16))
        scratch.append(vm((share, model), bf16))
    copies = 2 * (docs - 1) + 3 + 6 + 12 * 3 + 3 + 10
    scratch += [
        pltpu.SemaphoreType.DMA((copies,)),
        pltpu.SemaphoreType.DMA((copies,)),
        pltpu.SemaphoreType.DMA((48,)),
    ]
    return pl.pallas_call(
        functools.partial(backward_kernel, (n_seq, seq, model, queries, slots, table, docs)),
        out_shape=outs,
        in_specs=[smem_spec] * 4 + [vmem_spec] * 7 + [any_spec] * 18,
        out_specs=out_specs,
        scratch_shapes=scratch,
        compiler_params=pltpu.CompilerParams(
            collective_id=1, has_side_effects=True, vmem_limit_bytes=60 * MIB
        ),
        name="layer_backward",
    )(*tables, vocab, out_grad, *kept)


def finish_kernel(cfg, *refs):
    n_seq, docs = cfg
    output, res, gs, gwq, down, up, qkv, out, gt_in, nll_in, sums_in = refs[:11]
    output_out, nll_out, tokens_out, gs_out, qkv_out, b_qv_out, out_out = refs[11:18]
    b_out_out, gain_one_out, bias_one_out, up_out, b_up_out, down_out = refs[18:24]
    b_down_out, gain_two_out, bias_two_out, gwq_out, gt, nll, sums, whole = refs[24:32]
    held, sem, sem_out = refs[32:-2], refs[-2], refs[-1]
    d = lax.axis_index("doc")
    t = lax.axis_index("tensor")
    pairs = [(gt_in, gt), (sums_in, sums), (nll_in, nll), (res, whole.at[pl.ds(t * n_seq, n_seq)])]
    for k in range(1, 4):
        part = pl.ds(lax.rem(t + k, 4) * n_seq, n_seq)
        pairs.append((output.at[part], whole.at[part]))
    passed = ((down, down_out), (up, up_out), (qkv, qkv_out), (out, out_out), (gs, gs_out))
    passed += ((gwq, gwq_out),)
    pairs += [(pair[0], buf) for pair, buf in zip(passed, held)]
    copies = [pltpu.make_async_copy(*pair, sem.at[k]) for k, pair in enumerate(pairs)]
    for copy in copies:
        copy.start()
    ends = []

    def forward_to(number, src, dst):
        copies[number].wait()
        copy = pltpu.make_async_copy(src, dst, sem_out.at[len(ends)])
        copy.start()
        ends.append(copy)

    for k in range(4):
        part = pl.ds(lax.rem(t + k, 4) * n_seq, n_seq)
        forward_to(3 + k, whole.at[part], output_out.at[part])
    for k, (pair, buf) in enumerate(zip(passed, held)):
        forward_to(7 + k, buf, pair[1])
    part_width = gt.shape[-1] // n_seq
    copies[0].wait()
    for j in range(4):
        for s in range(n_seq):
            lanes = slice(s * part_width, (s + 1) * part_width)
            tokens_out[j * n_seq + s] = gt[j, :, lanes].astype(f32)
    copies[1].wait()
    copies[2].wait()
    nll_out[...] = nll[:, 0]
    heads = sums[t]
    b_qv_out[0:1] = heads[:, :part_width]
    b_qv_out[1:2] = heads[:, 2 * part_width : 3 * part_width]
    b_up_out[...] = sums[4 + t].reshape(b_up_out.shape)
    width = b_out_out.shape[0]
    singles = (b_out_out, gain_one_out, bias_one_out, b_down_out, gain_two_out, bias_two_out)
    for k, ref in enumerate(singles):
        row = sums[8 + k]
        own = jnp.zeros((1, width), f32)
        for j in range(docs):
            own = own + jnp.where(d == j, row[:, j * width : (j + 1) * width], 0.0)
        ref[...] = own.reshape(width)
    for copy in ends:
        copy.wait()


def finish(n_seq, docs, parts):
    output, res, gt, nll, gs, gwq, down, up, qkv, out, sums = parts
    model = sums.shape[-1]
    share = model // docs
    part_width = gt.shape[-1] // n_seq

    def sds(*shape):
        return jax.ShapeDtypeStruct(shape, f32)

    outs = [
        jax.ShapeDtypeStruct(output.shape, bf16),
        sds(nll.shape[0]),
        sds(4 * n_seq, gt.shape[1], part_width),
        sds(*gs.shape),
        sds(*qkv.shape),
        sds(2, part_width),
        sds(*out.shape),
        sds(share),
        sds(share),
        sds(share),
        sds(*up.shape),
        sds(model),
        sds(*down.shape),
        sds(share),
        sds(share),
        sds(share),
        sds(*gwq.shape),
    ]
    any_spec = pl.BlockSpec(memory_space=pltpu.HBM)
    vmem_spec = pl.BlockSpec(memory_space=pltpu.VMEM)
    out_specs = [vmem_spec] * 17
    for k in (0, 3, 4, 6, 10, 12, 16):
        out_specs[k] = any_spec
    results = pl.pallas_call(
        functools.partial(finish_kernel, (n_seq, docs)),
        out_shape=outs,
        in_specs=[any_spec] * 11,
        out_specs=out_specs,
        scratch_shapes=[
            pltpu.VMEM(gt.shape, gt.dtype),
            pltpu.VMEM(nll.shape, nll.dtype),
            pltpu.VMEM(sums.shape, sums.dtype),
            pltpu.VMEM(output.shape, output.dtype),
            *(pltpu.VMEM(a.shape, a.dtype) for a in (down, up, qkv, out, gs, gwq)),
            pltpu.SemaphoreType.DMA((13,)),
            pltpu.SemaphoreType.DMA((10,)),
        ],
        compiler_params=pltpu.CompilerParams(vmem_limit_bytes=62 * MIB),
        name="layer_results",
    )(output, res, gs, gwq, down, up, qkv, out, gt, nll, sums)
    results = list(results)
    results[12] = results[12].T
    return results


def joined(array, axis, combine):
    everything = jax.tree.map(lambda part: lax.all_gather(part, axis), array)
    initial = jax.tree.map(lambda part: part[0], everything)

    def step(k, so_far):
        return combine(so_far, jax.tree.map(lambda part: part[k], everything))

    return lax.fori_loop(1, lax.axis_size(axis), step, initial)


def norm_back(upstream, normed, factor, gain_vec):
    scaled = upstream * gain_vec
    inner = (
        scaled
        - jnp.mean(scaled, -1, keepdims=True)
        - normed * jnp.mean(scaled * normed, -1, keepdims=True)
    )
    return (inner * factor, jnp.sum(upstream * normed, 0), jnp.sum(upstream, 0))


def merge_pair(high_first, mass_first, high_second, mass_second):
    highest = jnp.maximum(high_first, high_second)
    return (
        highest,
        mass_first * jnp.exp(high_first - highest) + mass_second * jnp.exp(high_second - highest),
    )


def vocab_combine(first, second):
    highest, summed = merge_pair(first[0], first[1], second[0], second[1])
    return (highest, summed, first[2] + second[2])


def query_combine(first, second):
    prior_high, prior_mass = merge_pair(first[0], first[1], second[0], second[1])
    joint_high, joint_mass = merge_pair(first[2], first[3], second[2], second[3])
    return (prior_high, prior_mass, joint_high, joint_mass)


def partial_lse(members, values):
    highest = jnp.max(jnp.where(members, values[:, None], -1e30), 0)
    summed = jnp.sum(jnp.where(members, jnp.exp(values[:, None] - highest[None, :]), 0.0), 0)
    return (highest, summed)


def shards(
    tokens,
    query_states,
    w_qkv,
    b_qv,
    w_out,
    b_out,
    ln1_gain,
    ln1_bias,
    w_up,
    b_up,
    w_down,
    b_down,
    ln2_gain,
    ln2_bias,
    w_query,
    doc_table,
    vocab_table,
    doc_ids,
    lengths,
    positions,
    targets,
    out_grad,
    query_weight,
):
    sequences, seq_length, part_width = tokens.shape
    model_width = w_qkv.shape[1]
    n_seq = sequences // 4
    row_count = n_seq * seq_length
    queries = lengths.shape[0]
    t = lax.axis_index("tensor")
    hidden = w_up.shape[1]
    vectors = (b_qv, b_up, b_out, ln1_gain, ln1_bias, b_down, ln2_gain, ln2_bias)
    quarter = model_width // 4
    weights_in = (
        w_qkv.transpose(0, 2, 1).reshape(4, 3 * quarter // 4, model_width),
        w_out.reshape(4, quarter // 4, model_width),
        w_up.reshape(4, quarter, hidden),
        w_down.reshape(4, hidden // 4, model_width),
    )
    (x, qkv, lse, ctx, n1, f1, hl, act, gp, n2, f2, res, wq, wo, wu, wd, pk) = forward(
        n_seq,
        seq_length,
        model_width,
        queries,
        (lengths, positions),
        tokens,
        weights_in,
        vectors,
    )
    docs = lax.axis_size("doc")
    if docs == 8 and n_seq == 2:
        share = model_width // docs
        tables = (
            lengths,
            positions,
            targets,
            query_weight,
            query_states,
            doc_ids,
            doc_table,
            w_query.reshape(docs, share, w_query.shape[1]),
            ln1_gain,
            ln2_gain,
            pk,
        )
        kept = (res, x, qkv, lse, ctx, n1, f1, hl, act, gp, n2, f2, wq, wo, wu, wd)
        (output, nll, gt, gs, gwq, g_down, g_up, g_qkv, g_out, sums) = backward(
            n_seq, seq_length, model_width, docs, tables, vocab_table, out_grad, kept
        )
        return tuple(
            finish(n_seq, docs, (output, res, gt, nll, gs, gwq, g_down, g_up, g_qkv, g_out, sums))
        )
    output = lax.all_gather(res, "tensor", axis=0, tiled=True)
    row_index = lax.axis_index("doc") * sequences + jnp.arange(sequences, dtype=jnp.int32)
    slot_index = row_index // queries
    query_index = row_index % queries
    row_position = positions[query_index]
    row_target = targets[query_index]
    own = lambda a: lax.dynamic_slice_in_dim(a, t * n_seq, n_seq, 0)
    own_position = own(row_position)
    seq_base = jnp.arange(n_seq, dtype=jnp.int32)[:, None]
    picked = lax.all_gather(res[seq_base, own_position], "tensor", axis=0, tiled=True)
    vocab_logits = jnp.einsum("btd,vd->btv", picked, vocab_table, preferred_element_type=f32)
    vocab_local = vocab_table.shape[0]
    vocab_ids = t * vocab_local + jnp.arange(vocab_local, dtype=jnp.int32)
    target_hits = vocab_ids[None, None, :] == row_target[:, :, None]
    local_high = jnp.max(vocab_logits, -1)
    local_mass = jnp.sum(jnp.exp(vocab_logits - local_high[:, :, None]), -1)
    local_chosen = jnp.sum(jnp.where(target_hits, vocab_logits, 0.0), -1)
    vocab_high, vocab_mass, chosen = joined(
        (local_high, local_mass, local_chosen), "tensor", vocab_combine
    )
    vocab_lse = vocab_high + jnp.log(vocab_mass)
    loglik = jnp.sum(chosen - vocab_lse, -1)
    states = lax.all_gather(query_states, "doc", axis=1, tiled=True)
    query_emb = jnp.dot(states, w_query, preferred_element_type=f32)
    members = query_index[:, None] == jnp.arange(queries, dtype=jnp.int32)[None, :]
    member_weights = members.astype(f32)
    own_emb = jnp.dot(member_weights, query_emb, precision=precise)
    embeds = doc_table[doc_ids[query_index, slot_index]]
    retrieval = jnp.sum(own_emb * embeds, -1)
    joint_score = retrieval + loglik
    prior_high, prior_mass = partial_lse(members, retrieval)
    joint_high, joint_mass = partial_lse(members, joint_score)
    prior_high, prior_mass, joint_high, joint_mass = joined(
        (prior_high, prior_mass, joint_high, joint_mass), "doc", query_combine
    )
    prior_lse = prior_high + jnp.log(prior_mass)
    joint_lse = joint_high + jnp.log(joint_mass)
    query_nll = prior_lse - joint_lse
    row_weight = query_weight[query_index]
    posterior = jnp.exp(joint_score - jnp.dot(member_weights, joint_lse, precision=precise))
    prior_prob = jnp.exp(retrieval - jnp.dot(member_weights, prior_lse, precision=precise))
    grad_loglik = -row_weight * posterior
    grad_retrieval = row_weight * (prior_prob - posterior)
    vocab_probs = jnp.exp(vocab_logits - vocab_lse[:, :, None])
    grad_logits = (grad_loglik[:, None, None] * (target_hits.astype(f32) - vocab_probs)).astype(
        bf16
    )
    grad_picked = lax.psum_scatter(
        jnp.einsum("btv,vd->btd", grad_logits, vocab_table, preferred_element_type=f32),
        "tensor",
        scatter_dimension=0,
        tiled=True,
    )
    grad_emb = jnp.dot(
        member_weights.T, grad_retrieval[:, None] * embeds, precision=precise
    ).astype(bf16)
    grad_w_query = jnp.dot(states.T, grad_emb, preferred_element_type=f32)
    grad_states = jnp.dot(grad_emb, w_query.T, preferred_element_type=f32)
    flat = lambda a: a.reshape(row_count, a.shape[-1])
    grad_result = flat(own(out_grad).astype(f32).at[seq_base, own_position].add(grad_picked))
    n1, f1, n2, f2, hl, x = flat(n1), flat(f1), flat(n2), flat(f2), flat(hl), flat(x)
    dy2, dg2, db2 = norm_back(grad_result, n2, f2, ln2_gain)
    d_low = dy2.astype(bf16)
    act, gp = act.reshape(4, row_count, hidden), gp.reshape(4, row_count, hidden)
    wu, wd = wu.reshape(4, model_width, hidden), wd.reshape(4, hidden, model_width)
    wq, wo = wq.reshape(4, 576, model_width).transpose(0, 2, 1), wo.reshape(4, 192, model_width)
    qkv, ctx = qkv.reshape(4, n_seq, seq_length, 576), ctx.reshape(4, row_count, 192)
    g_down = jnp.einsum("tmf,md->tfd", act, d_low, preferred_element_type=f32)
    d_act = jnp.einsum("md,tfd->tmf", d_low, wd, preferred_element_type=f32)
    d_up = (d_act * gp.astype(f32)).astype(bf16)
    g_up = jnp.einsum("md,tmf->tdf", hl, d_up, preferred_element_type=f32)
    g_b_up = jnp.sum(d_up.astype(f32), 1)
    d_hidden = dy2 + jnp.einsum("tmf,tdf->md", d_up, wu, preferred_element_type=f32)
    dy1, dg1, db1 = norm_back(d_hidden, n1, f1, ln1_gain)
    d_att = dy1.astype(bf16)
    g_out = jnp.einsum("tme,md->ted", ctx, d_att, preferred_element_type=f32)
    d_ctx = jnp.einsum("md,ted->tme", d_att, wo, preferred_element_type=f32).astype(bf16)
    d_ctx = d_ctx.reshape(4, n_seq, seq_length, 3, 64)
    heads = qkv.reshape(4, n_seq, seq_length, 3, 3, 64)
    hq, hk, hv = heads[:, :, :, 0], heads[:, :, :, 1], heads[:, :, :, 2]
    row_length = own(lengths[query_index, slot_index])
    key_mask = (jnp.arange(seq_length, dtype=jnp.int32)[None, :] < row_length[:, None])[
        None, :, None, None, :
    ]
    scores = jnp.einsum("tbqhe,tbkhe->tbhqk", hq, hk, preferred_element_type=f32) * 0.125
    scores = jnp.where(key_mask, scores, -1000000000.0)
    prob = jnp.exp(scores - lse.reshape(4, n_seq, 3, seq_length, 1))
    d_v = jnp.einsum("tbhqk,tbqhe->tbkhe", prob.astype(bf16), d_ctx, preferred_element_type=f32)
    d_prob = jnp.einsum("tbqhe,tbkhe->tbhqk", d_ctx, hv, preferred_element_type=f32)
    d_s = (prob * (d_prob - jnp.sum(d_prob * prob, -1, keepdims=True))).astype(bf16)
    d_q = jnp.einsum("tbhqk,tbkhe->tbqhe", d_s, hk, preferred_element_type=f32) * 0.125
    d_k = jnp.einsum("tbhqk,tbqhe->tbkhe", d_s, hq, preferred_element_type=f32) * 0.125
    d_qkv = jnp.stack([d_q, d_k, d_v], 3).reshape(4, row_count, 576).astype(bf16)
    g_b = jnp.sum(d_qkv.astype(f32), 1)
    g_qkv = jnp.einsum("md,tme->tde", x, d_qkv, preferred_element_type=f32)
    d_x = dy1 + jnp.einsum("tme,tde->md", d_qkv, wq, preferred_element_type=f32)
    d_x = d_x.reshape(n_seq, seq_length, 4, part_width).astype(bf16)
    grad_tokens = lax.all_to_all(d_x, "tensor", split_axis=2, concat_axis=0, tiled=True)
    grad_tokens = grad_tokens.reshape(sequences, seq_length, part_width).astype(f32)
    over_t = lambda a: lax.psum_scatter(a, "tensor", scatter_dimension=0, tiled=True)[0]
    docs = lambda a, k: lax.psum_scatter(a, "doc", scatter_dimension=k, tiled=True)
    g_qkv = docs(over_t(g_qkv), 0)
    g_qkv = jnp.stack([g_qkv[:, :192], g_qkv[:, 192:384], g_qkv[:, 384:]])
    g_b = lax.psum(over_t(g_b), "doc")
    small = lambda v: docs(lax.psum(v, "tensor"), 0)
    return (
        output,
        query_nll,
        grad_tokens,
        docs(grad_states, 1),
        g_qkv,
        jnp.stack([g_b[:192], g_b[384:]]),
        docs(over_t(g_out), 1),
        small(jnp.sum(dy1, 0)),
        small(dg1),
        small(db1),
        docs(over_t(g_up), 0),
        lax.psum(over_t(g_b_up), "doc"),
        docs(over_t(g_down), 1),
        small(jnp.sum(dy2, 0)),
        small(dg2),
        small(db2),
        docs(grad_w_query, 0),
    )


def solution(mesh):
    in_specs = (
        P("doc", None, "tensor"),
        P(None, "doc"),
        P(None, None, "tensor"),
        P(None, "tensor"),
        P("tensor", None),
        P(),
        P(),
        P(),
        P(None, "tensor"),
        P("tensor"),
        P("tensor", None),
        P(),
        P(),
        P(),
        P(),
        P(),
        P("tensor", None),
        P(),
        P(),
        P(),
        P(),
        P("doc", None, None),
        P(),
    )
    out_specs = (
        P("doc", None, None),
        P(),
        P("doc", None, "tensor"),
        P(None, "doc"),
        P(None, "doc", "tensor"),
        P(None, "tensor"),
        P("tensor", "doc"),
        P("doc"),
        P("doc"),
        P("doc"),
        P("doc", "tensor"),
        P("tensor"),
        P("tensor", "doc"),
        P("doc"),
        P("doc"),
        P("doc"),
        P("doc", None),
    )
    return jax.shard_map(shards, mesh=mesh, in_specs=in_specs, out_specs=out_specs, check_vma=False)
```

```python
import functools

import jax
import jax.numpy as jnp
from jax import lax
from jax.experimental import pallas as pl
from jax.experimental.pallas import tpu as pltpu
from jax.sharding import PartitionSpec as P

MESH = pl.DeviceIdType.MESH
f32 = jnp.float32
bf16 = jnp.bfloat16
MIB = 1024 * 1024


def flip(index, bit):
    return index + bit * (1 - 2 * lax.rem(lax.div(index, bit), 2))


def dot(a, b):
    return lax.dot_general(a, b, (((1,), (0,)), ((), ())), preferred_element_type=f32)


def dot_nt(a, b):
    return lax.dot_general(a, b, (((1,), (1,)), ((), ())), preferred_element_type=f32)


def dot_tn(a, b):
    return lax.dot_general(a, b, (((0,), (0,)), ((), ())), preferred_element_type=f32)


def rows_of(block):
    return block.reshape(block.shape[0] * block.shape[1], block.shape[2])


def picks(positions, first_row, n_seq, queries):
    shape = (8 * n_seq, 32 * n_seq)
    lane = lax.broadcasted_iota(jnp.int32, shape, 1)
    line = lax.broadcasted_iota(jnp.int32, shape, 0)
    spot = jnp.zeros(shape, jnp.int32)
    for b in range(8 * n_seq):
        query = lax.rem(first_row + b // 8, queries)
        spot = jnp.where(line == b, positions[query, b % 8] + 32 * (b // 8), spot)
    return (lane == spot).astype(f32)


def norm_forward(y):
    centred = y - jnp.mean(y, -1, keepdims=True)
    factor = lax.rsqrt(jnp.mean(centred * centred, -1, keepdims=True) + 1e-12)
    return centred * factor, factor


def forward_kernel(
    cfg,
    lengths,
    positions,
    tokens,
    w_qkv,
    w_out,
    w_up,
    w_down,
    b_qv,
    b_up,
    b_out,
    gain_one,
    bias_one,
    b_down,
    gain_two,
    bias_two,
    x_out,
    qkv_out,
    lse_out,
    ctx_out,
    n1_out,
    f1_out,
    hl_out,
    act_out,
    gp_out,
    n2_out,
    f2_out,
    res_out,
    wq_all,
    wo_all,
    wu_all,
    wd_all,
    pk,
    raw,
    packed,
    tok,
    x_s,
    qkv_s,
    lse_s,
    ctx_s,
    att_s,
    n1_s,
    f1_s,
    hl_s,
    act_s,
    gp_s,
    n2_s,
    f2_s,
    res_s,
    wq,
    wo,
    wu,
    wd,
    vec,
    send_sem,
    recv_sem,
    local_sem,
    out_sem,
):
    n_seq, seq, model, queries = cfg
    d = lax.axis_index("doc")
    t = lax.axis_index("tensor")
    t1, t2 = flip(t, 1), flip(t, 2)
    t3 = flip(t1, 2)
    d1, d2 = flip(d, 1), flip(d, 2)
    q = lax.rem(d, 4)
    q1, q2 = flip(q, 1), flip(q, 2)
    q3 = flip(q1, 2)

    def local(number, src, dst):
        copy = pltpu.make_async_copy(src, dst, local_sem.at[number])
        copy.start()
        return copy

    own_tok = local(1, tokens, raw)
    own_q = local(0, w_qkv, wq.at[t])
    barrier = pltpu.get_barrier_semaphore()
    peers = ({"tensor": t1}, {"tensor": t2}, {"tensor": t3}, {"doc": d1}, {"doc": d2})
    for peer in peers:
        pl.semaphore_signal(barrier, inc=1, device_id=peer, device_id_type=MESH)
    pl.semaphore_wait(barrier, len(peers))

    def remote(number, src, dst, peer):
        return pltpu.make_async_remote_copy(
            src_ref=src,
            dst_ref=dst,
            send_sem=send_sem.at[number],
            recv_sem=recv_sem.at[number],
            device_id=peer,
            device_id_type=MESH,
        )

    gathered = (wq, wo, wu, wd)
    inputs = (w_qkv, w_out, w_up, w_down)
    started = []

    def send(number, src, dst, peer):
        copy = remote(number, src, dst, peer)
        copy.start()
        started.append(copy)

    half = model // 8
    sources = ((0, None), (1, None), (2, 0), (2, 1), (3, 0), (3, 1))
    hops = (({"doc": d1}, q1), ({"doc": d2}, q2))

    def rows_view(ref, k, begin=0, count=None):
        if k is None and count is None:
            return ref
        begin = begin + (0 if k is None else k * half)
        return ref.at[pl.ds(begin, half if count is None else count)]

    def piece(a, part, shard=None):
        which, k = sources[a]
        return rows_view(gathered[which].at[t2 if shard is None else shard, part], k)

    def send_x(a, pieces):
        which, k = sources[a]
        src, dst = inputs[which].at[q], gathered[which].at[t, q]
        count = (src.shape[0] if k is None else half) // pieces
        for n in range(pieces):
            part = rows_view(src, k, n * count, count)
            remote(8 * a, part, rows_view(dst, k, n * count, count), {"tensor": t2}).start()
        started.append(remote(8 * a, rows_view(src, k), rows_view(dst, k), {"tensor": t2}))

    def send_core(which):
        send(core_base + which, inputs[which], gathered[which].at[t], {"tensor": t1})

    def arrived(number, ref):
        remote(number, ref, ref, {"tensor": t1}).wait_recv()

    def own_core(which):
        arrived(core_base + which, gathered[which].at[t1])

    def after_x(a):
        (first, _), (second, _) = hops[:: -1 if a % 2 else 1]
        arrived(8 * a, piece(a, q))
        send(8 * a + 1, piece(a, q), piece(a, q), first)
        send(8 * a + 2, piece(a, q), piece(a, q), second)
        send(8 * a + 4, piece(a, q), piece(a, q), {"tensor": t1})

    def after_first(a):
        (_, part), (second, _) = hops[:: -1 if a % 2 else 1]
        arrived(8 * a + 1, piece(a, part))
        send(8 * a + 3, piece(a, part), piece(a, part), second)
        send(8 * a + 5, piece(a, part), piece(a, part), {"tensor": t1})

    def after_second(a):
        (_, _), (_, part) = hops[:: -1 if a % 2 else 1]
        arrived(8 * a + 2, piece(a, part))
        send(8 * a + 6, piece(a, part), piece(a, part), {"tensor": t1})
        arrived(8 * a + 3, piece(a, q3))
        send(8 * a + 7, piece(a, q3), piece(a, q3), {"tensor": t1})

    def after_core(a):
        (_, one), (_, two) = hops[:: -1 if a % 2 else 1]
        for k, part in enumerate((q, one, two, q3)):
            arrived(8 * a + 4 + k, piece(a, part, t3))

    core_base, tok_base, vec_base, pick_base = 48, 52, 55, 58
    own = pl.multiple_of(t * n_seq, n_seq)
    def send_tokens(k, peer):
        send(tok_base + k, packed.at[peer], tok.at[t], {"tensor": peer})

    send_x(0, 3)
    own_tok.wait()
    part_width = model // 4
    for j in range(4):
        packed[j] = jnp.concatenate([raw[j * n_seq + s] for s in range(n_seq)], 1)
    tok[t] = packed[t]
    send_tokens(2, t1)
    send_tokens(0, t2)
    send_tokens(1, t3)
    own_o = local(3, w_out, wo.at[t])
    gap = jnp.zeros((1, part_width), f32)
    vec[t, 1:2] = jnp.concatenate([b_qv[0:1], gap, b_qv[1:2], gap], 1)
    singles = (b_up, None, b_out, gain_one, bias_one, b_down, gain_two, bias_two)
    for k, ref in enumerate(singles):
        if ref is not None:
            vec[t, k : k + 1] = ref[...].reshape(1, model)
    for a in range(4):
        send_core(a)
    for k, peer in enumerate((t2, t3, t1)):
        send(vec_base + k, vec.at[t], vec.at[t], {"tensor": peer})
    own_u = local(4, w_up, wu.at[t])
    own_d = local(5, w_down, wd.at[t])
    after_x(0)
    send_x(1, 3)
    after_x(1)
    send_x(3, 2)
    for k, peer in enumerate((t2, t3, t1)):
        arrived(tok_base + k, tok.at[peer])

    def row(k):
        return vec[t, k : k + 1, :]

    stores = []

    def store(src, dst):
        copy = pltpu.make_async_copy(src, dst, out_sem.at[len(stores)])
        copy.start()
        stores.append(copy)

    for s in range(n_seq):
        lanes = slice(s * part_width, (s + 1) * part_width)
        x_s[s] = jnp.concatenate([tok[j, :, lanes] for j in range(4)], axis=1)

    store(x_s, x_out)

    key_index = lax.broadcasted_iota(jnp.int32, (seq, seq), 0)

    def attention(part, first):
        @pl.loop(0, n_seq)
        def _(s):
            row = d * (4 * n_seq) + t * n_seq + s
            length = lengths[lax.rem(row, queries), lax.div(row, queries)]
            bias = vec[part, 1:2, :576]
            z = (dot_nt(x_s[s], rows_of(wq[part])) + bias).astype(bf16)
            qkv_s[part, s] = z
            pieces = []
            for h in range(3):
                qh = z[:, h * 64 : h * 64 + 64] * 0.125
                kh = z[:, 192 + h * 64 : 256 + h * 64]
                vh = z[:, 384 + h * 64 : 448 + h * 64]
                st = jnp.where(key_index < length, dot_nt(kh, qh), -1000000000.0)
                high = jnp.max(st, 0, keepdims=True)
                e = jnp.exp(st - high)
                total = jnp.sum(e, 0, keepdims=True)
                prob = (e * (1.0 / total)).astype(bf16)
                lse_s[part, s, h] = high + jnp.log(total)
                pieces.append(dot_tn(vh, prob))
            ctx_s[part, s] = jnp.concatenate(pieces, axis=0).T.astype(bf16)

    def project(part, first):
        @pl.loop(0, n_seq)
        def _(s):
            for n in range(model // 256):
                cols = slice(n * 256, n * 256 + 256)
                term = dot(ctx_s[part, s], rows_of(wo[part, :, :, cols]))
                if first:
                    att_s[s, :, cols] = term
                else:
                    att_s[s, :, cols] += term

    own_q.wait()
    after_first(0)
    send_x(2, 2)
    attention(t, True)
    send_x(4, 3)
    after_first(1)
    own_o.wait()
    project(t, True)
    for k, peer in enumerate((t2, t3, t1)):
        arrived(vec_base + k, vec.at[peer])
    own_core(0)
    own_core(1)
    after_x(3)
    attention(t1, False)
    send_x(5, 3)
    project(t1, False)
    after_x(2)
    after_second(0)
    attention(t2, False)
    after_second(1)
    project(t2, False)
    after_x(4)
    after_core(0)
    attention(t3, False)
    after_x(5)
    after_core(1)
    project(t3, False)
    store(qkv_s, qkv_out)
    store(lse_s, lse_out)
    store(ctx_s, ctx_out)
    store(wq, wq_all)
    store(wo, wo_all)

    after_first(3)
    chunk = 96
    chunks = seq // chunk

    @pl.loop(0, n_seq * chunks)
    def _(i):
        s, r = lax.div(i, chunks), pl.multiple_of(lax.rem(i, chunks) * chunk, chunk)
        rows = pl.ds(r, chunk)
        y = x_s[s, rows].astype(f32) + att_s[s, rows] + row(2)
        n1, f1 = norm_forward(y)
        n1_s[s, rows] = n1
        f1_s[s, rows] = f1
        hl_s[s, rows] = (n1 * row(3) + row(4)).astype(bf16)

    store(n1_s, n1_out)
    store(f1_s, f1_out)
    store(hl_s, hl_out)
    after_first(2)
    own_u.wait()
    own_d.wait()

    def ffn_up(part):
        @pl.loop(0, n_seq * (model // 256))
        def _(i):
            s, n = lax.div(i, model // 256), lax.rem(i, model // 256)
            cols = pl.ds(pl.multiple_of(n * 256, 256), 256)
            u = dot(hl_s[s], rows_of(wu[part, :, :, cols])) + vec[part, 0:1, cols]
            cdf = 0.5 * (1.0 + lax.erf(u * 0.7071067811865476))
            pdf = jnp.exp(u * u * -0.5) * 0.3989422804014327
            act_s[part, s, :, cols] = (u * cdf).astype(bf16)
            gp_s[part, s, :, cols] = (cdf + u * pdf).astype(bf16)

    def ffn_down(part, first):
        @pl.loop(0, n_seq * (model // 256))
        def _(i):
            s, n = lax.div(i, model // 256), lax.rem(i, model // 256)
            cols = pl.ds(pl.multiple_of(n * 256, 256), 256)
            term = dot(act_s[part, s], rows_of(wd[part, :, :, cols]))
            if first:
                att_s[s, :, cols] = term
            else:
                att_s[s, :, cols] += term

    def store_ffn(part):
        store(act_s.at[part], act_out.at[part])
        store(gp_s.at[part], gp_out.at[part])
        store(wu.at[part], wu_all.at[part])
        store(wd.at[part], wd_all.at[part])

    def store_ffn(part):
        store(act_s.at[part], act_out.at[part])
        store(gp_s.at[part], gp_out.at[part])
        store(wu.at[part], wu_all.at[part])
        store(wd.at[part], wd_all.at[part])

    ffn_up(t)
    store_ffn(t)
    after_first(4)
    ffn_down(t, True)
    after_first(5)
    own_core(2)
    ffn_up(t1)
    own_core(3)
    store_ffn(t1)
    ffn_down(t1, False)
    after_second(3)
    after_second(2)
    ffn_up(t2)
    after_second(4)
    after_second(5)
    store_ffn(t2)
    ffn_down(t2, False)
    after_core(3)
    after_core(2)
    ffn_up(t3)
    after_core(4)
    after_core(5)
    store_ffn(t3)
    ffn_down(t3, False)

    @pl.loop(0, n_seq * chunks)
    def _(i):
        s, r = lax.div(i, chunks), pl.multiple_of(lax.rem(i, chunks) * chunk, chunk)
        rows = pl.ds(r, chunk)
        y = n1_s[s, rows] * row(3) + row(4) + att_s[s, rows] + row(5)
        n2, f2 = norm_forward(y)
        n2_s[s, rows] = n2
        f2_s[s, rows] = f2
        res_s[s, rows] = (n2 * row(6) + row(7)).astype(bf16)

    store(n2_s, n2_out)
    store(f2_s, f2_out)
    store(res_s, res_out)
    hot = picks(positions, d * (4 * n_seq) + t * n_seq, n_seq, queries).astype(bf16)
    pk[t] = dot(hot, rows_of(res_s[:, :32])).astype(bf16)
    for k, peer in enumerate((t2, t3, t1)):
        send(pick_base + k, pk.at[t], pk.at[t], {"tensor": peer})
    for k, peer in enumerate((t2, t3, t1)):
        arrived(pick_base + k, pk.at[peer])
    for copy in stores:
        copy.wait()
    for copy in started:
        copy.wait_send()


def forward(n_seq, seq, model, queries, tables, tokens, weights_in, vectors):
    def sds(shape, dtype):
        return jax.ShapeDtypeStruct(shape, dtype)

    acts = [
        ((n_seq, seq, model), bf16),
        ((4, n_seq, seq, 576), bf16),
        ((4, n_seq, 3, 1, seq), f32),
        ((4, n_seq, seq, 192), bf16),
        ((n_seq, seq, model), f32),
        ((n_seq, seq, 1), f32),
        ((n_seq, seq, model), bf16),
        ((4, n_seq, seq, model), bf16),
        ((4, n_seq, seq, model), bf16),
        ((n_seq, seq, model), f32),
        ((n_seq, seq, 1), f32),
        ((n_seq, seq, model), bf16),
    ]
    weights = [(4,) + w.shape for w in weights_in]
    any_spec = pl.BlockSpec(memory_space=pl.ANY)
    vmem_spec = pl.BlockSpec(memory_space=pltpu.VMEM)
    packed = (4, seq, n_seq * model // 4)
    scratch = [pltpu.VMEM(tokens.shape, bf16), pltpu.VMEM(packed, bf16), pltpu.VMEM(packed, bf16)]
    scratch += [pltpu.VMEM(*a) for a in acts[:4]]
    scratch += [pltpu.VMEM((n_seq, seq, model), f32)]
    scratch += [pltpu.VMEM(*a) for a in acts[4:]]
    scratch += [pltpu.VMEM(w, bf16) for w in weights]
    scratch += [pltpu.VMEM((4, 8, model), f32)]
    scratch += [
        pltpu.SemaphoreType.DMA((61,)),
        pltpu.SemaphoreType.DMA((61,)),
        pltpu.SemaphoreType.DMA((6,)),
        pltpu.SemaphoreType.DMA((32,)),
    ]
    return pl.pallas_call(
        functools.partial(forward_kernel, (n_seq, seq, model, queries)),
        out_shape=[sds(*a) for a in acts]
        + [sds(w, bf16) for w in weights]
        + [sds((4, 8 * n_seq, model), bf16)],
        in_specs=[pl.BlockSpec(memory_space=pltpu.SMEM)] * 2 + [any_spec] * 5 + [vmem_spec] * 8,
        out_specs=[any_spec] * 16 + [vmem_spec],
        scratch_shapes=scratch,
        compiler_params=pltpu.CompilerParams(
            collective_id=0, has_side_effects=True, vmem_limit_bytes=60 * MIB
        ),
        name="layer_forward",
    )(*tables, tokens, *weights_in, *vectors)


precise = lax.Precision.HIGHEST


def dot_f32(a, b, dims):
    return lax.dot_general(a, b, (dims, ((), ())), precision=precise, preferred_element_type=f32)


def square(block):
    return block.reshape(-1, block.shape[-1])


def norm_back_rows(upstream, normed, factor, gain_row):
    scaled = upstream * gain_row
    mean_one = jnp.mean(scaled, -1, keepdims=True)
    mean_two = jnp.mean(scaled * normed, -1, keepdims=True)
    return factor * (scaled - mean_one - normed * mean_two)


class Chain:
    def __init__(self, bits, wait, send, base, held, buffers):
        self.wait, self.send, self.base, self.held = wait, send, base, held
        self.one_y, self.one_z, self.two = buffers
        (self.y, self.y_peer), (self.z0, self.z0_peer) = bits["y"], bits["z0"]
        self.width = self.two.shape[-1] // 2

    def lanes(self, half):
        return slice(half * self.width, (half + 1) * self.width)

    def start(self):
        src = self.held.at[:, :, 1 - self.y, :, self.lanes(0)]
        self.send(self.base, src, self.one_y, self.y_peer)
        src = self.held.at[:, 1 - self.z0, :, :, self.lanes(1)]
        self.send(self.base + 1, src, self.one_z, self.z0_peer)

    def middle(self):
        low, high = self.lanes(0), self.lanes(1)
        self.wait(self.base, self.one_y)
        for a in range(2):
            there = self.one_y[a, 1 - self.z0].astype(f32)
            add = self.held[a, 1 - self.z0, self.y, :, low].astype(f32)
            self.one_y[a, 1 - self.z0] = (there + add).astype(bf16)
        src = self.one_y.at[:, 1 - self.z0]
        self.send(self.base + 2, src, self.two.at[:, :, low], self.z0_peer)
        self.wait(self.base + 1, self.one_z)
        for a in range(2):
            there = self.one_z[a, 1 - self.y].astype(f32)
            add = self.held[a, self.z0, 1 - self.y, :, high].astype(f32)
            self.one_z[a, 1 - self.y] = (there + add).astype(bf16)
        src = self.one_z.at[:, 1 - self.y]
        self.send(self.base + 3, src, self.two.at[:, :, high], self.y_peer)

    def finish(self, a):
        low, high = self.lanes(0), self.lanes(1)
        first = self.one_y[a, self.z0].astype(f32) + self.held[a, self.z0, self.y, :, low].astype(f32)
        second = self.one_z[a, self.y].astype(f32) + self.held[a, self.z0, self.y, :, high].astype(f32)
        return self.two[a].astype(f32) + jnp.concatenate([first, second], 1)

    def arrive(self):
        self.wait(self.base + 2, self.two.at[:, :, self.lanes(0)])
        self.wait(self.base + 3, self.two.at[:, :, self.lanes(1)])


class Reduction:
    def __init__(self, bits, wait, send, base, buffers):
        self.wait, self.send, self.base = wait, send, base
        self.held, self.x_in, self.last = buffers[0], buffers[7], buffers[8]
        (self.x, self.x_peer), (self.z1, self.z1_peer) = bits["x"], bits["z1"]
        self.other = Chain(bits, wait, send, base + 2, self.held.at[1 - self.x], buffers[1:4])
        self.mine = Chain(bits, wait, send, base + 6, self.held.at[self.x], buffers[4:7])

    def pass_other(self):
        self.other.arrive()
        for a in range(2):
            self.other.two[a] = self.other.finish(a).astype(bf16)
        self.send(self.base + 10, self.other.two, self.x_in, self.x_peer)

    def pass_mine(self):
        self.mine.arrive()
        self.wait(self.base + 10, self.x_in)
        for k in range(2):
            a = 1 - self.z1 if k == 0 else self.z1
            total = self.mine.finish(a) + self.x_in[a].astype(f32)
            self.mine.two[a] = total.astype(bf16)
            if k == 0:
                self.send(self.base + 11, self.mine.two.at[a], self.last, self.z1_peer)

    def result(self):
        self.wait(self.base + 11, self.last)
        return self.mine.two[self.z1].astype(f32) + self.last[...].astype(f32)


def backward_kernel(
    cfg,
    lengths,
    positions,
    targets,
    query_weight,
    states,
    doc_ids,
    doc_table,
    w_query,
    gain_one,
    gain_two,
    pk,
    vocab,
    out_grad,
    res,
    x_in,
    qkv_in,
    lse_in,
    ctx_in,
    n1_in,
    f1_in,
    hl_in,
    act_in,
    gp_in,
    n2_in,
    f2_in,
    wq_in,
    wo_in,
    wu_in,
    wd_in,
    output,
    nll_out,
    gt_out,
    gs_out,
    gwq_out,
    down_out,
    up_out,
    qkv_out,
    out_out,
    vec_out,
    big,
    shares,
    lg,
    ut,
    us,
    ur,
    sr,
    lb,
    dlog,
    st_all,
    diff,
    og,
    tmp,
    n1,
    n2,
    f1,
    f2,
    dy,
    act,
    gp,
    wq,
    wo,
    wu,
    wd,
    qkv,
    ctx,
    lse,
    d_t,
    x_t,
    d_up,
    dctx,
    dqkv,
    dxb,
    gt,
    sums,
    sums_in,
    own_states,
    attn_send,
    parts,
    *rest,
):
    n_seq, seq, model, queries, slots, table, docs = cfg
    red_bufs, (send_sem, recv_sem, local_sem) = rest[:-3], rest[-3:]
    m_rows = n_seq * seq
    own_rows = 8 * n_seq
    d = lax.axis_index("doc")
    t = lax.axis_index("tensor")
    t1, t2 = flip(t, 1), flip(t, 2)
    t3 = flip(t1, 2)
    x_bit = lax.div(t, 2)
    bits = {
        "x": (x_bit, {"tensor": t2}),
        "y": (lax.rem(d, 2), {"doc": flip(d, 1)}),
        "z0": (lax.rem(lax.div(d, 2), 2), {"doc": flip(d, 2)}),
        "z1": (lax.div(d, 4), {"doc": flip(d, 4)}),
    }

    loads = {}

    def load(name, src, dst):
        copy = pltpu.make_async_copy(src, dst, local_sem.at[len(loads)])
        copy.start()
        loads[name] = copy

    for j in range(vocab.shape[0]):
        load("vocab%d" % j, vocab.at[j], big.at[j])
    barrier = pltpu.get_barrier_semaphore()
    doc_peers = [lax.rem(d + k, docs) for k in range(1, docs)]
    peers = [{"tensor": p} for p in (t1, t2, t3)] + [{"doc": p} for p in doc_peers]
    for peer in peers:
        pl.semaphore_signal(barrier, inc=1, device_id=peer, device_id_type=MESH)
    pl.semaphore_wait(barrier, len(peers))

    def remote(number, src, dst, peer):
        return pltpu.make_async_remote_copy(
            src_ref=src,
            dst_ref=dst,
            send_sem=send_sem.at[number],
            recv_sem=recv_sem.at[number],
            device_id=peer,
            device_id_type=MESH,
        )

    started = []

    def send(number, src, dst, peer):
        copy = remote(number, src, dst, peer)
        copy.start()
        started.append(copy)

    def arrived(number, ref):
        remote(number, ref, ref, {"tensor": t1}).wait_recv()

    own = pl.multiple_of(t * n_seq, n_seq)
    base = 0
    share_width = model // docs
    wide = states[...].astype(f32)
    wide = jnp.concatenate([wide, jnp.zeros((queries, 128 - share_width), f32)], 1)
    fill = own_states.shape[0] - queries
    if fill:
        wide = jnp.concatenate([wide, jnp.zeros((fill, 128), f32)], 0)
    own_states[...] = wide.astype(bf16)
    st_all[d] = own_states[...]
    for k, p in enumerate(doc_peers):
        send(base + k, own_states, st_all.at[d], {"doc": p})
    states_base = base
    base += docs - 1
    order = (t3, t2, t1, t)
    down_order = (t3, t1, t2, t)
    first_row = d * (4 * n_seq)
    hot = picks(positions, first_row + t * n_seq, n_seq, queries)
    out_base = base
    base += 3
    all_rows = 4 * own_rows
    vocab_local = vocab.shape[0] * model
    chunk = model
    tall = lax.broadcasted_iota(jnp.int32, (all_rows, 1), 0)
    goal = jnp.zeros((all_rows, 1), jnp.int32)
    for b in range(all_rows):
        query = lax.rem(first_row + b // 8, queries)
        goal = jnp.where(tall == b, targets[query, b % 8], goal)
    goal = goal - t * vocab_local
    picked = rows_of(pk[...])
    for j in range(vocab_local // chunk):
        loads["vocab%d" % j].wait()
        lg[:, j * chunk : (j + 1) * chunk] = dot_nt(picked, square(big[j]))
    load("og", out_grad.at[pl.ds(own, n_seq)], og)
    load("n2", n2_in, n2)
    load("f2", f2_in, f2)
    load("hl", hl_in, tmp)

    high = jnp.max(lg[...], 1, keepdims=True)
    ut[...] = jnp.zeros_like(ut)

    def vocab_step(j, carry):
        mass, chosen = carry
        start = pl.multiple_of(j * chunk, chunk)
        values = lg[:, pl.ds(start, chunk)]
        e = jnp.exp(values - high)
        index = lax.broadcasted_iota(jnp.int32, (all_rows, chunk), 1) + start
        hits = (index == goal).astype(f32)
        both = jnp.concatenate([e, hits], 0).astype(bf16)
        ut[...] += dot(both, square(big[j]))
        mass = mass + jnp.sum(e, 1, keepdims=True)
        chosen = chosen + jnp.sum(hits * values, 1, keepdims=True)
        return mass, chosen

    zero = jnp.zeros((all_rows, 1), f32)
    mass, chosen = lax.fori_loop(0, vocab_local // chunk, vocab_step, (zero, zero))
    spread = lax.broadcasted_iota(jnp.int32, (all_rows, 128), 1)
    stats = jnp.where(spread == 0, high, jnp.where(spread == 1, mass, chosen))
    mean_row = (ut[:all_rows] * (1.0 / mass)).astype(bf16)
    goal_row = ut[all_rows:].astype(bf16)
    for j in range(4):
        part = slice(j * own_rows, (j + 1) * own_rows)
        us[j, :, :model] = mean_row[part]
        us[j, :, model:] = goal_row[part]
    part_base = base
    base += 6
    sr[t] = stats
    for k, p in enumerate((t2, t3, t1)):
        send(part_base + k, sr.at[t], sr.at[t], {"tensor": p})
    for k, p in enumerate((t2, t3, t1)):
        send(part_base + 3 + k, us.at[p], ur.at[t], {"tensor": p})
    ur[t] = us[t]
    for i in range(2):
        load("act%d" % i, act_in.at[down_order[i]], act.at[i])
    sums[0] = jnp.zeros(sums.shape[1:], f32)
    for name in ("og", "n2", "f2"):
        loads[name].wait()
    step_rows = 96

    def add_sum(row, value):
        sums[0, 8 + row] += jnp.sum(value, 0, keepdims=True)

    def second_norm(s, rows, flat, extra):
        upstream = og[s, rows].astype(f32)
        if extra is not None:
            upstream = upstream + extra
        normed = n2[flat]
        back = norm_back_rows(upstream, normed, f2[flat], gain_two[...].reshape(1, model))
        add_sum(4, upstream * normed)
        add_sum(5, upstream)
        add_sum(3, back)
        dy[flat] = back
        og[s, rows] = back.astype(bf16)

    for s in range(n_seq):

        @pl.loop(1, seq // step_rows)
        def _(i):
            start = pl.multiple_of(i * step_rows, step_rows)
            second_norm(s, pl.ds(start, step_rows), pl.ds(s * seq + start, step_rows), None)

    for k, p in enumerate((t2, t3, t1)):
        arrived(part_base + k, sr.at[p])
    highs = [sr[j, :, 0:1] for j in range(4)]
    top = jnp.maximum(jnp.maximum(highs[0], highs[1]), jnp.maximum(highs[2], highs[3]))
    masses = [sr[j, :, 1:2] * jnp.exp(highs[j] - top) for j in range(4)]
    whole = masses[0] + masses[1] + masses[2] + masses[3]
    picked_logit = sr[0, :, 2:3] + sr[1, :, 2:3] + sr[2, :, 2:3] + sr[3, :, 2:3]
    loglik = picked_logit - (top + jnp.log(whole))
    mine = first_row + t * n_seq
    for s in range(4 * n_seq):
        total = jnp.sum(loglik[8 * s : 8 * s + 8], 0, keepdims=True)
        lb[first_row + s] = jnp.broadcast_to(total, (1, 128))
    group_base = base
    base += docs - 1
    group_ref = lb.at[pl.ds(first_row, 4 * n_seq)]
    for k, p in enumerate(doc_peers):
        send(group_base + k, group_ref, group_ref, {"doc": p})
    for j in range(4):
        share = jnp.broadcast_to(masses[j] / whole, (all_rows, 128))
        shares[j] = share.reshape(4, own_rows, 128)
    loads["hl"].wait()
    x_t[...] = tmp[...].T
    load("x", x_in, tmp)
    for i in range(2):
        load("wd%d" % i, wd_in.at[order[i]], wd.at[i])
        load("gp%d" % i, gp_in.at[order[i]], gp.at[i])
        load("wu%d" % i, wu_in.at[order[i]], wu.at[i])
    for k, p in enumerate((t2, t3, t1)):
        arrived(part_base + 3 + k, ur.at[p])
    gap = jnp.zeros((own_rows, model), f32)
    for j in range(4):
        share = shares[j, t][:, 0:1]
        gap = gap + ur[j, :, model:].astype(f32) - share * ur[j, :, :model].astype(f32)
    diff[...] = gap
    for k in range(docs - 1):
        source = lax.rem(d + docs - 1 - k, docs)
        arrived(states_base + k, st_all.at[source])
    emb = jnp.zeros((own_states.shape[0], 128), f32)
    for j in range(docs):
        emb = emb + dot(st_all[j, :, :share_width], w_query[j])
    emb = emb[:queries]
    table_score = dot_f32(emb, doc_table[...], ((1,), (1,)))
    entry = lax.broadcasted_iota(jnp.int32, (queries, table), 1)
    hot_docs = [(entry == doc_ids[:, k : k + 1]).astype(f32) for k in range(slots)]
    prior = [jnp.sum(hot_docs[k] * table_score, 1, keepdims=True) for k in range(slots)]
    for k in range(docs - 1):
        source = lax.rem(d + docs - 1 - k, docs)
        arrived(group_base + k, lb.at[pl.ds(source * (4 * n_seq), 4 * n_seq)])
    joint = []
    for k in range(slots):
        column = lb[k * queries : (k + 1) * queries].reshape(queries, 128)
        joint.append(prior[k] + column[:, 0:1])

    def log_sum(values):
        largest = functools.reduce(jnp.maximum, values)
        total = functools.reduce(jnp.add, [jnp.exp(v - largest) for v in values])
        return largest + jnp.log(total)

    prior_lse, joint_lse = log_sum(prior), log_sum(joint)
    tall = lax.broadcasted_iota(jnp.int32, (queries, 1), 0)
    weight = jnp.zeros((queries, 1), f32)
    for k in range(queries):
        weight = jnp.where(tall == k, query_weight[k], weight)
    nll_out[...] = jnp.broadcast_to(prior_lse - joint_lse, (queries, 128))
    spread_docs = jnp.zeros((queries, table), f32)
    for k in range(slots):
        post = jnp.exp(joint[k] - joint_lse)
        before = jnp.exp(prior[k] - prior_lse)
        spread_docs = spread_docs + hot_docs[k] * (weight * (before - post))
        value = -weight * post
        dlog[k * queries : (k + 1) * queries] = jnp.broadcast_to(value, (queries, 128)).reshape(
            queries, 1, 128
        )
    d_emb = dot_f32(spread_docs, doc_table[...], ((1,), (0,))).astype(bf16)
    gs_out[...] = dot_nt(d_emb, w_query[d])
    gwq_out[...] = dot_tn(st_all[d, :queries, :share_width].astype(f32), d_emb.astype(f32))
    scattered = []
    for s in range(n_seq):
        coefficient = dlog[mine + s]
        rows = diff[8 * s : 8 * s + 8] * coefficient[:, 0:1]
        scattered.append(
            dot_f32(hot[8 * s : 8 * s + 8, 32 * s : 32 * s + 32], rows, ((0,), (0,)))
        )
    mine_out = output.at[pl.ds(own, n_seq)]
    send(out_base, res, mine_out, {"tensor": t2})
    send(out_base + 1, res, mine_out, {"tensor": t1})
    for s in range(n_seq):
        extra = jnp.concatenate([scattered[s], jnp.zeros((step_rows - 32, model), f32)], 0)
        second_norm(s, pl.ds(0, step_rows), pl.ds(s * seq, step_rows), extra)

    d_t[...] = rows_of(og[...]).T
    reds = []
    for k in range(3):
        reds.append(Reduction(bits, arrived, send, base, red_bufs[9 * k : 9 * k + 9]))
        base += 12
    down, up, attn = reds
    block_shape = (2, 2, 2, model // docs)

    def emit(red, shard, sending, lanes, value):
        value = value.reshape(block_shape + (value.shape[-1],))
        which = lax.div(shard, 2)
        if sending is not None:
            sending[which, :, :, :, :, lanes] = value.astype(bf16)
        else:
            total = value + red.held[which, :, :, :, :, lanes].astype(f32)
            red.held[which, :, :, :, :, lanes] = total.astype(bf16)

    def before_block(red, number, shard):
        arrived(red.base + number, red.held.at[lax.div(shard, 2)])

    def after_block(red, number, sending, shard):
        which = lax.div(shard, 2)
        send(red.base + number, sending.at[which], red.held.at[which], {"tensor": t1})

    down_send, up_send = big.at[0:2], big.at[2:4]
    tiles = model // 256
    for i, shard in enumerate(down_order):
        loads["act%d" % i].wait()
        if i >= 2:
            before_block(down, i - 2, shard)

        @pl.loop(0, tiles)
        def _(n):
            lanes = pl.ds(pl.multiple_of(n * 256, 256), 256)
            value = dot(d_t[...], act[i % 2, :, lanes])
            emit(down, shard, down_send if i < 2 else None, lanes, value)

        if i + 2 < 4:
            load("act%d" % (i + 2), act_in.at[down_order[i + 2]], act.at[i % 2])
        if i < 2:
            after_block(down, i, down_send, shard)
        if i == 2:
            down.other.start()
    load("n1", n1_in, n1)
    load("f1", f1_in, f1)
    load("wo", wo_in, wo)
    load("ctx", ctx_in, ctx)
    load("lse", lse_in, lse)
    for i in range(2):
        load("qkv%d" % i, qkv_in.at[order[i]], qkv.at[i])
        load("wq%d" % i, wq_in.at[order[i]], wq.at[i])
    for i, shard in enumerate(order):
        for name in ("gp", "wd", "wu"):
            loads["%s%d" % (name, i)].wait()

        @pl.loop(0, tiles)
        def _(n):
            lanes = pl.ds(pl.multiple_of(n * 256, 256), 256)
            value = dot_nt(rows_of(og[...]), wd[i % 2, lanes]) * gp[i % 2, :, lanes].astype(f32)
            low = value.astype(bf16)
            d_up[:, lanes] = low
            sums[0, 4 + shard, :, lanes] = jnp.sum(low.astype(f32), 0, keepdims=True)

        if i + 2 < 4:
            load("gp%d" % (i + 2), gp_in.at[order[i + 2]], gp.at[i % 2])
            load("wd%d" % (i + 2), wd_in.at[order[i + 2]], wd.at[i % 2])
        if i % 2:
            before_block(up, i // 2, shard)

        @pl.loop(0, tiles)
        def _(n):
            lanes = pl.ds(pl.multiple_of(n * 256, 256), 256)
            value = dot_nt(d_up[...], wu[i % 2, lanes])
            if i == 0:
                n2[:, lanes] = value
            else:
                n2[:, lanes] += value
            value = dot(x_t[...], d_up[:, lanes])
            emit(up, shard, None if i % 2 else up_send, lanes, value)

        if i + 2 < 4:
            load("wu%d" % (i + 2), wu_in.at[order[i + 2]], wu.at[i % 2])
        if i % 2 == 0:
            after_block(up, i // 2, up_send, shard)
        if i == 0:
            down.mine.start()
        if i == 2:
            up.other.start()
    arrived(out_base, output.at[pl.ds(t2 * n_seq, n_seq)])
    passed = output.at[pl.ds(t2 * n_seq, n_seq)]
    send(out_base + 2, passed, passed, {"tensor": t1})
    loads["n1"].wait()
    loads["f1"].wait()

    @pl.loop(0, m_rows // step_rows)
    def _(i):
        flat = pl.ds(pl.multiple_of(i * step_rows, step_rows), step_rows)
        s, start = lax.div(i, seq // step_rows), lax.rem(i, seq // step_rows) * step_rows
        upstream = dy[flat] + n2[flat]
        normed = n1[flat]
        back = norm_back_rows(upstream, normed, f1[flat], gain_one[...].reshape(1, model))
        add_sum(1, upstream * normed)
        add_sum(2, upstream)
        add_sum(0, back)
        dy[flat] = back
        og[s, pl.ds(pl.multiple_of(start, step_rows), step_rows)] = back.astype(bf16)

    d_t[...] = rows_of(og[...]).T
    up.mine.start()
    loads["x"].wait()
    x_t[...] = tmp[...].T
    for name in ("wo", "ctx", "lse"):
        loads[name].wait()
    vec_base = base
    vec_peers = [{"tensor": t1}, bits["y"][1], bits["z0"][1], bits["x"][1], bits["z1"][1]]
    base += 2 * len(vec_peers)
    early, late = pl.ds(4, 10), pl.ds(0, 4)

    def vec_start(k, rows):
        number = vec_base + k + (5 if rows is late else 0)
        send(number, sums.at[k, rows], sums_in.at[k, rows], vec_peers[k])

    def vec_finish(k, rows):
        number = vec_base + k + (5 if rows is late else 0)
        arrived(number, sums_in.at[k, rows])
        sums[k + 1, rows] = sums[k, rows] + sums_in[k, rows]

    def vec_next(k, rows):
        vec_finish(k, rows)
        vec_start(k + 1, rows)

    vec_start(0, early)

    def add_dx(i, first):
        @pl.loop(0, tiles)
        def _(n):
            lanes = pl.ds(pl.multiple_of(n * 256, 256), 256)
            value = dot(dqkv[i % 2], wq[i % 2, :, lanes])
            if first:
                n1[:, lanes] = value
            else:
                n1[:, lanes] += value

    key_index = lax.broadcasted_iota(jnp.int32, (seq, seq), 0)
    for i, shard in enumerate(order):
        loads["qkv%d" % i].wait()
        loads["wq%d" % i].wait()
        dctx[...] = dot_nt(rows_of(og[...]), wo[shard]).astype(bf16)

        @pl.loop(0, n_seq)
        def _(s):
            rows = pl.ds(pl.multiple_of(s * seq, 32), seq)
            row = first_row + t * n_seq + s
            length = lengths[lax.rem(row, queries), lax.div(row, queries)]
            z = qkv[i % 2, s]
            upstream = dctx[rows]
            d_q, d_k, d_v = [], [], []
            for h in range(3):
                qh = z[:, h * 64 : h * 64 + 64]
                kh = z[:, 192 + h * 64 : 256 + h * 64]
                vh = z[:, 384 + h * 64 : 448 + h * 64]
                dc = upstream[:, h * 64 : h * 64 + 64]
                scores = jnp.where(key_index < length, dot_nt(kh, qh * 0.125), -1000000000.0)
                prob = jnp.exp(scores - lse[shard, s, h])
                d_v.append(dot(prob.astype(bf16), dc))
                d_prob = dot_nt(vh, dc)
                inner = jnp.sum(d_prob * prob, 0, keepdims=True)
                d_score = (prob * (d_prob - inner)).astype(bf16)
                d_k.append(dot(d_score, qh) * 0.125)
                d_q.append(dot_tn(kh, d_score) * 0.125)
            first = jnp.concatenate(d_q, 0).T
            both = jnp.concatenate([first] + d_k + d_v, 1).astype(bf16)
            dqkv[i % 2, rows] = both
            lse_sum = jnp.sum(both.astype(f32), 0, keepdims=True)
            parts[s] = lse_sum

        total = parts[0]
        for s in range(1, n_seq):
            total = total + parts[s]
        sums[0, shard, :, : 3 * 192] = total
        if i % 2:
            before_block(attn, i // 2, shard)
        value = jnp.concatenate([dot(x_t[...], dqkv[i % 2]), dot(d_t[...], ctx[shard])], 1)
        emit(attn, shard, None if i % 2 else attn_send, slice(None), value)
        if i % 2 == 0:
            after_block(attn, i // 2, attn_send, shard)
        if i == 0:
            down.other.middle()
            down.mine.middle()
            up.other.middle()
            down.pass_other()
        if i == 1:
            attn.other.start()
            up.mine.middle()
            up.pass_other()
        if i == 2:
            down.pass_mine()
            attn.other.middle()
        if i == 3:
            attn.mine.start()
            vec_start(0, late)
        if i < 4:
            vec_next(i, early)
        if i < 2:
            add_dx(i, i == 0)
            load("qkv%d" % (i + 2), qkv_in.at[order[i + 2]], qkv.at[i])
            load("wq%d" % (i + 2), wq_in.at[order[i + 2]], wq.at[i])

    add_dx(2, False)
    up.pass_mine()
    add_dx(3, False)
    vec_next(0, late)
    attn.pass_other()
    for j in range(4):
        lanes = slice(j * 192, j * 192 + 192)
        block = (n1[:, lanes] + dy[:, lanes]).astype(bf16)
        dxb[j] = jnp.concatenate([block[k * seq : (k + 1) * seq] for k in range(n_seq)], 1)
    tok_base = base
    base += 3
    for k, p in enumerate((t2, t3, t1)):
        send(tok_base + k, dxb.at[p], gt.at[t], {"tensor": p})
    gt[t] = dxb[t]
    vec_next(1, late)
    down_out[...] = down.result()
    attn.mine.middle()
    vec_next(2, late)
    vec_finish(4, early)
    attn.pass_mine()
    vec_next(3, late)
    up_out[...] = up.result()
    vec_finish(4, late)
    vec_out[...] = sums[5]
    for k, p in enumerate((t2, t3, t1)):
        arrived(tok_base + k, gt.at[p])
    load("gt", gt, gt_out)
    total = attn.result()
    for k in range(3):
        qkv_out[k] = total[:, k * 192 : k * 192 + 192]
    out_out[...] = total[:, 576:].T
    arrived(out_base + 1, output.at[pl.ds(t1 * n_seq, n_seq)])
    arrived(out_base + 2, output.at[pl.ds(t3 * n_seq, n_seq)])
    loads["gt"].wait()
    for copy in started:
        copy.wait_send()


def backward(
    n_seq,
    seq,
    model,
    docs,
    tables,
    vocab,
    out_grad,
    kept,
):
    states, doc_ids, doc_table, w_query = tables[4:8]
    queries, slots = doc_ids.shape
    table = doc_table.shape[0]
    m_rows = n_seq * seq
    own_rows = 8 * n_seq
    all_rows = 4 * own_rows
    share = model // docs
    states_rows = -(-queries // 16) * 16
    (res, x, qkv, lse, ctx, n1, f1, hl, act, gp, n2, f2, wq, wo, wu, wd) = kept

    def flat(a):
        return a.reshape(a.shape[:-3] + (a.shape[-3] * a.shape[-2], a.shape[-1]))

    kept = [
        res,
        flat(x),
        qkv,
        lse,
        flat(ctx),
        flat(n1),
        flat(f1),
        flat(hl),
        flat(act),
        flat(gp),
        flat(n2),
        flat(f2),
        flat(wq),
        flat(wo),
        flat(wu),
        flat(wd),
    ]
    vocab = vocab.reshape(vocab.shape[0] // model, 2, 2, 2, share, model)

    def sds(shape, dtype):
        return jax.ShapeDtypeStruct(shape, dtype)

    any_spec = pl.BlockSpec(memory_space=pl.ANY)
    vmem_spec = pl.BlockSpec(memory_space=pltpu.VMEM)
    smem_spec = pl.BlockSpec(memory_space=pltpu.SMEM)
    outs = [
        sds((4 * n_seq, seq, model), bf16),
        sds((queries, 128), f32),
        sds((4, seq, n_seq * 192), bf16),
        sds((queries, share), f32),
        sds((share, 128), f32),
        sds((share, model), f32),
        sds((share, model), f32),
        sds((3, share, 192), f32),
        sds((192, share), f32),
        sds((14, 1, model), f32),
    ]
    out_specs = [any_spec, vmem_spec, any_spec] + [vmem_spec] * 7

    def vm(shape, dtype):
        return pltpu.VMEM(shape, dtype)

    scratch = [
        vm(vocab.shape, bf16),
        vm((4, 4, own_rows, 128), f32),
        vm((all_rows, vocab.shape[0] * model), f32),
        vm((2 * all_rows, model), f32),
        vm((4, own_rows, 2 * model), bf16),
        vm((4, own_rows, 2 * model), bf16),
        vm((4, all_rows, 128), f32),
        vm((docs * 4 * n_seq, 1, 128), f32),
        vm((docs * 4 * n_seq, 1, 128), f32),
        vm((docs, states_rows, 128), bf16),
        vm((own_rows, model), f32),
        vm((n_seq, seq, model), bf16),
        vm((m_rows, model), bf16),
        vm((m_rows, model), f32),
        vm((m_rows, model), f32),
        vm((m_rows, 1), f32),
        vm((m_rows, 1), f32),
        vm((m_rows, model), f32),
        vm((2, m_rows, model), bf16),
        vm((2, m_rows, model), bf16),
        vm((2, 576, model), bf16),
        vm((4, 192, model), bf16),
        vm((2, model, model), bf16),
        vm((2, model, model), bf16),
        vm((2, n_seq, seq, 576), bf16),
        vm((4, m_rows, 192), bf16),
        vm((4, n_seq, 3, 1, seq), f32),
        vm((model, m_rows), bf16),
        vm((model, m_rows), bf16),
        vm((m_rows, model), bf16),
        vm((m_rows, 192), bf16),
        vm((2, m_rows, 576), bf16),
        vm((4, seq, n_seq * 192), bf16),
        vm((4, seq, n_seq * 192), bf16),
        vm((6, 14, 1, model), f32),
        vm((5, 14, 1, model), f32),
        vm((states_rows, 128), bf16),
        vm((2, 2, 2, 2, share, model), bf16),
        vm((n_seq, 1, 576), f32),
    ]
    for _ in range(3):
        scratch.append(vm((2, 2, 2, 2, share, model), bf16))
        for _ in range(2):
            scratch.append(vm((2, 2, share, model // 2), bf16))
            scratch.append(vm((2, 2, share, model // 2), bf16))
            scratch.append(vm((2, share, model), bf16))
        scratch.append(vm((2, share, model), bf16))
        scratch.append(vm((share, model), bf16))
    copies = 2 * (docs - 1) + 3 + 6 + 12 * 3 + 3 + 10
    scratch += [
        pltpu.SemaphoreType.DMA((copies,)),
        pltpu.SemaphoreType.DMA((copies,)),
        pltpu.SemaphoreType.DMA((48,)),
    ]
    return pl.pallas_call(
        functools.partial(backward_kernel, (n_seq, seq, model, queries, slots, table, docs)),
        out_shape=outs,
        in_specs=[smem_spec] * 4 + [vmem_spec] * 7 + [any_spec] * 18,
        out_specs=out_specs,
        scratch_shapes=scratch,
        compiler_params=pltpu.CompilerParams(
            collective_id=1, has_side_effects=True, vmem_limit_bytes=60 * MIB
        ),
        name="layer_backward",
    )(*tables, vocab, out_grad, *kept)


def finish_kernel(cfg, *refs):
    n_seq, docs = cfg
    output, res, gs, gwq, down, up, qkv, out, gt_in, nll_in, sums_in = refs[:11]
    output_out, nll_out, tokens_out, gs_out, qkv_out, b_qv_out, out_out = refs[11:18]
    b_out_out, gain_one_out, bias_one_out, up_out, b_up_out, down_out = refs[18:24]
    b_down_out, gain_two_out, bias_two_out, gwq_out, gt, nll, sums, whole = refs[24:32]
    wide, held, sem, sem_out = refs[32], refs[33:-2], refs[-2], refs[-1]
    d = lax.axis_index("doc")
    t = lax.axis_index("tensor")
    pairs = [(gt_in, gt), (sums_in, sums), (nll_in, nll), (res, whole.at[pl.ds(t * n_seq, n_seq)])]
    for k in range(1, 4):
        part = pl.ds(lax.rem(t + k, 4) * n_seq, n_seq)
        pairs.append((output.at[part], whole.at[part]))
    passed = ((down, down_out), (up, up_out), (qkv, qkv_out), (out, out_out), (gs, gs_out))
    passed += ((gwq, gwq_out),)
    pairs += [(pair[0], buf) for pair, buf in zip(passed, held)]
    copies = [pltpu.make_async_copy(*pair, sem.at[k]) for k, pair in enumerate(pairs)]
    for copy in copies:
        copy.start()
    ends = []

    def forward_to(number, src, dst):
        copies[number].wait()
        copy = pltpu.make_async_copy(src, dst, sem_out.at[len(ends)])
        copy.start()
        ends.append(copy)

    part_width = gt.shape[-1] // n_seq
    copies[0].wait()
    for j in range(4):
        for s in range(n_seq):
            lanes = slice(s * part_width, (s + 1) * part_width)
            wide[j * n_seq + s] = gt[j, :, lanes].astype(f32)
        part = pl.ds(j * n_seq, n_seq)
        copy = pltpu.make_async_copy(wide.at[part], tokens_out.at[part], sem_out.at[len(ends)])
        copy.start()
        ends.append(copy)
    for k in range(4):
        part = pl.ds(lax.rem(t + k, 4) * n_seq, n_seq)
        forward_to(3 + k, whole.at[part], output_out.at[part])
    for k, (pair, buf) in enumerate(zip(passed, held)):
        forward_to(7 + k, buf, pair[1])
    copies[1].wait()
    copies[2].wait()
    nll_out[...] = nll[:, 0]
    heads = sums[t]
    b_qv_out[0:1] = heads[:, :part_width]
    b_qv_out[1:2] = heads[:, 2 * part_width : 3 * part_width]
    b_up_out[...] = sums[4 + t].reshape(b_up_out.shape)
    width = b_out_out.shape[0]
    singles = (b_out_out, gain_one_out, bias_one_out, b_down_out, gain_two_out, bias_two_out)
    for k, ref in enumerate(singles):
        row = sums[8 + k]
        own = jnp.zeros((1, width), f32)
        for j in range(docs):
            own = own + jnp.where(d == j, row[:, j * width : (j + 1) * width], 0.0)
        ref[...] = own.reshape(width)
    for copy in ends:
        copy.wait()


def finish(n_seq, docs, parts):
    output, res, gt, nll, gs, gwq, down, up, qkv, out, sums = parts
    model = sums.shape[-1]
    share = model // docs
    part_width = gt.shape[-1] // n_seq

    def sds(*shape):
        return jax.ShapeDtypeStruct(shape, f32)

    outs = [
        jax.ShapeDtypeStruct(output.shape, bf16),
        sds(nll.shape[0]),
        sds(4 * n_seq, gt.shape[1], part_width),
        sds(*gs.shape),
        sds(*qkv.shape),
        sds(2, part_width),
        sds(*out.shape),
        sds(share),
        sds(share),
        sds(share),
        sds(*up.shape),
        sds(model),
        sds(*down.shape),
        sds(share),
        sds(share),
        sds(share),
        sds(*gwq.shape),
    ]
    any_spec = pl.BlockSpec(memory_space=pltpu.HBM)
    vmem_spec = pl.BlockSpec(memory_space=pltpu.VMEM)
    out_specs = [vmem_spec] * 17
    for k in (0, 2, 3, 4, 6, 10, 12, 16):
        out_specs[k] = any_spec
    results = pl.pallas_call(
        functools.partial(finish_kernel, (n_seq, docs)),
        out_shape=outs,
        in_specs=[any_spec] * 11,
        out_specs=out_specs,
        scratch_shapes=[
            pltpu.VMEM(gt.shape, gt.dtype),
            pltpu.VMEM(nll.shape, nll.dtype),
            pltpu.VMEM(sums.shape, sums.dtype),
            pltpu.VMEM(output.shape, output.dtype),
            pltpu.VMEM((4 * n_seq, gt.shape[1], part_width), f32),
            *(pltpu.VMEM(a.shape, a.dtype) for a in (down, up, qkv, out, gs, gwq)),
            pltpu.SemaphoreType.DMA((13,)),
            pltpu.SemaphoreType.DMA((14,)),
        ],
        compiler_params=pltpu.CompilerParams(vmem_limit_bytes=62 * MIB),
        name="layer_results",
    )(output, res, gs, gwq, down, up, qkv, out, gt, nll, sums)
    results = list(results)
    results[12] = results[12].T
    return results


def joined(array, axis, combine):
    everything = jax.tree.map(lambda part: lax.all_gather(part, axis), array)
    initial = jax.tree.map(lambda part: part[0], everything)

    def step(k, so_far):
        return combine(so_far, jax.tree.map(lambda part: part[k], everything))

    return lax.fori_loop(1, lax.axis_size(axis), step, initial)


def norm_back(upstream, normed, factor, gain_vec):
    scaled = upstream * gain_vec
    inner = (
        scaled
        - jnp.mean(scaled, -1, keepdims=True)
        - normed * jnp.mean(scaled * normed, -1, keepdims=True)
    )
    return (inner * factor, jnp.sum(upstream * normed, 0), jnp.sum(upstream, 0))


def merge_pair(high_first, mass_first, high_second, mass_second):
    highest = jnp.maximum(high_first, high_second)
    return (
        highest,
        mass_first * jnp.exp(high_first - highest) + mass_second * jnp.exp(high_second - highest),
    )


def vocab_combine(first, second):
    highest, summed = merge_pair(first[0], first[1], second[0], second[1])
    return (highest, summed, first[2] + second[2])


def query_combine(first, second):
    prior_high, prior_mass = merge_pair(first[0], first[1], second[0], second[1])
    joint_high, joint_mass = merge_pair(first[2], first[3], second[2], second[3])
    return (prior_high, prior_mass, joint_high, joint_mass)


def partial_lse(members, values):
    highest = jnp.max(jnp.where(members, values[:, None], -1e30), 0)
    summed = jnp.sum(jnp.where(members, jnp.exp(values[:, None] - highest[None, :]), 0.0), 0)
    return (highest, summed)


def shards(
    tokens,
    query_states,
    w_qkv,
    b_qv,
    w_out,
    b_out,
    ln1_gain,
    ln1_bias,
    w_up,
    b_up,
    w_down,
    b_down,
    ln2_gain,
    ln2_bias,
    w_query,
    doc_table,
    vocab_table,
    doc_ids,
    lengths,
    positions,
    targets,
    out_grad,
    query_weight,
):
    sequences, seq_length, part_width = tokens.shape
    model_width = w_qkv.shape[1]
    n_seq = sequences // 4
    row_count = n_seq * seq_length
    queries = lengths.shape[0]
    t = lax.axis_index("tensor")
    hidden = w_up.shape[1]
    vectors = (b_qv, b_up, b_out, ln1_gain, ln1_bias, b_down, ln2_gain, ln2_bias)
    quarter = model_width // 4
    weights_in = (
        w_qkv.transpose(0, 2, 1).reshape(4, 3 * quarter // 4, model_width),
        w_out.reshape(4, quarter // 4, model_width),
        w_up.reshape(4, quarter, hidden),
        w_down.reshape(4, hidden // 4, model_width),
    )
    (x, qkv, lse, ctx, n1, f1, hl, act, gp, n2, f2, res, wq, wo, wu, wd, pk) = forward(
        n_seq,
        seq_length,
        model_width,
        queries,
        (lengths, positions),
        tokens,
        weights_in,
        vectors,
    )
    docs = lax.axis_size("doc")
    if docs == 8 and n_seq == 2:
        share = model_width // docs
        tables = (
            lengths,
            positions,
            targets,
            query_weight,
            query_states,
            doc_ids,
            doc_table,
            w_query.reshape(docs, share, w_query.shape[1]),
            ln1_gain,
            ln2_gain,
            pk,
        )
        kept = (res, x, qkv, lse, ctx, n1, f1, hl, act, gp, n2, f2, wq, wo, wu, wd)
        (output, nll, gt, gs, gwq, g_down, g_up, g_qkv, g_out, sums) = backward(
            n_seq, seq_length, model_width, docs, tables, vocab_table, out_grad, kept
        )
        return tuple(
            finish(n_seq, docs, (output, res, gt, nll, gs, gwq, g_down, g_up, g_qkv, g_out, sums))
        )
    output = lax.all_gather(res, "tensor", axis=0, tiled=True)
    row_index = lax.axis_index("doc") * sequences + jnp.arange(sequences, dtype=jnp.int32)
    slot_index = row_index // queries
    query_index = row_index % queries
    row_position = positions[query_index]
    row_target = targets[query_index]
    own = lambda a: lax.dynamic_slice_in_dim(a, t * n_seq, n_seq, 0)
    own_position = own(row_position)
    seq_base = jnp.arange(n_seq, dtype=jnp.int32)[:, None]
    picked = lax.all_gather(res[seq_base, own_position], "tensor", axis=0, tiled=True)
    vocab_logits = jnp.einsum("btd,vd->btv", picked, vocab_table, preferred_element_type=f32)
    vocab_local = vocab_table.shape[0]
    vocab_ids = t * vocab_local + jnp.arange(vocab_local, dtype=jnp.int32)
    target_hits = vocab_ids[None, None, :] == row_target[:, :, None]
    local_high = jnp.max(vocab_logits, -1)
    local_mass = jnp.sum(jnp.exp(vocab_logits - local_high[:, :, None]), -1)
    local_chosen = jnp.sum(jnp.where(target_hits, vocab_logits, 0.0), -1)
    vocab_high, vocab_mass, chosen = joined(
        (local_high, local_mass, local_chosen), "tensor", vocab_combine
    )
    vocab_lse = vocab_high + jnp.log(vocab_mass)
    loglik = jnp.sum(chosen - vocab_lse, -1)
    states = lax.all_gather(query_states, "doc", axis=1, tiled=True)
    query_emb = jnp.dot(states, w_query, preferred_element_type=f32)
    members = query_index[:, None] == jnp.arange(queries, dtype=jnp.int32)[None, :]
    member_weights = members.astype(f32)
    own_emb = jnp.dot(member_weights, query_emb, precision=precise)
    embeds = doc_table[doc_ids[query_index, slot_index]]
    retrieval = jnp.sum(own_emb * embeds, -1)
    joint_score = retrieval + loglik
    prior_high, prior_mass = partial_lse(members, retrieval)
    joint_high, joint_mass = partial_lse(members, joint_score)
    prior_high, prior_mass, joint_high, joint_mass = joined(
        (prior_high, prior_mass, joint_high, joint_mass), "doc", query_combine
    )
    prior_lse = prior_high + jnp.log(prior_mass)
    joint_lse = joint_high + jnp.log(joint_mass)
    query_nll = prior_lse - joint_lse
    row_weight = query_weight[query_index]
    posterior = jnp.exp(joint_score - jnp.dot(member_weights, joint_lse, precision=precise))
    prior_prob = jnp.exp(retrieval - jnp.dot(member_weights, prior_lse, precision=precise))
    grad_loglik = -row_weight * posterior
    grad_retrieval = row_weight * (prior_prob - posterior)
    vocab_probs = jnp.exp(vocab_logits - vocab_lse[:, :, None])
    grad_logits = (grad_loglik[:, None, None] * (target_hits.astype(f32) - vocab_probs)).astype(
        bf16
    )
    grad_picked = lax.psum_scatter(
        jnp.einsum("btv,vd->btd", grad_logits, vocab_table, preferred_element_type=f32),
        "tensor",
        scatter_dimension=0,
        tiled=True,
    )
    grad_emb = jnp.dot(
        member_weights.T, grad_retrieval[:, None] * embeds, precision=precise
    ).astype(bf16)
    grad_w_query = jnp.dot(states.T, grad_emb, preferred_element_type=f32)
    grad_states = jnp.dot(grad_emb, w_query.T, preferred_element_type=f32)
    flat = lambda a: a.reshape(row_count, a.shape[-1])
    grad_result = flat(own(out_grad).astype(f32).at[seq_base, own_position].add(grad_picked))
    n1, f1, n2, f2, hl, x = flat(n1), flat(f1), flat(n2), flat(f2), flat(hl), flat(x)
    dy2, dg2, db2 = norm_back(grad_result, n2, f2, ln2_gain)
    d_low = dy2.astype(bf16)
    act, gp = act.reshape(4, row_count, hidden), gp.reshape(4, row_count, hidden)
    wu, wd = wu.reshape(4, model_width, hidden), wd.reshape(4, hidden, model_width)
    wq, wo = wq.reshape(4, 576, model_width).transpose(0, 2, 1), wo.reshape(4, 192, model_width)
    qkv, ctx = qkv.reshape(4, n_seq, seq_length, 576), ctx.reshape(4, row_count, 192)
    g_down = jnp.einsum("tmf,md->tfd", act, d_low, preferred_element_type=f32)
    d_act = jnp.einsum("md,tfd->tmf", d_low, wd, preferred_element_type=f32)
    d_up = (d_act * gp.astype(f32)).astype(bf16)
    g_up = jnp.einsum("md,tmf->tdf", hl, d_up, preferred_element_type=f32)
    g_b_up = jnp.sum(d_up.astype(f32), 1)
    d_hidden = dy2 + jnp.einsum("tmf,tdf->md", d_up, wu, preferred_element_type=f32)
    dy1, dg1, db1 = norm_back(d_hidden, n1, f1, ln1_gain)
    d_att = dy1.astype(bf16)
    g_out = jnp.einsum("tme,md->ted", ctx, d_att, preferred_element_type=f32)
    d_ctx = jnp.einsum("md,ted->tme", d_att, wo, preferred_element_type=f32).astype(bf16)
    d_ctx = d_ctx.reshape(4, n_seq, seq_length, 3, 64)
    heads = qkv.reshape(4, n_seq, seq_length, 3, 3, 64)
    hq, hk, hv = heads[:, :, :, 0], heads[:, :, :, 1], heads[:, :, :, 2]
    row_length = own(lengths[query_index, slot_index])
    key_mask = (jnp.arange(seq_length, dtype=jnp.int32)[None, :] < row_length[:, None])[
        None, :, None, None, :
    ]
    scores = jnp.einsum("tbqhe,tbkhe->tbhqk", hq, hk, preferred_element_type=f32) * 0.125
    scores = jnp.where(key_mask, scores, -1000000000.0)
    prob = jnp.exp(scores - lse.reshape(4, n_seq, 3, seq_length, 1))
    d_v = jnp.einsum("tbhqk,tbqhe->tbkhe", prob.astype(bf16), d_ctx, preferred_element_type=f32)
    d_prob = jnp.einsum("tbqhe,tbkhe->tbhqk", d_ctx, hv, preferred_element_type=f32)
    d_s = (prob * (d_prob - jnp.sum(d_prob * prob, -1, keepdims=True))).astype(bf16)
    d_q = jnp.einsum("tbhqk,tbkhe->tbqhe", d_s, hk, preferred_element_type=f32) * 0.125
    d_k = jnp.einsum("tbhqk,tbqhe->tbkhe", d_s, hq, preferred_element_type=f32) * 0.125
    d_qkv = jnp.stack([d_q, d_k, d_v], 3).reshape(4, row_count, 576).astype(bf16)
    g_b = jnp.sum(d_qkv.astype(f32), 1)
    g_qkv = jnp.einsum("md,tme->tde", x, d_qkv, preferred_element_type=f32)
    d_x = dy1 + jnp.einsum("tme,tde->md", d_qkv, wq, preferred_element_type=f32)
    d_x = d_x.reshape(n_seq, seq_length, 4, part_width).astype(bf16)
    grad_tokens = lax.all_to_all(d_x, "tensor", split_axis=2, concat_axis=0, tiled=True)
    grad_tokens = grad_tokens.reshape(sequences, seq_length, part_width).astype(f32)
    over_t = lambda a: lax.psum_scatter(a, "tensor", scatter_dimension=0, tiled=True)[0]
    docs = lambda a, k: lax.psum_scatter(a, "doc", scatter_dimension=k, tiled=True)
    g_qkv = docs(over_t(g_qkv), 0)
    g_qkv = jnp.stack([g_qkv[:, :192], g_qkv[:, 192:384], g_qkv[:, 384:]])
    g_b = lax.psum(over_t(g_b), "doc")
    small = lambda v: docs(lax.psum(v, "tensor"), 0)
    return (
        output,
        query_nll,
        grad_tokens,
        docs(grad_states, 1),
        g_qkv,
        jnp.stack([g_b[:192], g_b[384:]]),
        docs(over_t(g_out), 1),
        small(jnp.sum(dy1, 0)),
        small(dg1),
        small(db1),
        docs(over_t(g_up), 0),
        lax.psum(over_t(g_b_up), "doc"),
        docs(over_t(g_down), 1),
        small(jnp.sum(dy2, 0)),
        small(dg2),
        small(db2),
        docs(grad_w_query, 0),
    )


def solution(mesh):
    in_specs = (
        P("doc", None, "tensor"),
        P(None, "doc"),
        P(None, None, "tensor"),
        P(None, "tensor"),
        P("tensor", None),
        P(),
        P(),
        P(),
        P(None, "tensor"),
        P("tensor"),
        P("tensor", None),
        P(),
        P(),
        P(),
        P(),
        P(),
        P("tensor", None),
        P(),
        P(),
        P(),
        P(),
        P("doc", None, None),
        P(),
    )
    out_specs = (
        P("doc", None, None),
        P(),
        P("doc", None, "tensor"),
        P(None, "doc"),
        P(None, "doc", "tensor"),
        P(None, "tensor"),
        P("tensor", "doc"),
        P("doc"),
        P("doc"),
        P("doc"),
        P("doc", "tensor"),
        P("tensor"),
        P("tensor", "doc"),
        P("doc"),
        P("doc"),
        P("doc"),
        P("doc", None),
    )
    return jax.shard_map(shards, mesh=mesh, in_specs=in_specs, out_specs=out_specs, check_vma=False)
```
